32 devices in a mesh: rep: 2 (over x), seq: 16 (over z, y, core).
Axes of the slice: x: 2, y: 2, z: 4, core: 2. Of those that a mesh axis runs over, the one named last changes fastest.
Arguments:
- projected: bfloat16 [24576, 4096], P(('rep', 'seq')), parts along dimension 0, may hold values from -6 to 6
- history_in: bfloat16 [24576, 1024], P(('rep', 'seq')), parts along dimension 0, may hold values from -6 to 6
- norm_gain: float32 [1024], replicated, may hold values from 0.1 to 1.9
- out_proj: bfloat16 [1024, 1024], replicated, may hold values from -0.1875 to 0.1875
- user_spans: int32 [16], P('rep'), parts along dimension 0, may hold values from 1 to 4, as said below
- user_tails: int32 [16], P('rep'), parts along dimension 0, may hold values from 1 to 768
- cand_emb: bfloat16 [4096, 1024], P(('rep', 'seq')), parts along dimension 0, may hold values from -6 to 6
- cand_user: int32 [4096], P(('rep', 'seq')), parts along dimension 0, may hold values from 0 to 7
- cross_down: bfloat16 [2048, 128], replicated, may hold values from -0.125 to 0.125
- cross_up: bfloat16 [128, 2048], replicated, may hold values from -0.5 to 0.5
- cross_bias: float32 [2048], replicated, may hold values from -4 to 4
- score_weight: float32 [2048], replicated, may hold values from -0.125 to 0.125
Outputs:
- history_out: bfloat16 [24576, 1024], P(('rep', 'seq')), parts along dimension 0
- scores: float32 [4096], P(('rep', 'seq')), parts along dimension 0
The draws below stay inside these ranges and needn't reach their ends.
There are 2 independent parts, one for each index of `rep`. The reference program is written for one: setup_inputs(seed, part) draws one part's arguments, and reference() takes and returns one part's arrays. A program takes and returns all parts, laid end to end along the dimension named above; an argument that names none is the same for every part. Nothing has to cross between parts.
Inputs may be any that keep to these rules, and one draw needn't show every extreme that they name: `user_spans`: users own consecutive segments in order and together own all 16 segments; some user owns exactly 4.
All inputs are finite; a program needn't handle non-finite values.
Results may differ from the reference program's by a relative error of at most 0.0059.
Values may be sent and summed in bfloat16 or wider, within the bound.
No kernel may reach another device: no remote copies, remote signals or barrier semaphores. Data moves between devices by JAX's collectives and lax.ppermute only.
A program may use at most 128 MiB of HBM per device.

```python
import jax
import jax.numpy as jnp
from jax import lax

D = 1024
HEADS = 8
RANK = 128
ROWS_DEV = 768
CAND_DEV = 128
SPAN = 4
USERS = 8
TOKENS = 12288
CANDS = 2048


def draw_user_spans(key, part):
    four_count = max(1, USERS // 8)
    three_count = USERS // 8
    one_count = 2 * four_count + three_count
    two_count = USERS - four_count - three_count - one_count
    pieces = [jnp.full((four_count,), 4, jnp.int32), jnp.full((one_count,), 1, jnp.int32)]
    if three_count > 0:
        pieces.append(jnp.full((three_count,), 3, jnp.int32))
    if two_count > 0:
        pieces.append(jnp.full((two_count,), 2, jnp.int32))
    spans = jnp.concatenate(pieces).astype(jnp.int32)
    return jax.random.permutation(jax.random.fold_in(key, 21), spans).astype(jnp.int32)


def touch_ends(result, stream_key, smallest, largest):
    spot = [jax.random.randint(jax.random.fold_in(stream_key, axis), (), 0, length) for axis, length in enumerate(result.shape)]
    longest = result.shape.index(max(result.shape))
    beside = spot[:longest] + [(spot[longest] + 1) % result.shape[longest]] + spot[longest + 1:]
    return result.at[tuple(spot)].set(smallest).at[tuple(beside)].set(largest)


def steps_of(key, shape, shards, low, top_value):
    loudness = 1.0
    for dim, blocks in shards:
        draws = jax.random.uniform(jax.random.fold_in(jax.random.fold_in(key, 6), dim), (blocks,), jnp.float32, low / len(shards), top_value / len(shards))
        loudness = loudness * jnp.repeat(jnp.exp(draws), shape[dim] // blocks).reshape((-1,) + (1,) * (len(shape) - 1 - dim))
    return loudness


def normal_values(stream_key, extent, width, reach, split=(), held_as=jnp.bfloat16):
    result = width * jax.random.normal(stream_key, extent, jnp.float32)
    if split:
        result = result * steps_of(stream_key, extent, split, -0.22, 0.18)
    return jnp.clip(result, -reach, reach).astype(held_as)


def setup_inputs(seed: int = 0, part: int = 0) -> dict:
    seeds = jax.random.split(jax.random.key(seed), 13)
    part_keys = jax.random.split(jax.random.fold_in(seeds[12], part), 13)
    return {
        "projected": normal_values(part_keys[0], (TOKENS, 4 * D), 1.0, 6.0, ((0, 16),)),
        "history_in": normal_values(part_keys[1], (TOKENS, D), 0.5, 6.0, ((0, 16),)),
        "norm_gain": jnp.clip(1.0 + 0.18 * jax.random.normal(seeds[2], (D,), jnp.float32), 0.1, 1.9),
        "out_proj": normal_values(seeds[3], (D, D), D ** -0.5, 0.1875),
        "user_spans": draw_user_spans(jax.random.fold_in(jax.random.fold_in(seeds[12], part), 71), part),
        "user_tails": touch_ends(jax.random.randint(part_keys[5], (USERS,), 1, ROWS_DEV + 1), jax.random.fold_in(part_keys[5], 1), 1, ROWS_DEV).astype(jnp.int32),
        "cand_emb": normal_values(part_keys[6], (CANDS, D), 1.0, 6.0, ((0, 16),)),
        "cand_user": touch_ends(jax.random.randint(part_keys[7], (CANDS,), 0, USERS), jax.random.fold_in(part_keys[7], 1), 0, USERS - 1).astype(jnp.int32),
        "cross_down": normal_values(seeds[8], (2 * D, RANK), (2 * D) ** -0.5, 0.125),
        "cross_up": normal_values(seeds[9], (RANK, 2 * D), RANK ** -0.5, 0.5),
        "cross_bias": normal_values(seeds[10], (2 * D,), 0.5, 4.0, (), jnp.float32),
        "score_weight": normal_values(seeds[11], (2 * D,), (2 * D) ** -0.5, 0.125, (), jnp.float32),
    }


def segment_owners(user_spans, user_tails, devices, row_count):
    last_dev = jnp.cumsum(user_spans).astype(jnp.int32) - 1
    first_dev = last_dev - user_spans.astype(jnp.int32) + 1
    device_ids = jnp.arange(devices, dtype=jnp.int32)
    owner_of = lax.optimization_barrier(jnp.sum((first_dev[None, :] <= device_ids[:, None]).astype(jnp.int32), axis=1)).astype(jnp.int32) - 1
    is_end = device_ids == last_dev[owner_of]
    valid_rows = jnp.where(is_end, user_tails[owner_of], row_count).astype(jnp.int32)
    return (last_dev, owner_of, valid_rows)

def reference(projected, history_in, norm_gain, out_proj, user_spans, user_tails, cand_emb, cand_user, cross_down, cross_up, cross_bias, score_weight):
    devices = USERS * 2
    row_count = ROWS_DEV
    model_width = D
    head_size = model_width // HEADS
    score_scale = head_size ** (-0.5)
    last_dev, owner_of, valid_rows = segment_owners(user_spans, user_tails, devices, row_count)
    blocks = projected.reshape(devices, row_count, 4 * model_width)
    residual_in = history_in.reshape(devices, row_count, model_width)
    row_ids = jnp.arange(row_count, dtype=jnp.int32)
    causal = (row_ids[None, :] <= row_ids[:, None]).astype(jnp.float32)

    def one_segment(my_index):
        own_block = blocks[my_index]
        queries = own_block[:, model_width:2 * model_width].reshape(row_count, HEADS, head_size).astype(jnp.float32)

        def attend(totals, source, weight_mask):
            key_values = blocks[source]
            key_part = key_values[:, 2 * model_width:3 * model_width].reshape(row_count, HEADS, head_size).astype(jnp.float32)
            value_part = key_values[:, 3 * model_width:].reshape(row_count, HEADS, head_size).astype(jnp.float32)
            logits = jnp.einsum('qhd,khd->hqk', queries, key_part) * score_scale
            weights = lax.optimization_barrier((jax.nn.silu(logits) * weight_mask).astype(jnp.bfloat16)).astype(jnp.float32)
            return totals + jnp.einsum('hqk,khd->qhd', weights, value_part)
        totals = attend(jnp.zeros((row_count, HEADS, head_size), jnp.float32), my_index, causal)

        def visit_block(offset, totals):
            source = (my_index - offset).astype(jnp.int32)
            clipped = jnp.maximum(source, 0).astype(jnp.int32)
            same_user = (source >= 0) & (owner_of[clipped] == owner_of[my_index])
            return lax.cond(same_user, lambda current: attend(current, clipped, jnp.float32(1.0)), lambda current: current, totals)
        totals = lax.fori_loop(1, SPAN, visit_block, totals)
        row_valid = (row_ids < valid_rows[my_index]).astype(jnp.float32)
        attention = totals.reshape(row_count, model_width) * row_valid[:, None]
        row_mean = lax.optimization_barrier(jnp.mean(attention, axis=1, keepdims=True))
        centered = attention - row_mean
        row_var = lax.optimization_barrier(jnp.mean(centered * centered, axis=1, keepdims=True))
        normed = centered * lax.rsqrt(row_var + 1e-06) * norm_gain
        gated = (normed * own_block[:, :model_width].astype(jnp.float32)).astype(jnp.bfloat16)
        return (jnp.dot(gated, out_proj, preferred_element_type=jnp.float32) + residual_in[my_index].astype(jnp.float32)).astype(jnp.bfloat16)
    history = lax.map(one_segment, jnp.arange(devices, dtype=jnp.int32))
    history_rows = history.reshape(devices * row_count, model_width)
    last_rows = (last_dev * row_count + user_tails - 1).astype(jnp.int32)
    user_rows = history_rows[last_rows]
    cand_blocks = cand_emb.reshape(devices, CAND_DEV, model_width)
    user_blocks = cand_user.reshape(devices, CAND_DEV)

    def score_block(pair):
        cand_rows, cand_users = pair
        crossed_in = jnp.concatenate([user_rows[cand_users], cand_rows], axis=1)
        low_rank = jnp.dot(crossed_in, cross_down, preferred_element_type=jnp.float32).astype(jnp.bfloat16)
        up_part = jnp.dot(low_rank, cross_up, preferred_element_type=jnp.float32)
        input_float = crossed_in.astype(jnp.float32)
        crossed = input_float * (up_part + cross_bias) + input_float
        return lax.optimization_barrier(jnp.sum(crossed * score_weight, axis=1))
    scores = lax.map(score_block, (cand_blocks, user_blocks)).reshape(devices * CAND_DEV)
    return (history_rows, scores)
```

```python
import functools

import jax
import jax.numpy as jnp
from jax import lax
from jax.experimental import pallas as pl
from jax.experimental.pallas import tpu as pltpu
from jax.sharding import PartitionSpec as P

HEADS = 8
SPAN = 4
CHUNKS = 4
VMEM_LIMIT = 48 * 1024 * 1024


def silu_weights(logits, score_scale):
    half = logits * (0.5 * score_scale)
    return half + half * jnp.tanh(half)


def row_tile(row_count):
    return 256 if row_count % 256 == 0 else row_count


def dot_nt(left, right):
    return lax.dot_general(left, right, (((1,), (1,)), ((), ())), preferred_element_type=jnp.float32)


def place_kernel(me_ref, spans_ref, tails_ref, place_ref, last_ref):
    users = spans_ref.shape[0]
    me = me_ref[0]

    def visit(user, state):
        begin, span, start, tail = state
        end = begin + spans_ref[user]
        mine = (begin <= me) & (me < end)
        last_ref[user] = end - 1
        return (
            end,
            jnp.where(mine, spans_ref[user], span),
            jnp.where(mine, begin, start),
            jnp.where(mine, tails_ref[user], tail),
        )

    zero = jnp.int32(0)
    _, span, start, tail = lax.fori_loop(0, users, visit, (zero, zero + 1, zero, zero))
    place_ref[0] = span
    place_ref[1] = start
    place_ref[2] = me - start
    place_ref[3] = tail
    place_ref[4] = jnp.where(span < 2, 0, 1 + (span - 2) * SPAN + lax.rem(start, SPAN))


def find_place(me, user_spans, user_tails):
    smem = pl.BlockSpec(memory_space=pltpu.SMEM)
    return pl.pallas_call(
        place_kernel,
        out_shape=(
            jax.ShapeDtypeStruct((8,), jnp.int32),
            jax.ShapeDtypeStruct(user_spans.shape, jnp.int32),
        ),
        in_specs=[smem] * 3,
        out_specs=(smem, smem),
    )(me.reshape(1), user_spans, user_tails)


def own_kernel(score_scale, q_ref, k_ref, v_ref, out_ref):
    row_count = q_ref.shape[0]
    tile = row_tile(row_count)
    for first in range(0, row_count, tile):
        queries = q_ref[first : first + tile, :]
        logits = dot_nt(queries, k_ref[first : first + tile, :])
        weights = silu_weights(logits, score_scale)
        row_ids = lax.broadcasted_iota(jnp.int32, weights.shape, 0)
        key_ids = lax.broadcasted_iota(jnp.int32, weights.shape, 1)
        weights = jnp.where(key_ids <= row_ids, weights, 0.0).astype(jnp.bfloat16)
        total = jnp.dot(weights, v_ref[first : first + tile, :], preferred_element_type=jnp.float32)
        if first:
            logits = dot_nt(queries, k_ref[:first, :])
            weights = silu_weights(logits, score_scale).astype(jnp.bfloat16)
            total += jnp.dot(weights, v_ref[:first, :], preferred_element_type=jnp.float32)
        out_ref[first : first + tile, :] = total


def own_attention(projected):
    row_count, width = projected.shape
    model_width = width // 4
    head_size = model_width // HEADS

    def columns(part):
        return pl.BlockSpec((row_count, head_size), lambda head: (0, part * HEADS + head))

    return pl.pallas_call(
        functools.partial(own_kernel, head_size ** (-0.5)),
        out_shape=jax.ShapeDtypeStruct((row_count, model_width), jnp.float32),
        grid=(HEADS,),
        in_specs=[columns(1), columns(2), columns(3)],
        out_specs=pl.BlockSpec((row_count, head_size), lambda head: (0, head)),
        compiler_params=pltpu.CompilerParams(vmem_limit_bytes=VMEM_LIMIT),
        cost_estimate=pl.CostEstimate(
            flops=4 * row_count * row_count * model_width,
            bytes_accessed=10 * row_count * model_width,
            transcendentals=row_count * row_count * HEADS,
        ),
    )(projected, projected, projected)


def add_kernel(score_scale, holders, place_ref, q_ref, *refs):
    source_refs, total_ref, out_ref = refs[: 2 * len(holders)], refs[-2], refs[-1]
    position = place_ref[2]
    row_count = q_ref.shape[0]
    tile = row_tile(row_count)
    out_ref[...] = total_ref[...]
    for index, positions in enumerate(holders):
        k_ref, v_ref = source_refs[2 * index], source_refs[2 * index + 1]
        held = functools.reduce(jnp.logical_or, [position == p for p in positions])

        @pl.when(held)
        def _():
            for first in range(0, row_count, tile):
                logits = dot_nt(q_ref[first : first + tile, :], k_ref[...])
                weights = silu_weights(logits, score_scale).astype(jnp.bfloat16)
                out_ref[first : first + tile, :] += jnp.dot(
                    weights, v_ref[...], preferred_element_type=jnp.float32
                )


def add_sources(place, projected, totals, sources, first_head):
    row_count, width = projected.shape
    model_width = width // 4
    head_size = model_width // HEADS
    heads = sources[0][0].shape[1] // (2 * head_size)
    arrays, specs, holders = [], [], []
    for array, positions in sources:
        arrays += [array, array]
        specs.append(pl.BlockSpec((row_count, head_size), lambda head, place: (0, head)))
        specs.append(pl.BlockSpec((row_count, head_size), lambda head, place: (0, heads + head)))
        holders.append(positions)
    total_spec = pl.BlockSpec((row_count, head_size), lambda head, place: (0, first_head + head))
    return pl.pallas_call(
        functools.partial(add_kernel, head_size ** (-0.5), holders),
        out_shape=jax.ShapeDtypeStruct(totals.shape, totals.dtype),
        grid_spec=pltpu.PrefetchScalarGridSpec(
            num_scalar_prefetch=1,
            grid=(heads,),
            in_specs=[
                pl.BlockSpec((row_count, head_size), lambda head, place: (0, HEADS + first_head + head)),
                *specs,
                total_spec,
            ],
            out_specs=total_spec,
        ),
        input_output_aliases={2 + len(arrays): 0},
        compiler_params=pltpu.CompilerParams(vmem_limit_bytes=VMEM_LIMIT),
        cost_estimate=pl.CostEstimate(
            flops=4 * row_count * row_count * heads * head_size * len(sources),
            bytes_accessed=(6 + 4 * len(sources)) * row_count * heads * head_size,
            transcendentals=row_count * row_count * heads * len(sources),
        ),
    )(place, projected, *arrays, totals)


def pack_kernel(k_ref, v_ref, after_ref, out_ref):
    width = k_ref.shape[1]
    out_ref[:, :width] = k_ref[...]
    out_ref[:, width:] = v_ref[...]


def pack_key_values(projected, after, index):
    row_count, width = projected.shape
    chunk = width // 4 // CHUNKS
    return pl.pallas_call(
        pack_kernel,
        out_shape=jax.ShapeDtypeStruct((row_count, 2 * chunk), projected.dtype),
        grid=(1,),
        in_specs=[
            pl.BlockSpec((row_count, chunk), lambda step: (0, 2 * CHUNKS + index)),
            pl.BlockSpec((row_count, chunk), lambda step: (0, 3 * CHUNKS + index)),
            pl.BlockSpec(memory_space=pl.ANY),
        ],
        out_specs=pl.BlockSpec((row_count, 2 * chunk), lambda step: (0, 0)),
        compiler_params=pltpu.CompilerParams(vmem_limit_bytes=VMEM_LIMIT),
        cost_estimate=pl.CostEstimate(
            flops=0, bytes_accessed=8 * row_count * chunk, transcendentals=0
        ),
    )(projected, projected, after)


def group_attention(span, residue, peers, place, projected):
    if span == 1:
        return own_attention(projected)

    def send(array, position, by):
        lowest = (residue + position) % SPAN
        pairs = [(s, s + by) for s in range(lowest, peers, SPAN) if s + by < peers]
        return lax.ppermute(array, "seq", pairs)

    def swap(array, position):
        lowest = (residue + position) % SPAN
        pairs = [(s, s + 1) for s in range(lowest, peers, SPAN) if s + 1 < peers]
        return lax.ppermute(array, "seq", pairs + [(b, a) for a, b in pairs])

    chips = {}
    for position in range(span):
        chips.setdefault((residue + position) // 2, []).append(position)
    chips = list(chips.values())
    inner = [chip for chip in chips if len(chip) == 2]
    sources = []
    crossing = [projected] * CHUNKS
    for index in range(CHUNKS):
        after = crossing[index - 2] if index >= 2 else place
        mine = pack_key_values(projected, after, index)
        found = []
        for near, chip in enumerate(chips):
            for far in chips[near + 1 :]:
                if len(far) == 1:
                    for position in chip:
                        came = send(mine, position, far[0] - position)
                        found.append((came, [far[0]]))
                elif len(chip) == 1:
                    came = send(mine, chip[0], far[1] - chip[0])
                    found.append((came, [far[1]]))
                    found.append((swap(came, far[0]), [far[0]]))
                else:
                    came = send(mine, chip[0], 2) + send(mine, chip[1], 2)
                    found += [(came, far), (swap(came, far[0]), far)]
                crossing[index] = came
        for chip in inner:
            found.append((send(mine, chip[0], 1), [chip[1]]))
            if len(chips) == 1:
                crossing[index] = found[-1][0]
        sources.append(found)
    totals = own_attention(projected)
    heads = HEADS // CHUNKS
    for index in range(CHUNKS):
        totals = add_sources(place, projected, totals, sources[index], index * heads)
    return totals


def finish_kernel(place_ref, total_ref, u_ref, history_ref, gain_ref, weight_ref, out_ref, last_ref):
    step = pl.program_id(0)
    tile = total_ref.shape[0]
    row_count = tile * pl.num_programs(0)
    span, position, tail = place_ref[0], place_ref[2], place_ref[3]
    valid = jnp.where(position == span - 1, tail, row_count)
    row_ids = step * tile + lax.broadcasted_iota(jnp.int32, (tile, 1), 0)
    attention = jnp.where(row_ids < valid, total_ref[...], 0.0)
    row_mean = jnp.mean(attention, axis=1, keepdims=True)
    centered = attention - row_mean
    row_var = jnp.mean(centered * centered, axis=1, keepdims=True)
    normed = centered * lax.rsqrt(row_var + 1e-06) * gain_ref[...]
    gated = (normed * u_ref[...].astype(jnp.float32)).astype(jnp.bfloat16)
    out = jnp.dot(gated, weight_ref[...], preferred_element_type=jnp.float32)
    out = (out + history_ref[...].astype(jnp.float32)).astype(jnp.bfloat16)
    out_ref[...] = out
    final = jnp.sum(jnp.where(row_ids == valid - 1, out.astype(jnp.float32), 0.0), axis=0, keepdims=True)

    @pl.when(step == 0)
    def _():
        last_ref[...] = final

    @pl.when(step > 0)
    def _():
        last_ref[...] += final


def finish(place, totals, projected, history_in, norm_gain, out_proj):
    row_count, model_width = history_in.shape
    tile = row_tile(row_count)
    rows = pl.BlockSpec((tile, model_width), lambda step, place: (step, 0))
    whole = pl.BlockSpec((1, model_width), lambda step, place: (0, 0))
    return pl.pallas_call(
        finish_kernel,
        out_shape=(
            jax.ShapeDtypeStruct(history_in.shape, history_in.dtype),
            jax.ShapeDtypeStruct((1, model_width), jnp.float32),
        ),
        grid_spec=pltpu.PrefetchScalarGridSpec(
            num_scalar_prefetch=1,
            grid=(row_count // tile,),
            in_specs=[
                rows,
                rows,
                rows,
                whole,
                pl.BlockSpec(out_proj.shape, lambda step, place: (0, 0)),
            ],
            out_specs=(rows, whole),
        ),
        compiler_params=pltpu.CompilerParams(vmem_limit_bytes=VMEM_LIMIT),
        cost_estimate=pl.CostEstimate(
            flops=2 * row_count * model_width * model_width,
            bytes_accessed=10 * row_count * model_width + 2 * model_width * model_width,
            transcendentals=row_count,
        ),
    )(place, totals, projected, history_in, norm_gain.reshape(1, -1), out_proj)


def score_kernel(last_ref, rows_ref, user_ref, cand_ref, down_ref, up_ref, bias_ref, weight_ref, out_ref):
    peers, model_width = rows_ref.shape
    cand_count = cand_ref.shape[0]
    cand_user = user_ref[...]

    def visit(user, found):
        return jnp.where(cand_user == user, last_ref[user], found)

    cand_dev = lax.fori_loop(0, last_ref.shape[0], visit, jnp.zeros_like(cand_user))
    device_ids = lax.broadcasted_iota(jnp.int32, (peers, cand_count), 0)
    selector = jnp.where(device_ids == cand_dev, 1.0, 0.0).astype(jnp.bfloat16)
    user_part = lax.dot_general(
        selector,
        rows_ref[...].astype(jnp.bfloat16),
        (((0,), (0,)), ((), ())),
        preferred_element_type=jnp.float32,
    ).astype(jnp.bfloat16)
    cand_part = cand_ref[...]
    low_rank = jnp.dot(user_part, down_ref[:model_width, :], preferred_element_type=jnp.float32)
    low_rank += jnp.dot(cand_part, down_ref[model_width:, :], preferred_element_type=jnp.float32)
    low_rank = low_rank.astype(jnp.bfloat16)
    score = jnp.zeros((cand_count, 1), jnp.float32)
    for part, low in ((user_part, 0), (cand_part, model_width)):
        cut = slice(low, low + model_width)
        up_part = jnp.dot(low_rank, up_ref[:, cut], preferred_element_type=jnp.float32)
        value = part.astype(jnp.float32)
        crossed = value * (up_part + bias_ref[:, cut]) + value
        score += jnp.sum(crossed * weight_ref[:, cut], axis=1, keepdims=True)
    row_ids = lax.broadcasted_iota(jnp.int32, (cand_count, cand_count), 0)
    column_ids = lax.broadcasted_iota(jnp.int32, (cand_count, cand_count), 1)
    out_ref[...] = jnp.sum(jnp.where(row_ids == column_ids, score, 0.0), axis=0, keepdims=True)


def score(last_dev, user_rows, cand_user, cand_emb, cross_down, cross_up, cross_bias, score_weight):
    vmem = pl.BlockSpec(memory_space=pltpu.VMEM)
    cand_count = cand_emb.shape[0]
    scores = pl.pallas_call(
        score_kernel,
        out_shape=jax.ShapeDtypeStruct((1, cand_count), jnp.float32),
        in_specs=[pl.BlockSpec(memory_space=pltpu.SMEM)] + [vmem] * 7,
        out_specs=vmem,
        compiler_params=pltpu.CompilerParams(vmem_limit_bytes=VMEM_LIMIT),
    )(
        last_dev,
        user_rows,
        cand_user.reshape(1, -1),
        cand_emb,
        cross_down,
        cross_up,
        cross_bias.reshape(1, -1),
        score_weight.reshape(1, -1),
    )
    return scores.reshape(-1)


def body(
    projected,
    history_in,
    norm_gain,
    out_proj,
    user_spans,
    user_tails,
    cand_emb,
    cand_user,
    cross_down,
    cross_up,
    cross_bias,
    score_weight,
):
    peers = lax.axis_size("seq")
    place, last_dev = find_place(lax.axis_index("seq"), user_spans, user_tails)
    branches = [functools.partial(group_attention, 1, 0, peers)]
    for span in range(2, SPAN + 1):
        for residue in range(SPAN):
            branches.append(functools.partial(group_attention, span, residue, peers))
    totals = lax.switch(place[4], branches, place, projected)
    history_out, final_row = finish(place, totals, projected, history_in, norm_gain, out_proj)
    user_rows = lax.all_gather(final_row, "seq", axis=0, tiled=True)
    scores = score(
        last_dev, user_rows, cand_user, cand_emb, cross_down, cross_up, cross_bias, score_weight
    )
    return (history_out, scores)


def solution(mesh):
    in_specs = (
        P(("rep", "seq"), None),
        P(("rep", "seq"), None),
        P(),
        P(),
        P("rep"),
        P("rep"),
        P(("rep", "seq"), None),
        P(("rep", "seq")),
        P(),
        P(),
        P(),
        P(),
    )
    out_specs = (P(("rep", "seq"), None), P(("rep", "seq")))
    return jax.shard_map(body, mesh=mesh, in_specs=in_specs, out_specs=out_specs, check_vma=False)
```

```python
import functools

import jax
import jax.numpy as jnp
from jax import lax
from jax.experimental import pallas as pl
from jax.experimental.pallas import tpu as pltpu
from jax.sharding import PartitionSpec as P

HEADS = 8
SPAN = 4
CHUNKS = 2
VMEM_LIMIT = 32 * 1024 * 1024


def silu_weights(logits, score_scale):
    half = logits * (0.5 * score_scale)
    return half + half * jnp.tanh(half)


def row_tile(row_count):
    return 256 if row_count % 256 == 0 else row_count


def dot_nt(left, right):
    return lax.dot_general(left, right, (((1,), (1,)), ((), ())), preferred_element_type=jnp.float32)


def place_kernel(me_ref, spans_ref, tails_ref, place_ref, last_ref):
    users = spans_ref.shape[0]
    me = me_ref[0]

    def visit(user, state):
        begin, span, start, tail = state
        end = begin + spans_ref[user]
        mine = (begin <= me) & (me < end)
        last_ref[user] = end - 1
        return (
            end,
            jnp.where(mine, spans_ref[user], span),
            jnp.where(mine, begin, start),
            jnp.where(mine, tails_ref[user], tail),
        )

    zero = jnp.int32(0)
    _, span, start, tail = lax.fori_loop(0, users, visit, (zero, zero + 1, zero, zero))
    place_ref[0] = span
    place_ref[1] = start
    place_ref[2] = me - start
    place_ref[3] = tail
    place_ref[4] = jnp.where(span < 2, 0, 1 + (span - 2) * SPAN + lax.rem(start, SPAN))


def find_place(me, user_spans, user_tails):
    smem = pl.BlockSpec(memory_space=pltpu.SMEM)
    return pl.pallas_call(
        place_kernel,
        out_shape=(
            jax.ShapeDtypeStruct((8,), jnp.int32),
            jax.ShapeDtypeStruct(user_spans.shape, jnp.int32),
        ),
        in_specs=[smem] * 3,
        out_specs=(smem, smem),
    )(me.reshape(1), user_spans, user_tails)


def own_kernel(score_scale, q_ref, k_ref, v_ref, out_ref):
    row_count = q_ref.shape[0]
    tile = row_tile(row_count)

    @pl.loop(0, row_count // tile)
    def _(step):
        rows = pl.ds(pl.multiple_of(step * tile, tile), tile)
        out_ref[rows, :] = jnp.zeros((tile, q_ref.shape[1]), jnp.float32)

        @pl.loop(0, step + 1)
        def _(key_step):
            keys = pl.ds(pl.multiple_of(key_step * tile, tile), tile)
            weights = silu_weights(dot_nt(q_ref[rows, :], k_ref[keys, :]), score_scale)
            row_ids = step * tile + lax.broadcasted_iota(jnp.int32, weights.shape, 0)
            key_ids = key_step * tile + lax.broadcasted_iota(jnp.int32, weights.shape, 1)
            weights = jnp.where(key_ids <= row_ids, weights, 0.0).astype(jnp.bfloat16)
            out_ref[rows, :] += jnp.dot(weights, v_ref[keys, :], preferred_element_type=jnp.float32)


def own_attention(projected):
    row_count, width = projected.shape
    model_width = width // 4
    head_size = model_width // HEADS

    def columns(part):
        return pl.BlockSpec((row_count, head_size), lambda head: (0, part * HEADS + head))

    return pl.pallas_call(
        functools.partial(own_kernel, head_size ** (-0.5)),
        out_shape=jax.ShapeDtypeStruct((row_count, model_width), jnp.float32),
        grid=(HEADS,),
        in_specs=[columns(1), columns(2), columns(3)],
        out_specs=pl.BlockSpec((row_count, head_size), lambda head: (0, head)),
        compiler_params=pltpu.CompilerParams(vmem_limit_bytes=VMEM_LIMIT),
        cost_estimate=pl.CostEstimate(
            flops=4 * row_count * row_count * model_width,
            bytes_accessed=10 * row_count * model_width,
            transcendentals=row_count * row_count * HEADS,
        ),
    )(projected, projected, projected)


def add_kernel(score_scale, holders, place_ref, q_ref, *refs):
    source_refs, (total_ref, out_ref, slots, arrived) = refs[: len(holders)], refs[-4:]
    head, position = pl.program_id(0), place_ref[2]
    row_count, head_size = q_ref.shape
    tile = row_tile(row_count)
    counts = {}
    for source_ref, positions in zip(source_refs, holders):
        for place in positions:
            slot = counts.get(place, 0)
            counts[place] = slot + 1

            @pl.when((head == 0) & (position == place))
            def _():
                pltpu.make_async_copy(source_ref, slots.at[slot], arrived.at[slot]).start()

    out_ref[...] = total_ref[...]
    count = sum(jnp.where(position == place, number, 0) for place, number in counts.items())
    low = pl.multiple_of(head * head_size, head_size)
    key_columns = pl.ds(low, head_size)
    value_columns = pl.ds(pl.multiple_of(slots.shape[2] // 2 + low, head_size), head_size)

    @pl.loop(0, count)
    def _(slot):
        @pl.when(head == 0)
        def _():
            pltpu.make_async_copy(source_refs[0], slots.at[slot], arrived.at[slot]).wait()

        @pl.loop(0, row_count // tile)
        def _(step):
            rows = pl.ds(pl.multiple_of(step * tile, tile), tile)
            logits = dot_nt(q_ref[rows, :], slots[slot, :, key_columns])
            weights = silu_weights(logits, score_scale).astype(jnp.bfloat16)
            out_ref[rows, :] += jnp.dot(
                weights, slots[slot, :, value_columns], preferred_element_type=jnp.float32
            )


def add_sources(place, projected, totals, sources, first_head):
    row_count, width = projected.shape
    model_width = width // 4
    head_size = model_width // HEADS
    arrays = [array for array, _ in sources]
    holders = [positions for _, positions in sources]
    everyone = [position for positions in holders for position in positions]
    most = max(everyone.count(position) for position in everyone)
    heads = arrays[0].shape[1] // (2 * head_size)
    total_spec = pl.BlockSpec((row_count, head_size), lambda head, place: (0, first_head + head))
    return pl.pallas_call(
        functools.partial(add_kernel, head_size ** (-0.5), holders),
        out_shape=jax.ShapeDtypeStruct(totals.shape, totals.dtype),
        grid_spec=pltpu.PrefetchScalarGridSpec(
            num_scalar_prefetch=1,
            grid=(heads,),
            in_specs=[
                pl.BlockSpec((row_count, head_size), lambda head, place: (0, HEADS + first_head + head)),
                *[pl.BlockSpec(memory_space=pl.ANY)] * len(arrays),
                total_spec,
            ],
            out_specs=total_spec,
            scratch_shapes=[
                pltpu.VMEM((most, *arrays[0].shape), projected.dtype),
                pltpu.SemaphoreType.DMA((most,)),
            ],
        ),
        input_output_aliases={2 + len(arrays): 0},
        compiler_params=pltpu.CompilerParams(vmem_limit_bytes=VMEM_LIMIT),
        cost_estimate=pl.CostEstimate(
            flops=4 * row_count * row_count * heads * head_size * most,
            bytes_accessed=(6 + 4 * most) * row_count * heads * head_size,
            transcendentals=row_count * row_count * heads * most,
        ),
    )(place, projected, *arrays, totals)


def pack_kernel(k_ref, v_ref, after_ref, out_ref):
    width = k_ref.shape[1]
    out_ref[:, :width] = k_ref[...]
    out_ref[:, width:] = v_ref[...]


def pack_key_values(projected, after, index):
    row_count, width = projected.shape
    chunk = width // 4 // CHUNKS
    return pl.pallas_call(
        pack_kernel,
        out_shape=jax.ShapeDtypeStruct((row_count, 2 * chunk), projected.dtype),
        grid=(1,),
        in_specs=[
            pl.BlockSpec((row_count, chunk), lambda step: (0, 2 * CHUNKS + index)),
            pl.BlockSpec((row_count, chunk), lambda step: (0, 3 * CHUNKS + index)),
            pl.BlockSpec(memory_space=pl.ANY),
        ],
        out_specs=pl.BlockSpec((row_count, 2 * chunk), lambda step: (0, 0)),
        compiler_params=pltpu.CompilerParams(vmem_limit_bytes=VMEM_LIMIT),
        cost_estimate=pl.CostEstimate(
            flops=0, bytes_accessed=8 * row_count * chunk, transcendentals=0
        ),
    )(projected, projected, after)


def group_attention(span, residue, peers, place, projected):
    if span == 1:
        return own_attention(projected)

    def send(array, position, by):
        lowest = (residue + position) % SPAN
        pairs = [(s, s + by) for s in range(lowest, peers, SPAN) if s + by < peers]
        return lax.ppermute(array, "seq", pairs)

    def swap(array, position):
        lowest = (residue + position) % SPAN
        pairs = [(s, s + 1) for s in range(lowest, peers, SPAN) if s + 1 < peers]
        return lax.ppermute(array, "seq", pairs + [(b, a) for a, b in pairs])

    chips = {}
    for position in range(span):
        chips.setdefault((residue + position) // 2, []).append(position)
    chips = list(chips.values())
    inner = [chip for chip in chips if len(chip) == 2]
    sources = []
    crossing = [projected] * CHUNKS
    for index in range(CHUNKS):
        after = crossing[index - 2] if index >= 2 else place
        mine = pack_key_values(projected, after, index)
        found = []
        for near, chip in enumerate(chips):
            for far in chips[near + 1 :]:
                if len(far) == 1:
                    for position in chip:
                        came = send(mine, position, far[0] - position)
                        found.append((came, [far[0]]))
                elif len(chip) == 1:
                    came = send(mine, chip[0], far[1] - chip[0])
                    found.append((came, [far[1]]))
                    found.append((swap(came, far[0]), [far[0]]))
                else:
                    came = send(mine, chip[0], 2) + send(mine, chip[1], 2)
                    found += [(came, far), (swap(came, far[0]), far)]
                crossing[index] = came
        for chip in inner:
            found.append((send(mine, chip[0], 1), [chip[1]]))
            if len(chips) == 1:
                crossing[index] = found[-1][0]
        sources.append(found)
    totals = own_attention(projected)
    heads = HEADS // CHUNKS
    for index in range(CHUNKS):
        totals = add_sources(place, projected, totals, sources[index], index * heads)
    return totals


def finish_kernel(place_ref, total_ref, u_ref, history_ref, gain_ref, weight_ref, out_ref, last_ref):
    step = pl.program_id(0)
    tile = total_ref.shape[0]
    row_count = tile * pl.num_programs(0)
    span, position, tail = place_ref[0], place_ref[2], place_ref[3]
    valid = jnp.where(position == span - 1, tail, row_count)
    row_ids = step * tile + lax.broadcasted_iota(jnp.int32, (tile, 1), 0)
    attention = jnp.where(row_ids < valid, total_ref[...], 0.0)
    row_mean = jnp.mean(attention, axis=1, keepdims=True)
    centered = attention - row_mean
    row_var = jnp.mean(centered * centered, axis=1, keepdims=True)
    normed = centered * lax.rsqrt(row_var + 1e-06) * gain_ref[...]
    gated = (normed * u_ref[...].astype(jnp.float32)).astype(jnp.bfloat16)
    out = jnp.dot(gated, weight_ref[...], preferred_element_type=jnp.float32)
    out = (out + history_ref[...].astype(jnp.float32)).astype(jnp.bfloat16)
    out_ref[...] = out
    final = jnp.sum(jnp.where(row_ids == valid - 1, out.astype(jnp.float32), 0.0), axis=0, keepdims=True)

    @pl.when(step == 0)
    def _():
        last_ref[...] = final

    @pl.when(step > 0)
    def _():
        last_ref[...] += final


def finish(place, totals, projected, history_in, norm_gain, out_proj):
    row_count, model_width = history_in.shape
    tile = row_tile(row_count)
    rows = pl.BlockSpec((tile, model_width), lambda step, place: (step, 0))
    whole = pl.BlockSpec((1, model_width), lambda step, place: (0, 0))
    return pl.pallas_call(
        finish_kernel,
        out_shape=(
            jax.ShapeDtypeStruct(history_in.shape, history_in.dtype),
            jax.ShapeDtypeStruct((1, model_width), jnp.float32),
        ),
        grid_spec=pltpu.PrefetchScalarGridSpec(
            num_scalar_prefetch=1,
            grid=(row_count // tile,),
            in_specs=[
                rows,
                rows,
                rows,
                whole,
                pl.BlockSpec(out_proj.shape, lambda step, place: (0, 0)),
            ],
            out_specs=(rows, whole),
        ),
        compiler_params=pltpu.CompilerParams(vmem_limit_bytes=VMEM_LIMIT),
        cost_estimate=pl.CostEstimate(
            flops=2 * row_count * model_width * model_width,
            bytes_accessed=10 * row_count * model_width + 2 * model_width * model_width,
            transcendentals=row_count,
        ),
    )(place, totals, projected, history_in, norm_gain.reshape(1, -1), out_proj)


def score_kernel(last_ref, rows_ref, user_ref, cand_ref, down_ref, up_ref, bias_ref, weight_ref, out_ref):
    peers, model_width = rows_ref.shape
    cand_count = cand_ref.shape[0]
    cand_user = user_ref[...]

    def visit(user, found):
        return jnp.where(cand_user == user, last_ref[user], found)

    cand_dev = lax.fori_loop(0, last_ref.shape[0], visit, jnp.zeros_like(cand_user))
    device_ids = lax.broadcasted_iota(jnp.int32, (peers, cand_count), 0)
    selector = jnp.where(device_ids == cand_dev, 1.0, 0.0).astype(jnp.bfloat16)
    user_part = lax.dot_general(
        selector,
        rows_ref[...].astype(jnp.bfloat16),
        (((0,), (0,)), ((), ())),
        preferred_element_type=jnp.float32,
    ).astype(jnp.bfloat16)
    cand_part = cand_ref[...]
    low_rank = jnp.dot(user_part, down_ref[:model_width, :], preferred_element_type=jnp.float32)
    low_rank += jnp.dot(cand_part, down_ref[model_width:, :], preferred_element_type=jnp.float32)
    low_rank = low_rank.astype(jnp.bfloat16)
    score = jnp.zeros((cand_count, 1), jnp.float32)
    for part, low in ((user_part, 0), (cand_part, model_width)):
        cut = slice(low, low + model_width)
        up_part = jnp.dot(low_rank, up_ref[:, cut], preferred_element_type=jnp.float32)
        value = part.astype(jnp.float32)
        crossed = value * (up_part + bias_ref[:, cut]) + value
        score += jnp.sum(crossed * weight_ref[:, cut], axis=1, keepdims=True)
    row_ids = lax.broadcasted_iota(jnp.int32, (cand_count, cand_count), 0)
    column_ids = lax.broadcasted_iota(jnp.int32, (cand_count, cand_count), 1)
    out_ref[...] = jnp.sum(jnp.where(row_ids == column_ids, score, 0.0), axis=0, keepdims=True)


def score(last_dev, user_rows, cand_user, cand_emb, cross_down, cross_up, cross_bias, score_weight):
    vmem = pl.BlockSpec(memory_space=pltpu.VMEM)
    cand_count = cand_emb.shape[0]
    scores = pl.pallas_call(
        score_kernel,
        out_shape=jax.ShapeDtypeStruct((1, cand_count), jnp.float32),
        in_specs=[pl.BlockSpec(memory_space=pltpu.SMEM)] + [vmem] * 7,
        out_specs=vmem,
        compiler_params=pltpu.CompilerParams(vmem_limit_bytes=VMEM_LIMIT),
    )(
        last_dev,
        user_rows,
        cand_user.reshape(1, -1),
        cand_emb,
        cross_down,
        cross_up,
        cross_bias.reshape(1, -1),
        score_weight.reshape(1, -1),
    )
    return scores.reshape(-1)


def body(
    projected,
    history_in,
    norm_gain,
    out_proj,
    user_spans,
    user_tails,
    cand_emb,
    cand_user,
    cross_down,
    cross_up,
    cross_bias,
    score_weight,
):
    peers = lax.axis_size("seq")
    place, last_dev = find_place(lax.axis_index("seq"), user_spans, user_tails)
    branches = [functools.partial(group_attention, 1, 0, peers)]
    for span in range(2, SPAN + 1):
        for residue in range(SPAN):
            branches.append(functools.partial(group_attention, span, residue, peers))
    totals = lax.switch(place[4], branches, place, projected)
    history_out, final_row = finish(place, totals, projected, history_in, norm_gain, out_proj)
    user_rows = lax.all_gather(final_row, "seq", axis=0, tiled=True)
    scores = score(
        last_dev, user_rows, cand_user, cand_emb, cross_down, cross_up, cross_bias, score_weight
    )
    return (history_out, scores)


def solution(mesh):
    in_specs = (
        P(("rep", "seq"), None),
        P(("rep", "seq"), None),
        P(),
        P(),
        P("rep"),
        P("rep"),
        P(("rep", "seq"), None),
        P(("rep", "seq")),
        P(),
        P(),
        P(),
        P(),
    )
    out_specs = (P(("rep", "seq"), None), P(("rep", "seq")))
    return jax.shard_map(body, mesh=mesh, in_specs=in_specs, out_specs=out_specs, check_vma=False)
```

```python
import functools

import jax
import jax.numpy as jnp
from jax import lax
from jax.experimental import pallas as pl
from jax.experimental.pallas import tpu as pltpu
from jax.sharding import PartitionSpec as P

HEADS = 8
SPAN = 4
CHUNK_PARTS = (5, 3)
COST_SCALE = 5
VMEM_LIMIT = 32 * 1024 * 1024


def silu_weights(logits, score_scale):
    half = logits * (0.5 * score_scale)
    return half + half * jnp.tanh(half)


def row_tile(row_count):
    return 256 if row_count % 256 == 0 else row_count


def dot_nt(left, right):
    return lax.dot_general(left, right, (((1,), (1,)), ((), ())), preferred_element_type=jnp.float32)


def place_kernel(me_ref, spans_ref, tails_ref, place_ref, last_ref):
    users = spans_ref.shape[0]
    me = me_ref[0]

    def visit(user, state):
        begin, span, start, tail = state
        end = begin + spans_ref[user]
        mine = (begin <= me) & (me < end)
        last_ref[user] = end - 1
        return (
            end,
            jnp.where(mine, spans_ref[user], span),
            jnp.where(mine, begin, start),
            jnp.where(mine, tails_ref[user], tail),
        )

    zero = jnp.int32(0)
    _, span, start, tail = lax.fori_loop(0, users, visit, (zero, zero + 1, zero, zero))
    place_ref[0] = span
    place_ref[1] = start
    place_ref[2] = me - start
    place_ref[3] = tail
    place_ref[4] = jnp.where(span < 2, 0, 1 + (span - 2) * SPAN + lax.rem(start, SPAN))


def find_place(me, user_spans, user_tails):
    smem = pl.BlockSpec(memory_space=pltpu.SMEM)
    return pl.pallas_call(
        place_kernel,
        out_shape=(
            jax.ShapeDtypeStruct((8,), jnp.int32),
            jax.ShapeDtypeStruct(user_spans.shape, jnp.int32),
        ),
        in_specs=[smem] * 3,
        out_specs=(smem, smem),
    )(me.reshape(1), user_spans, user_tails)


def own_kernel(score_scale, q_ref, k_ref, v_ref, out_ref):
    row_count = q_ref.shape[0]
    tile = row_tile(row_count)
    for first in range(0, row_count, tile):
        last = first + tile
        weights = silu_weights(dot_nt(q_ref[first:last, :], k_ref[:last, :]), score_scale)
        row_ids = first + lax.broadcasted_iota(jnp.int32, weights.shape, 0)
        key_ids = lax.broadcasted_iota(jnp.int32, weights.shape, 1)
        weights = jnp.where(key_ids <= row_ids, weights, 0.0).astype(jnp.bfloat16)
        out_ref[first:last, :] = jnp.dot(
            weights, v_ref[:last, :], preferred_element_type=jnp.float32
        )


def own_attention(projected):
    row_count, width = projected.shape
    model_width = width // 4
    head_size = model_width // HEADS

    def columns(part):
        return pl.BlockSpec((row_count, head_size), lambda head: (0, part * HEADS + head))

    return pl.pallas_call(
        functools.partial(own_kernel, head_size ** (-0.5)),
        out_shape=jax.ShapeDtypeStruct((row_count, model_width), jnp.float32),
        grid=(HEADS,),
        in_specs=[columns(1), columns(2), columns(3)],
        out_specs=pl.BlockSpec((row_count, head_size), lambda head: (0, head)),
        compiler_params=pltpu.CompilerParams(vmem_limit_bytes=VMEM_LIMIT),
        cost_estimate=pl.CostEstimate(
            flops=COST_SCALE * 3 * row_count * row_count * model_width,
            bytes_accessed=10 * row_count * model_width,
            transcendentals=row_count * row_count * HEADS,
        ),
    )(projected, projected, projected)


def add_kernel(score_scale, holders, place_ref, q_ref, *refs):
    source_refs, (total_ref, out_ref, slots, arrived) = refs[: len(holders)], refs[-4:]
    head, position = pl.program_id(0), place_ref[2]
    row_count, head_size = q_ref.shape
    tile = row_tile(row_count)
    counts = {}
    for source_ref, positions in zip(source_refs, holders):
        for place in positions:
            slot = counts.get(place, 0)
            counts[place] = slot + 1

            @pl.when((head == 0) & (position == place))
            def _():
                pltpu.make_async_copy(source_ref, slots.at[slot], arrived.at[slot]).start()

    out_ref[...] = total_ref[...]
    count = sum(jnp.where(position == place, number, 0) for place, number in counts.items())
    key_columns = pl.ds(pl.multiple_of(2 * head * head_size, head_size), head_size)
    value_columns = pl.ds(pl.multiple_of((2 * head + 1) * head_size, head_size), head_size)

    @pl.loop(0, count)
    def _(slot):
        @pl.when(head == 0)
        def _():
            pltpu.make_async_copy(source_refs[0], slots.at[slot], arrived.at[slot]).wait()

        for first in range(0, row_count, tile):
            rows = slice(first, first + tile)
            logits = dot_nt(q_ref[rows, :], slots[slot, :, key_columns])
            weights = silu_weights(logits, score_scale).astype(jnp.bfloat16)
            out_ref[rows, :] += jnp.dot(
                weights, slots[slot, :, value_columns], preferred_element_type=jnp.float32
            )


def add_sources(place, projected, totals, sources, first_head):
    row_count, width = projected.shape
    model_width = width // 4
    head_size = model_width // HEADS
    arrays = [array for array, _ in sources]
    holders = [positions for _, positions in sources]
    everyone = [position for positions in holders for position in positions]
    most = max(everyone.count(position) for position in everyone)
    heads = arrays[0].shape[1] // (2 * head_size)
    total_spec = pl.BlockSpec((row_count, head_size), lambda head, place: (0, first_head + head))
    return pl.pallas_call(
        functools.partial(add_kernel, head_size ** (-0.5), holders),
        out_shape=jax.ShapeDtypeStruct(totals.shape, totals.dtype),
        grid_spec=pltpu.PrefetchScalarGridSpec(
            num_scalar_prefetch=1,
            grid=(heads,),
            in_specs=[
                pl.BlockSpec((row_count, head_size), lambda head, place: (0, HEADS + first_head + head)),
                *[pl.BlockSpec(memory_space=pl.ANY)] * len(arrays),
                total_spec,
            ],
            out_specs=total_spec,
            scratch_shapes=[
                pltpu.VMEM((most, *arrays[0].shape), projected.dtype),
                pltpu.SemaphoreType.DMA((most,)),
            ],
        ),
        input_output_aliases={2 + len(arrays): 0},
        compiler_params=pltpu.CompilerParams(vmem_limit_bytes=VMEM_LIMIT),
        cost_estimate=pl.CostEstimate(
            flops=COST_SCALE * 4 * row_count * row_count * heads * head_size * most,
            bytes_accessed=(6 + 4 * most) * row_count * heads * head_size,
            transcendentals=row_count * row_count * heads * most,
        ),
    )(place, projected, *arrays, totals)


def pack_kernel(k_ref, v_ref, out_ref):
    width = k_ref.shape[1]
    out_ref[:, :width] = k_ref[...]
    out_ref[:, width:] = v_ref[...]


def pack_key_values(projected, first_head, heads):
    row_count, width = projected.shape
    head_size = width // 4 // HEADS
    return pl.pallas_call(
        pack_kernel,
        out_shape=jax.ShapeDtypeStruct((row_count, 2 * heads * head_size), projected.dtype),
        grid=(heads,),
        in_specs=[
            pl.BlockSpec((row_count, head_size), lambda head: (0, 2 * HEADS + first_head + head)),
            pl.BlockSpec((row_count, head_size), lambda head: (0, 3 * HEADS + first_head + head)),
        ],
        out_specs=pl.BlockSpec((row_count, 2 * head_size), lambda head: (0, head)),
        compiler_params=pltpu.CompilerParams(vmem_limit_bytes=VMEM_LIMIT),
        cost_estimate=pl.CostEstimate(
            flops=0, bytes_accessed=8 * row_count * heads * head_size, transcendentals=0
        ),
    )(projected, projected)


def group_attention(span, residue, peers, place, projected):
    if span == 1:
        return own_attention(projected)

    def send(array, *hops):
        pairs = []
        for position, target in hops:
            lowest, by = (residue + position) % SPAN, target - position
            pairs += [(s, s + by) for s in range(lowest, peers, SPAN) if s + by < peers]
        return lax.ppermute(array, "seq", pairs)

    def swap(array, position):
        lowest = (residue + position) % SPAN
        pairs = [(s, s + 1) for s in range(lowest, peers, SPAN) if s + 1 < peers]
        return lax.ppermute(array, "seq", pairs + [(b, a) for a, b in pairs])

    chips = {}
    for position in range(span):
        chips.setdefault((residue + position) // 2, []).append(position)
    chips = list(chips.values())
    chunks, first_head = [], 0
    for heads in CHUNK_PARTS:
        mine = pack_key_values(projected, first_head, heads)
        found = []
        inner = [tuple(chip) for chip in chips if len(chip) == 2]
        if len(chips) == 1:
            found.append((send(mine, *inner), [1]))
        elif len(chips) == 3:
            came = send(mine, (0, 2), (1, 3))
            found.append((came, [2, 3]))
            found.append((send(mine, (2, 3)), [3]))
            found.append((send(mine, (0, 3), (1, 2)), [2, 3]))
            found.append((swap(came, 1), [1]))
        elif span == 4:
            came = send(mine, (0, 2), (1, 3))
            found += [(came, [2, 3]), (swap(came, 2), [2, 3])]
            found.append((send(mine, *inner), [1, 3]))
        elif span == 2:
            found.append((send(mine, (0, 1)), [1]))
        elif len(chips[0]) == 2:
            found.append((send(mine, (0, 2)), [2]))
            found.append((send(mine, (1, 2)), [2]))
            found.append((send(mine, *inner), [1]))
        else:
            came = send(mine, (0, 2))
            found += [(came, [2]), (swap(came, 1), [1])]
            found.append((send(mine, *inner), [2]))
        chunks.append((first_head, found))
        first_head += heads
    totals = own_attention(projected)
    for first_head, found in chunks:
        totals = add_sources(place, projected, totals, found, first_head)
    return totals


def finish_kernel(place_ref, total_ref, u_ref, history_ref, gain_ref, weight_ref, out_ref, last_ref):
    step = pl.program_id(0)
    tile = total_ref.shape[0]
    row_count = tile * pl.num_programs(0)
    span, position, tail = place_ref[0], place_ref[2], place_ref[3]
    valid = jnp.where(position == span - 1, tail, row_count)
    row_ids = step * tile + lax.broadcasted_iota(jnp.int32, (tile, 1), 0)
    attention = jnp.where(row_ids < valid, total_ref[...], 0.0)
    row_mean = jnp.mean(attention, axis=1, keepdims=True)
    centered = attention - row_mean
    row_var = jnp.mean(centered * centered, axis=1, keepdims=True)
    normed = centered * lax.rsqrt(row_var + 1e-06) * gain_ref[...]
    gated = (normed * u_ref[...].astype(jnp.float32)).astype(jnp.bfloat16)
    out = jnp.dot(gated, weight_ref[...], preferred_element_type=jnp.float32)
    out = (out + history_ref[...].astype(jnp.float32)).astype(jnp.bfloat16)
    out_ref[...] = out
    final = jnp.sum(jnp.where(row_ids == valid - 1, out.astype(jnp.float32), 0.0), axis=0, keepdims=True)

    @pl.when(step == 0)
    def _():
        last_ref[...] = final

    @pl.when(step > 0)
    def _():
        last_ref[...] += final


def finish(place, totals, projected, history_in, norm_gain, out_proj):
    row_count, model_width = history_in.shape
    tile = row_tile(row_count)
    rows = pl.BlockSpec((tile, model_width), lambda step, place: (step, 0))
    whole = pl.BlockSpec((1, model_width), lambda step, place: (0, 0))
    return pl.pallas_call(
        finish_kernel,
        out_shape=(
            jax.ShapeDtypeStruct(history_in.shape, history_in.dtype),
            jax.ShapeDtypeStruct((1, model_width), jnp.float32),
        ),
        grid_spec=pltpu.PrefetchScalarGridSpec(
            num_scalar_prefetch=1,
            grid=(row_count // tile,),
            in_specs=[
                rows,
                rows,
                rows,
                whole,
                pl.BlockSpec(out_proj.shape, lambda step, place: (0, 0)),
            ],
            out_specs=(rows, whole),
        ),
        compiler_params=pltpu.CompilerParams(vmem_limit_bytes=VMEM_LIMIT),
        cost_estimate=pl.CostEstimate(
            flops=2 * row_count * model_width * model_width,
            bytes_accessed=10 * row_count * model_width + 2 * model_width * model_width,
            transcendentals=row_count,
        ),
    )(place, totals, projected, history_in, norm_gain.reshape(1, -1), out_proj)


def score_kernel(last_ref, rows_ref, user_ref, cand_ref, down_ref, up_ref, bias_ref, weight_ref, out_ref):
    peers, model_width = rows_ref.shape
    cand_count = cand_ref.shape[0]
    cand_user = user_ref[...]

    def visit(user, found):
        return jnp.where(cand_user == user, last_ref[user], found)

    cand_dev = lax.fori_loop(0, last_ref.shape[0], visit, jnp.zeros_like(cand_user))
    device_ids = lax.broadcasted_iota(jnp.int32, (peers, cand_count), 0)
    selector = jnp.where(device_ids == cand_dev, 1.0, 0.0).astype(jnp.bfloat16)
    user_part = lax.dot_general(
        selector,
        rows_ref[...].astype(jnp.bfloat16),
        (((0,), (0,)), ((), ())),
        preferred_element_type=jnp.float32,
    ).astype(jnp.bfloat16)
    cand_part = cand_ref[...]
    low_rank = jnp.dot(user_part, down_ref[:model_width, :], preferred_element_type=jnp.float32)
    low_rank += jnp.dot(cand_part, down_ref[model_width:, :], preferred_element_type=jnp.float32)
    low_rank = low_rank.astype(jnp.bfloat16)
    score = jnp.zeros((cand_count, 1), jnp.float32)
    for part, low in ((user_part, 0), (cand_part, model_width)):
        cut = slice(low, low + model_width)
        up_part = jnp.dot(low_rank, up_ref[:, cut], preferred_element_type=jnp.float32)
        value = part.astype(jnp.float32)
        crossed = value * (up_part + bias_ref[:, cut]) + value
        score += jnp.sum(crossed * weight_ref[:, cut], axis=1, keepdims=True)
    row_ids = lax.broadcasted_iota(jnp.int32, (cand_count, cand_count), 0)
    column_ids = lax.broadcasted_iota(jnp.int32, (cand_count, cand_count), 1)
    out_ref[...] = jnp.sum(jnp.where(row_ids == column_ids, score, 0.0), axis=0, keepdims=True)


def score(last_dev, user_rows, cand_user, cand_emb, cross_down, cross_up, cross_bias, score_weight):
    vmem = pl.BlockSpec(memory_space=pltpu.VMEM)
    cand_count = cand_emb.shape[0]
    scores = pl.pallas_call(
        score_kernel,
        out_shape=jax.ShapeDtypeStruct((1, cand_count), jnp.float32),
        in_specs=[pl.BlockSpec(memory_space=pltpu.SMEM)] + [vmem] * 7,
        out_specs=vmem,
        compiler_params=pltpu.CompilerParams(vmem_limit_bytes=VMEM_LIMIT),
    )(
        last_dev,
        user_rows,
        cand_user.reshape(1, -1),
        cand_emb,
        cross_down,
        cross_up,
        cross_bias.reshape(1, -1),
        score_weight.reshape(1, -1),
    )
    return scores.reshape(-1)


def body(
    projected,
    history_in,
    norm_gain,
    out_proj,
    user_spans,
    user_tails,
    cand_emb,
    cand_user,
    cross_down,
    cross_up,
    cross_bias,
    score_weight,
):
    peers = lax.axis_size("seq")
    place, last_dev = find_place(lax.axis_index("seq"), user_spans, user_tails)
    branches = [functools.partial(group_attention, 1, 0, peers)]
    for span in range(2, SPAN + 1):
        for residue in range(SPAN):
            branches.append(functools.partial(group_attention, span, residue, peers))
    totals = lax.switch(place[4], branches, place, projected)
    history_out, final_row = finish(place, totals, projected, history_in, norm_gain, out_proj)
    user_rows = lax.all_gather(final_row, "seq", axis=0, tiled=True)
    scores = score(
        last_dev, user_rows, cand_user, cand_emb, cross_down, cross_up, cross_bias, score_weight
    )
    return (history_out, scores)


def solution(mesh):
    in_specs = (
        P(("rep", "seq"), None),
        P(("rep", "seq"), None),
        P(),
        P(),
        P("rep"),
        P("rep"),
        P(("rep", "seq"), None),
        P(("rep", "seq")),
        P(),
        P(),
        P(),
        P(),
    )
    out_specs = (P(("rep", "seq"), None), P(("rep", "seq")))
    return jax.shard_map(body, mesh=mesh, in_specs=in_specs, out_specs=out_specs, check_vma=False)
```

```python
import functools

import jax
import jax.numpy as jnp
from jax import lax
from jax.experimental import pallas as pl
from jax.experimental.pallas import tpu as pltpu
from jax.sharding import PartitionSpec as P

HEADS = 8
SPAN = 4
CHUNK_PARTS = (5, 3)
COST_SCALE = 5
VMEM_LIMIT = 63 * 1024 * 1024


def silu_weights(logits, score_scale):
    half = logits * (0.5 * score_scale)
    return half + half * jnp.tanh(half)


def row_tile(row_count):
    return 256 if row_count % 256 == 0 else row_count


def dot_nt(left, right):
    return lax.dot_general(left, right, (((1,), (1,)), ((), ())), preferred_element_type=jnp.float32)


def place_kernel(me_ref, spans_ref, tails_ref, place_ref, last_ref):
    users = spans_ref.shape[0]
    me = me_ref[0]

    def visit(user, state):
        begin, span, start, tail = state
        end = begin + spans_ref[user]
        mine = (begin <= me) & (me < end)
        last_ref[user] = end - 1
        return (
            end,
            jnp.where(mine, spans_ref[user], span),
            jnp.where(mine, begin, start),
            jnp.where(mine, tails_ref[user], tail),
        )

    zero = jnp.int32(0)
    _, span, start, tail = lax.fori_loop(0, users, visit, (zero, zero + 1, zero, zero))
    place_ref[0] = span
    place_ref[1] = start
    place_ref[2] = me - start
    place_ref[3] = tail
    later = 3 + (span - 3) * SPAN + lax.rem(start, SPAN)
    place_ref[4] = jnp.where(span == 1, 0, jnp.where(span == 2, 1 + lax.rem(start, 2), later))


def find_place(me, user_spans, user_tails):
    smem = pl.BlockSpec(memory_space=pltpu.SMEM)
    return pl.pallas_call(
        place_kernel,
        out_shape=(
            jax.ShapeDtypeStruct((8,), jnp.int32),
            jax.ShapeDtypeStruct(user_spans.shape, jnp.int32),
        ),
        in_specs=[smem] * 3,
        out_specs=(smem, smem),
    )(me.reshape(1), user_spans, user_tails)


def own_kernel(score_scale, q_ref, k_ref, v_ref, out_ref):
    row_count = q_ref.shape[0]
    tile = row_tile(row_count)
    for first in range(0, row_count, tile):
        last = first + tile
        weights = silu_weights(dot_nt(q_ref[first:last, :], k_ref[:last, :]), score_scale)
        row_ids = first + lax.broadcasted_iota(jnp.int32, weights.shape, 0)
        key_ids = lax.broadcasted_iota(jnp.int32, weights.shape, 1)
        weights = jnp.where(key_ids <= row_ids, weights, 0.0).astype(jnp.bfloat16)
        out_ref[first:last, :] = jnp.dot(
            weights, v_ref[:last, :], preferred_element_type=jnp.float32
        )


def own_attention(projected):
    row_count, width = projected.shape
    model_width = width // 4
    head_size = model_width // HEADS

    def columns(part):
        return pl.BlockSpec((row_count, head_size), lambda head: (0, part * HEADS + head))

    return pl.pallas_call(
        functools.partial(own_kernel, head_size ** (-0.5)),
        out_shape=jax.ShapeDtypeStruct((row_count, model_width), jnp.float32),
        grid=(HEADS,),
        in_specs=[columns(1), columns(2), columns(3)],
        out_specs=pl.BlockSpec((row_count, head_size), lambda head: (0, head)),
        compiler_params=pltpu.CompilerParams(vmem_limit_bytes=VMEM_LIMIT),
        cost_estimate=pl.CostEstimate(
            flops=COST_SCALE * 3 * row_count * row_count * model_width,
            bytes_accessed=10 * row_count * model_width,
            transcendentals=row_count * row_count * HEADS,
        ),
    )(projected, projected, projected)


def add_kernel(score_scale, holders, skipped, unrolled, place_ref, q_ref, *refs):
    source_refs, (total_ref, out_ref, slots, arrived) = refs[: len(holders)], refs[-4:]
    head, position = pl.program_id(0), place_ref[2]
    row_count, head_size = q_ref.shape
    tile = row_tile(row_count)
    counts = {}
    for source_ref, positions in zip(source_refs, holders):
        for place in positions:
            slot = counts.get(place, 0)
            counts[place] = slot + 1

            @pl.when((head == 0) & (position == place))
            def _():
                pltpu.make_async_copy(source_ref, slots.at[slot], arrived.at[slot]).start()

    out_ref[...] = total_ref[...]
    count = sum(jnp.where(position == place, number, 0) for place, number in counts.items())
    low = 2 * (skipped + head) * head_size
    key_columns = pl.ds(pl.multiple_of(low, head_size), head_size)
    value_columns = pl.ds(pl.multiple_of(low + head_size, head_size), head_size)

    @pl.loop(0, count)
    def _(slot):
        @pl.when(head == 0)
        def _():
            pltpu.make_async_copy(source_refs[0], slots.at[slot], arrived.at[slot]).wait()

        def add_rows(step):
            rows = pl.ds(pl.multiple_of(step * tile, tile), tile)
            logits = dot_nt(q_ref[rows, :], slots[slot, :, key_columns])
            weights = silu_weights(logits, score_scale).astype(jnp.bfloat16)
            out_ref[rows, :] += jnp.dot(
                weights, slots[slot, :, value_columns], preferred_element_type=jnp.float32
            )

        if unrolled:
            for step in range(row_count // tile):
                add_rows(step)
        else:
            pl.loop(0, row_count // tile)(add_rows)


def add_sources(place, projected, totals, sources, first_head, skipped, heads, unrolled):
    row_count, width = projected.shape
    model_width = width // 4
    head_size = model_width // HEADS
    arrays = [array for array, _ in sources]
    holders = [positions for _, positions in sources]
    everyone = [position for positions in holders for position in positions]
    most = max(everyone.count(position) for position in everyone)
    first_head += skipped
    total_spec = pl.BlockSpec((row_count, head_size), lambda head, place: (0, first_head + head))
    return pl.pallas_call(
        functools.partial(add_kernel, head_size ** (-0.5), holders, skipped, unrolled),
        out_shape=jax.ShapeDtypeStruct(totals.shape, totals.dtype),
        grid_spec=pltpu.PrefetchScalarGridSpec(
            num_scalar_prefetch=1,
            grid=(heads,),
            in_specs=[
                pl.BlockSpec((row_count, head_size), lambda head, place: (0, HEADS + first_head + head)),
                *[pl.BlockSpec(memory_space=pl.ANY)] * len(arrays),
                total_spec,
            ],
            out_specs=total_spec,
            scratch_shapes=[
                pltpu.VMEM((most, *arrays[0].shape), projected.dtype),
                pltpu.SemaphoreType.DMA((most,)),
            ],
        ),
        input_output_aliases={2 + len(arrays): 0},
        compiler_params=pltpu.CompilerParams(vmem_limit_bytes=VMEM_LIMIT),
        cost_estimate=pl.CostEstimate(
            flops=COST_SCALE * 4 * row_count * row_count * heads * head_size * most,
            bytes_accessed=(6 + 4 * most) * row_count * heads * head_size,
            transcendentals=row_count * row_count * heads * most,
        ),
    )(place, projected, *arrays, totals)


def pack_kernel(k_ref, v_ref, after_ref, out_ref):
    width = k_ref.shape[1]
    out_ref[:, :width] = k_ref[...]
    out_ref[:, width:] = v_ref[...]


def pack_key_values(projected, after, first_head, heads):
    row_count, width = projected.shape
    head_size = width // 4 // HEADS
    return pl.pallas_call(
        pack_kernel,
        out_shape=jax.ShapeDtypeStruct((row_count, 2 * heads * head_size), projected.dtype),
        grid=(heads,),
        in_specs=[
            pl.BlockSpec((row_count, head_size), lambda head: (0, 2 * HEADS + first_head + head)),
            pl.BlockSpec((row_count, head_size), lambda head: (0, 3 * HEADS + first_head + head)),
            pl.BlockSpec(memory_space=pl.ANY),
        ],
        out_specs=pl.BlockSpec((row_count, 2 * head_size), lambda head: (0, head)),
        compiler_params=pltpu.CompilerParams(vmem_limit_bytes=VMEM_LIMIT),
        cost_estimate=pl.CostEstimate(
            flops=0, bytes_accessed=8 * row_count * heads * head_size, transcendentals=0
        ),
    )(projected, projected, after)


def tie_kernel(array_ref, after_ref, out_ref):
    pass


def tie(array, after):
    anywhere = pl.BlockSpec(memory_space=pl.ANY)
    return pl.pallas_call(
        tie_kernel,
        out_shape=jax.ShapeDtypeStruct(array.shape, array.dtype),
        in_specs=[anywhere, anywhere],
        out_specs=anywhere,
        input_output_aliases={0: 0},
    )(array, after)


def group_attention(span, residue, peers, place, projected):
    if span == 1:
        return own_attention(projected)
    period = 2 if span == 2 else SPAN

    def send(array, *hops):
        pairs = []
        for position, target in hops:
            lowest, by = (residue + position) % period, target - position
            pairs += [(s, s + by) for s in range(lowest, peers, period) if s + by < peers]
        return lax.ppermute(array, "seq", pairs)

    def swap(array, position):
        lowest = (residue + position) % period
        pairs = [(s, s + 1) for s in range(lowest, peers, period) if s + 1 < peers]
        return lax.ppermute(array, "seq", pairs + [(b, a) for a, b in pairs])

    chips = {}
    for position in range(span):
        chips.setdefault((residue + position) // 2, []).append(position)
    chips = list(chips.values())
    inner = [tuple(chip) for chip in chips if len(chip) == 2]

    def exchange(mine, after):
        if len(chips) == 1:
            return [(send(mine, *inner), [1])]
        if span == 2:
            return [(send(mine, (0, 1)), [1])]
        if len(chips) == 3:
            came = send(mine, (0, 2), (1, 3))
            found = [(send(mine, (2, 3)), [3]), (send(mine, (0, 3), (1, 2)), [2, 3])]
            came = tie(came, after)
            return [(came, [2, 3]), (swap(came, 1), [1]), *found]
        if span == 4:
            found = [(send(mine, *inner), [1, 3])]
            came = tie(send(mine, (0, 2), (1, 3)), after)
            return [(came, [2, 3]), (swap(came, 2), [2, 3]), *found]
        if len(chips[0]) == 2:
            return [(send(mine, (0, 2)), [2]), (send(mine, (1, 2)), [2]), (send(mine, *inner), [1])]
        found = [(send(mine, *inner), [2])]
        came = tie(send(mine, (0, 2)), after)
        return [(came, [2]), (swap(came, 1), [1]), *found]

    early, late = CHUNK_PARTS
    totals = own_attention(projected)
    found = exchange(pack_key_values(projected, place, 0, early), totals)
    totals = add_sources(place, projected, totals, found, 0, 0, early - 1, False)
    more = exchange(pack_key_values(projected, place, early, late), totals)
    totals = add_sources(place, projected, totals, found, 0, early - 1, 1, False)
    return add_sources(place, projected, totals, more, early, 0, late, True)


def finish_kernel(place_ref, total_ref, u_ref, history_ref, gain_ref, weight_ref, out_ref, last_ref):
    step = pl.program_id(0)
    tile = total_ref.shape[0]
    row_count = tile * pl.num_programs(0)
    span, position, tail = place_ref[0], place_ref[2], place_ref[3]
    valid = jnp.where(position == span - 1, tail, row_count)
    row_ids = step * tile + lax.broadcasted_iota(jnp.int32, (tile, 1), 0)
    attention = jnp.where(row_ids < valid, total_ref[...], 0.0)
    row_mean = jnp.mean(attention, axis=1, keepdims=True)
    centered = attention - row_mean
    row_var = jnp.mean(centered * centered, axis=1, keepdims=True)
    normed = centered * lax.rsqrt(row_var + 1e-06) * gain_ref[...]
    gated = (normed * u_ref[...].astype(jnp.float32)).astype(jnp.bfloat16)
    out = jnp.dot(gated, weight_ref[...], preferred_element_type=jnp.float32)
    out = (out + history_ref[...].astype(jnp.float32)).astype(jnp.bfloat16)
    out_ref[...] = out
    final = jnp.sum(jnp.where(row_ids == valid - 1, out.astype(jnp.float32), 0.0), axis=0, keepdims=True)

    @pl.when(step == 0)
    def _():
        last_ref[...] = final

    @pl.when(step > 0)
    def _():
        last_ref[...] += final


def finish(place, totals, projected, history_in, norm_gain, out_proj):
    row_count, model_width = history_in.shape
    tile = row_tile(row_count)
    rows = pl.BlockSpec((tile, model_width), lambda step, place: (step, 0))
    whole = pl.BlockSpec((1, model_width), lambda step, place: (0, 0))
    return pl.pallas_call(
        finish_kernel,
        out_shape=(
            jax.ShapeDtypeStruct(history_in.shape, history_in.dtype),
            jax.ShapeDtypeStruct((1, model_width), jnp.float32),
        ),
        grid_spec=pltpu.PrefetchScalarGridSpec(
            num_scalar_prefetch=1,
            grid=(row_count // tile,),
            in_specs=[
                rows,
                rows,
                rows,
                whole,
                pl.BlockSpec(out_proj.shape, lambda step, place: (0, 0)),
            ],
            out_specs=(rows, whole),
        ),
        compiler_params=pltpu.CompilerParams(vmem_limit_bytes=VMEM_LIMIT),
        cost_estimate=pl.CostEstimate(
            flops=2 * row_count * model_width * model_width,
            bytes_accessed=10 * row_count * model_width + 2 * model_width * model_width,
            transcendentals=row_count,
        ),
    )(place, totals, projected, history_in, norm_gain.reshape(1, -1), out_proj)


def score_kernel(last_ref, rows_ref, user_ref, cand_ref, down_ref, up_ref, bias_ref, weight_ref, out_ref):
    peers, model_width = rows_ref.shape
    cand_count = cand_ref.shape[0]
    cand_user = user_ref[...]

    def visit(user, found):
        return jnp.where(cand_user == user, last_ref[user], found)

    cand_dev = lax.fori_loop(0, last_ref.shape[0], visit, jnp.zeros_like(cand_user))
    device_ids = lax.broadcasted_iota(jnp.int32, (peers, cand_count), 0)
    selector = jnp.where(device_ids == cand_dev, 1.0, 0.0).astype(jnp.bfloat16)
    user_part = lax.dot_general(
        selector,
        rows_ref[...].astype(jnp.bfloat16),
        (((0,), (0,)), ((), ())),
        preferred_element_type=jnp.float32,
    ).astype(jnp.bfloat16)
    cand_part = cand_ref[...]
    low_rank = jnp.dot(user_part, down_ref[:model_width, :], preferred_element_type=jnp.float32)
    low_rank += jnp.dot(cand_part, down_ref[model_width:, :], preferred_element_type=jnp.float32)
    low_rank = low_rank.astype(jnp.bfloat16)
    score = jnp.zeros((cand_count, 1), jnp.float32)
    for part, low in ((user_part, 0), (cand_part, model_width)):
        cut = slice(low, low + model_width)
        up_part = jnp.dot(low_rank, up_ref[:, cut], preferred_element_type=jnp.float32)
        value = part.astype(jnp.float32)
        crossed = value * (up_part + bias_ref[:, cut]) + value
        score += jnp.sum(crossed * weight_ref[:, cut], axis=1, keepdims=True)
    row_ids = lax.broadcasted_iota(jnp.int32, (cand_count, cand_count), 0)
    column_ids = lax.broadcasted_iota(jnp.int32, (cand_count, cand_count), 1)
    out_ref[...] = jnp.sum(jnp.where(row_ids == column_ids, score, 0.0), axis=0, keepdims=True)


def score(last_dev, user_rows, cand_user, cand_emb, cross_down, cross_up, cross_bias, score_weight):
    vmem = pl.BlockSpec(memory_space=pltpu.VMEM)
    cand_count = cand_emb.shape[0]
    scores = pl.pallas_call(
        score_kernel,
        out_shape=jax.ShapeDtypeStruct((1, cand_count), jnp.float32),
        in_specs=[pl.BlockSpec(memory_space=pltpu.SMEM)] + [vmem] * 7,
        out_specs=vmem,
        compiler_params=pltpu.CompilerParams(vmem_limit_bytes=VMEM_LIMIT),
    )(
        last_dev,
        user_rows,
        cand_user.reshape(1, -1),
        cand_emb,
        cross_down,
        cross_up,
        cross_bias.reshape(1, -1),
        score_weight.reshape(1, -1),
    )
    return scores.reshape(-1)


def body(
    projected,
    history_in,
    norm_gain,
    out_proj,
    user_spans,
    user_tails,
    cand_emb,
    cand_user,
    cross_down,
    cross_up,
    cross_bias,
    score_weight,
):
    peers = lax.axis_size("seq")
    place, last_dev = find_place(lax.axis_index("seq"), user_spans, user_tails)
    branches = [functools.partial(group_attention, 1, 0, peers)]
    for span in range(2, SPAN + 1):
        for residue in range(2 if span == 2 else SPAN):
            branches.append(functools.partial(group_attention, span, residue, peers))
    totals = lax.switch(place[4], branches, place, projected)
    history_out, final_row = finish(place, totals, projected, history_in, norm_gain, out_proj)
    user_rows = lax.all_gather(final_row, "seq", axis=0, tiled=True)
    scores = score(
        last_dev, user_rows, cand_user, cand_emb, cross_down, cross_up, cross_bias, score_weight
    )
    return (history_out, scores)


def solution(mesh):
    in_specs = (
        P(("rep", "seq"), None),
        P(("rep", "seq"), None),
        P(),
        P(),
        P("rep"),
        P("rep"),
        P(("rep", "seq"), None),
        P(("rep", "seq")),
        P(),
        P(),
        P(),
        P(),
    )
    out_specs = (P(("rep", "seq"), None), P(("rep", "seq")))
    return jax.shard_map(body, mesh=mesh, in_specs=in_specs, out_specs=out_specs, check_vma=False)
```

```python
import functools

import jax
import jax.numpy as jnp
from jax import lax
from jax.experimental import pallas as pl
from jax.experimental.pallas import tpu as pltpu
from jax.sharding import PartitionSpec as P

HEADS = 8
SPAN = 4
CHUNK_PARTS = (5, 3)
COST_SCALE = 5
VMEM_LIMIT = 63 * 1024 * 1024


def silu_weights(logits, score_scale):
    half = logits * (0.5 * score_scale)
    return half + half * jnp.tanh(half)


def row_tile(row_count):
    return 256 if row_count % 256 == 0 else row_count


def dot_nt(left, right):
    return lax.dot_general(left, right, (((1,), (1,)), ((), ())), preferred_element_type=jnp.float32)


def place_kernel(me_ref, spans_ref, tails_ref, place_ref, last_ref):
    users = spans_ref.shape[0]
    me = me_ref[0]

    def visit(user, state):
        begin, span, start, tail = state
        end = begin + spans_ref[user]
        mine = (begin <= me) & (me < end)
        last_ref[user] = end - 1
        return (
            end,
            jnp.where(mine, spans_ref[user], span),
            jnp.where(mine, begin, start),
            jnp.where(mine, tails_ref[user], tail),
        )

    zero = jnp.int32(0)
    _, span, start, tail = lax.fori_loop(0, users, visit, (zero, zero + 1, zero, zero))
    place_ref[0] = span
    place_ref[1] = start
    place_ref[2] = me - start
    place_ref[3] = tail
    later = 3 + (span - 3) * SPAN + lax.rem(start, SPAN)
    place_ref[4] = jnp.where(span == 1, 0, jnp.where(span == 2, 1 + lax.rem(start, 2), later))


def find_place(me, user_spans, user_tails):
    smem = pl.BlockSpec(memory_space=pltpu.SMEM)
    return pl.pallas_call(
        place_kernel,
        out_shape=(
            jax.ShapeDtypeStruct((8,), jnp.int32),
            jax.ShapeDtypeStruct(user_spans.shape, jnp.int32),
        ),
        in_specs=[smem] * 3,
        out_specs=(smem, smem),
    )(me.reshape(1), user_spans, user_tails)


def own_kernel(score_scale, q_ref, k_ref, v_ref, out_ref):
    row_count = q_ref.shape[0]
    tile = row_tile(row_count)
    for first in range(0, row_count, tile):
        last = first + tile
        weights = silu_weights(dot_nt(q_ref[first:last, :], k_ref[:last, :]), score_scale)
        row_ids = first + lax.broadcasted_iota(jnp.int32, weights.shape, 0)
        key_ids = lax.broadcasted_iota(jnp.int32, weights.shape, 1)
        weights = jnp.where(key_ids <= row_ids, weights, 0.0).astype(jnp.bfloat16)
        out_ref[first:last, :] = jnp.dot(
            weights, v_ref[:last, :], preferred_element_type=jnp.float32
        )


def own_attention(projected):
    row_count, width = projected.shape
    model_width = width // 4
    head_size = model_width // HEADS

    def columns(part):
        return pl.BlockSpec((row_count, head_size), lambda head: (0, part * HEADS + head))

    return pl.pallas_call(
        functools.partial(own_kernel, head_size ** (-0.5)),
        out_shape=jax.ShapeDtypeStruct((row_count, model_width), jnp.float32),
        grid=(HEADS,),
        in_specs=[columns(1), columns(2), columns(3)],
        out_specs=pl.BlockSpec((row_count, head_size), lambda head: (0, head)),
        compiler_params=pltpu.CompilerParams(vmem_limit_bytes=VMEM_LIMIT),
        cost_estimate=pl.CostEstimate(
            flops=COST_SCALE * 3 * row_count * row_count * model_width,
            bytes_accessed=10 * row_count * model_width,
            transcendentals=row_count * row_count * HEADS,
        ),
    )(projected, projected, projected)


def add_kernel(score_scale, holders, skipped, unrolled, place_ref, q_ref, *refs):
    source_refs, (total_ref, out_ref, slots, arrived) = refs[: len(holders)], refs[-4:]
    head, position = pl.program_id(0), place_ref[2]
    row_count, head_size = q_ref.shape
    tile = row_tile(row_count)
    counts = {}
    for source_ref, positions in zip(source_refs, holders):
        for place in positions:
            slot = counts.get(place, 0)
            counts[place] = slot + 1

            @pl.when((head == 0) & (position == place))
            def _():
                pltpu.make_async_copy(source_ref, slots.at[slot], arrived.at[slot]).start()

    out_ref[...] = total_ref[...]
    count = sum(jnp.where(position == place, number, 0) for place, number in counts.items())
    low = pl.multiple_of((skipped + head) * head_size, head_size)
    key_columns = pl.ds(low, head_size)
    value_columns = pl.ds(pl.multiple_of(slots.shape[2] // 2 + low, head_size), head_size)

    @pl.loop(0, count)
    def _(slot):
        @pl.when(head == 0)
        def _():
            pltpu.make_async_copy(source_refs[0], slots.at[slot], arrived.at[slot]).wait()

        def add_rows(step):
            rows = pl.ds(pl.multiple_of(step * tile, tile), tile)
            logits = dot_nt(q_ref[rows, :], slots[slot, :, key_columns])
            weights = silu_weights(logits, score_scale).astype(jnp.bfloat16)
            out_ref[rows, :] += jnp.dot(
                weights, slots[slot, :, value_columns], preferred_element_type=jnp.float32
            )

        if unrolled:
            for step in range(row_count // tile):
                add_rows(step)
        else:
            pl.loop(0, row_count // tile)(add_rows)


def add_sources(place, projected, totals, sources, first_head, skipped, heads, unrolled):
    row_count, width = projected.shape
    model_width = width // 4
    head_size = model_width // HEADS
    arrays = [array for array, _ in sources]
    holders = [positions for _, positions in sources]
    everyone = [position for positions in holders for position in positions]
    most = max(everyone.count(position) for position in everyone)
    first_head += skipped
    total_spec = pl.BlockSpec((row_count, head_size), lambda head, place: (0, first_head + head))
    return pl.pallas_call(
        functools.partial(add_kernel, head_size ** (-0.5), holders, skipped, unrolled),
        out_shape=jax.ShapeDtypeStruct(totals.shape, totals.dtype),
        grid_spec=pltpu.PrefetchScalarGridSpec(
            num_scalar_prefetch=1,
            grid=(heads,),
            in_specs=[
                pl.BlockSpec((row_count, head_size), lambda head, place: (0, HEADS + first_head + head)),
                *[pl.BlockSpec(memory_space=pl.ANY)] * len(arrays),
                total_spec,
            ],
            out_specs=total_spec,
            scratch_shapes=[
                pltpu.VMEM((most, *arrays[0].shape), projected.dtype),
                pltpu.SemaphoreType.DMA((most,)),
            ],
        ),
        input_output_aliases={2 + len(arrays): 0},
        compiler_params=pltpu.CompilerParams(vmem_limit_bytes=VMEM_LIMIT),
        cost_estimate=pl.CostEstimate(
            flops=COST_SCALE * 4 * row_count * row_count * heads * head_size * most,
            bytes_accessed=(6 + 4 * most) * row_count * heads * head_size,
            transcendentals=row_count * row_count * heads * most,
        ),
    )(place, projected, *arrays, totals)


def pack_kernel(projected_ref, *refs):
    packed_refs, copied = refs[:-1], refs[-1]
    model_width = projected_ref.shape[1] // 4
    low, copies = 0, []
    for packed_ref in packed_refs:
        width = packed_ref.shape[1] // 2
        for part in range(2):
            source = projected_ref.at[:, pl.ds((2 + part) * model_width + low, width)]
            target = packed_ref.at[:, pl.ds(part * width, width)]
            copies.append(pltpu.make_async_copy(source, target, copied.at[len(copies)]))
            copies[-1].start()
        low += width
    for copy in copies:
        copy.wait()


def pack_key_values(projected, parts):
    row_count, width = projected.shape
    anywhere = pl.BlockSpec(memory_space=pl.ANY)
    return pl.pallas_call(
        pack_kernel,
        out_shape=[
            jax.ShapeDtypeStruct((row_count, heads * width // (2 * HEADS)), projected.dtype)
            for heads in parts
        ],
        in_specs=[anywhere],
        out_specs=[anywhere] * len(parts),
        scratch_shapes=[pltpu.SemaphoreType.DMA((2 * len(parts),))],
        compiler_params=pltpu.CompilerParams(vmem_limit_bytes=VMEM_LIMIT),
        cost_estimate=pl.CostEstimate(
            flops=0, bytes_accessed=2 * row_count * width, transcendentals=0
        ),
    )(projected)


def tie_kernel(array_ref, after_ref, out_ref):
    pass


def tie(array, after):
    anywhere = pl.BlockSpec(memory_space=pl.ANY)
    return pl.pallas_call(
        tie_kernel,
        out_shape=jax.ShapeDtypeStruct(array.shape, array.dtype),
        in_specs=[anywhere, anywhere],
        out_specs=anywhere,
        input_output_aliases={0: 0},
    )(array, after)


def group_attention(span, residue, peers, place, projected):
    if span == 1:
        return own_attention(projected)
    period = 2 if span == 2 else SPAN

    def send(array, *hops):
        pairs = []
        for position, target in hops:
            lowest, by = (residue + position) % period, target - position
            pairs += [(s, s + by) for s in range(lowest, peers, period) if s + by < peers]
        return lax.ppermute(array, "seq", pairs)

    def swap(array, position):
        lowest = (residue + position) % period
        pairs = [(s, s + 1) for s in range(lowest, peers, period) if s + 1 < peers]
        return lax.ppermute(array, "seq", pairs + [(b, a) for a, b in pairs])

    chips = {}
    for position in range(span):
        chips.setdefault((residue + position) // 2, []).append(position)
    chips = list(chips.values())
    inner = [tuple(chip) for chip in chips if len(chip) == 2]

    def exchange(mine, after):
        if span == 2:
            return [(send(mine, (0, 1)), [1])]
        if span == 3 and len(chips[0]) == 2:
            return [(send(mine, (0, 2)), [2]), (send(mine, (1, 2)), [2])]
        if span == 3:
            came = tie(send(mine, (0, 2)), after)
            return [(came, [2]), (swap(came, 1), [1])]
        came = send(mine, (0, 2), (1, 3))
        if len(chips) == 2:
            came = tie(came, after)
            return [(came, [2, 3]), (swap(came, 2), [2, 3])]
        found = [(send(mine, (2, 3)), [3])]
        came = tie(came, after)
        return [(came, [2, 3]), (swap(came, 1), [1]), *found]

    early, late = CHUNK_PARTS
    mine, rest = pack_key_values(projected, CHUNK_PARTS)
    totals = own_attention(projected)
    if span > 2:
        hops = inner if len(chips) == 2 else [(0, 3), (1, 2)]
        whole = send(pack_key_values(projected, (HEADS,))[0], *hops)
        sources = [(whole, [target for _, target in hops])]
        totals = add_sources(place, projected, totals, sources, 0, 0, HEADS, False)
    found = exchange(mine, totals)
    totals = add_sources(place, projected, totals, found, 0, 0, early - 1, False)
    more = exchange(rest, totals)
    totals = add_sources(place, projected, totals, found, 0, early - 1, 1, False)
    return add_sources(place, projected, totals, more, early, 0, late, True)


def finish_kernel(place_ref, total_ref, u_ref, history_ref, gain_ref, weight_ref, out_ref, last_ref):
    step = pl.program_id(0)
    tile = total_ref.shape[0]
    row_count = tile * pl.num_programs(0)
    span, position, tail = place_ref[0], place_ref[2], place_ref[3]
    valid = jnp.where(position == span - 1, tail, row_count)
    row_ids = step * tile + lax.broadcasted_iota(jnp.int32, (tile, 1), 0)
    attention = jnp.where(row_ids < valid, total_ref[...], 0.0)
    row_mean = jnp.mean(attention, axis=1, keepdims=True)
    centered = attention - row_mean
    row_var = jnp.mean(centered * centered, axis=1, keepdims=True)
    normed = centered * lax.rsqrt(row_var + 1e-06) * gain_ref[...]
    gated = (normed * u_ref[...].astype(jnp.float32)).astype(jnp.bfloat16)
    out = jnp.dot(gated, weight_ref[...], preferred_element_type=jnp.float32)
    out = (out + history_ref[...].astype(jnp.float32)).astype(jnp.bfloat16)
    out_ref[...] = out
    final = jnp.sum(jnp.where(row_ids == valid - 1, out.astype(jnp.float32), 0.0), axis=0, keepdims=True)

    @pl.when(step == 0)
    def _():
        last_ref[...] = final

    @pl.when(step > 0)
    def _():
        last_ref[...] += final


def finish(place, totals, projected, history_in, norm_gain, out_proj):
    row_count, model_width = history_in.shape
    tile = row_tile(row_count)
    rows = pl.BlockSpec((tile, model_width), lambda step, place: (step, 0))
    whole = pl.BlockSpec((1, model_width), lambda step, place: (0, 0))
    return pl.pallas_call(
        finish_kernel,
        out_shape=(
            jax.ShapeDtypeStruct(history_in.shape, history_in.dtype),
            jax.ShapeDtypeStruct((1, model_width), jnp.float32),
        ),
        grid_spec=pltpu.PrefetchScalarGridSpec(
            num_scalar_prefetch=1,
            grid=(row_count // tile,),
            in_specs=[
                rows,
                rows,
                rows,
                whole,
                pl.BlockSpec(out_proj.shape, lambda step, place: (0, 0)),
            ],
            out_specs=(rows, whole),
        ),
        compiler_params=pltpu.CompilerParams(vmem_limit_bytes=VMEM_LIMIT),
        cost_estimate=pl.CostEstimate(
            flops=2 * row_count * model_width * model_width,
            bytes_accessed=10 * row_count * model_width + 2 * model_width * model_width,
            transcendentals=row_count,
        ),
    )(place, totals, projected, history_in, norm_gain.reshape(1, -1), out_proj)


def score_kernel(last_ref, rows_ref, user_ref, cand_ref, down_ref, up_ref, bias_ref, weight_ref, out_ref):
    peers, model_width = rows_ref.shape
    cand_count = cand_ref.shape[0]
    cand_user = user_ref[...]

    def visit(user, found):
        return jnp.where(cand_user == user, last_ref[user], found)

    cand_dev = lax.fori_loop(0, last_ref.shape[0], visit, jnp.zeros_like(cand_user))
    device_ids = lax.broadcasted_iota(jnp.int32, (peers, cand_count), 0)
    selector = jnp.where(device_ids == cand_dev, 1.0, 0.0).astype(jnp.bfloat16)
    user_part = lax.dot_general(
        selector,
        rows_ref[...].astype(jnp.bfloat16),
        (((0,), (0,)), ((), ())),
        preferred_element_type=jnp.float32,
    ).astype(jnp.bfloat16)
    cand_part = cand_ref[...]
    low_rank = jnp.dot(user_part, down_ref[:model_width, :], preferred_element_type=jnp.float32)
    low_rank += jnp.dot(cand_part, down_ref[model_width:, :], preferred_element_type=jnp.float32)
    low_rank = low_rank.astype(jnp.bfloat16)
    score = jnp.zeros((cand_count, 1), jnp.float32)
    for part, low in ((user_part, 0), (cand_part, model_width)):
        cut = slice(low, low + model_width)
        up_part = jnp.dot(low_rank, up_ref[:, cut], preferred_element_type=jnp.float32)
        value = part.astype(jnp.float32)
        crossed = value * (up_part + bias_ref[:, cut]) + value
        score += jnp.sum(crossed * weight_ref[:, cut], axis=1, keepdims=True)
    row_ids = lax.broadcasted_iota(jnp.int32, (cand_count, cand_count), 0)
    column_ids = lax.broadcasted_iota(jnp.int32, (cand_count, cand_count), 1)
    out_ref[...] = jnp.sum(jnp.where(row_ids == column_ids, score, 0.0), axis=0, keepdims=True)


def score(last_dev, user_rows, cand_user, cand_emb, cross_down, cross_up, cross_bias, score_weight):
    vmem = pl.BlockSpec(memory_space=pltpu.VMEM)
    cand_count = cand_emb.shape[0]
    scores = pl.pallas_call(
        score_kernel,
        out_shape=jax.ShapeDtypeStruct((1, cand_count), jnp.float32),
        in_specs=[pl.BlockSpec(memory_space=pltpu.SMEM)] + [vmem] * 7,
        out_specs=vmem,
        compiler_params=pltpu.CompilerParams(vmem_limit_bytes=VMEM_LIMIT),
    )(
        last_dev,
        user_rows,
        cand_user.reshape(1, -1),
        cand_emb,
        cross_down,
        cross_up,
        cross_bias.reshape(1, -1),
        score_weight.reshape(1, -1),
    )
    return scores.reshape(-1)


def body(
    projected,
    history_in,
    norm_gain,
    out_proj,
    user_spans,
    user_tails,
    cand_emb,
    cand_user,
    cross_down,
    cross_up,
    cross_bias,
    score_weight,
):
    peers = lax.axis_size("seq")
    place, last_dev = find_place(lax.axis_index("seq"), user_spans, user_tails)
    branches = [functools.partial(group_attention, 1, 0, peers)]
    for span in range(2, SPAN + 1):
        for residue in range(2 if span == 2 else SPAN):
            branches.append(functools.partial(group_attention, span, residue, peers))
    totals = lax.switch(place[4], branches, place, projected)
    history_out, final_row = finish(place, totals, projected, history_in, norm_gain, out_proj)
    user_rows = lax.all_gather(final_row, "seq", axis=0, tiled=True)
    scores = score(
        last_dev, user_rows, cand_user, cand_emb, cross_down, cross_up, cross_bias, score_weight
    )
    return (history_out, scores)


def solution(mesh):
    in_specs = (
        P(("rep", "seq"), None),
        P(("rep", "seq"), None),
        P(),
        P(),
        P("rep"),
        P("rep"),
        P(("rep", "seq"), None),
        P(("rep", "seq")),
        P(),
        P(),
        P(),
        P(),
    )
    out_specs = (P(("rep", "seq"), None), P(("rep", "seq")))
    return jax.shard_map(body, mesh=mesh, in_specs=in_specs, out_specs=out_specs, check_vma=False)
```

```python
import functools

import jax
import jax.numpy as jnp
from jax import lax
from jax.experimental import pallas as pl
from jax.experimental.pallas import tpu as pltpu
from jax.sharding import PartitionSpec as P

HEADS = 8
SPAN = 4
CHUNK_PARTS = (5, 3)
COST_SCALE = 5
VMEM_LIMIT = 63 * 1024 * 1024


def silu_weights(logits, score_scale):
    half = logits * (0.5 * score_scale)
    return half + half * jnp.tanh(half)


def row_tile(row_count):
    return 256 if row_count % 256 == 0 else row_count


def dot_nt(left, right):
    return lax.dot_general(left, right, (((1,), (1,)), ((), ())), preferred_element_type=jnp.float32)


def place_kernel(me_ref, spans_ref, tails_ref, place_ref, last_ref):
    users = spans_ref.shape[0]
    me = me_ref[0]

    def visit(user, state):
        begin, span, start, tail = state
        end = begin + spans_ref[user]
        mine = (begin <= me) & (me < end)
        last_ref[user] = end - 1
        return (
            end,
            jnp.where(mine, spans_ref[user], span),
            jnp.where(mine, begin, start),
            jnp.where(mine, tails_ref[user], tail),
        )

    zero = jnp.int32(0)
    _, span, start, tail = lax.fori_loop(0, users, visit, (zero, zero + 1, zero, zero))
    place_ref[0] = span
    place_ref[1] = start
    place_ref[2] = me - start
    place_ref[3] = tail
    later = 3 + (span - 3) * SPAN + lax.rem(start, SPAN)
    place_ref[4] = jnp.where(span == 1, 0, jnp.where(span == 2, 1 + lax.rem(start, 2), later))


def find_place(me, user_spans, user_tails):
    smem = pl.BlockSpec(memory_space=pltpu.SMEM)
    return pl.pallas_call(
        place_kernel,
        out_shape=(
            jax.ShapeDtypeStruct((8,), jnp.int32),
            jax.ShapeDtypeStruct(user_spans.shape, jnp.int32),
        ),
        in_specs=[smem] * 3,
        out_specs=(smem, smem),
    )(me.reshape(1), user_spans, user_tails)


def own_kernel(score_scale, q_ref, k_ref, v_ref, out_ref):
    row_count = q_ref.shape[0]
    tile = row_tile(row_count)
    for first in range(0, row_count, tile):
        last = first + tile
        weights = silu_weights(dot_nt(q_ref[first:last, :], k_ref[:last, :]), score_scale)
        row_ids = first + lax.broadcasted_iota(jnp.int32, weights.shape, 0)
        key_ids = lax.broadcasted_iota(jnp.int32, weights.shape, 1)
        weights = jnp.where(key_ids <= row_ids, weights, 0.0).astype(jnp.bfloat16)
        out_ref[first:last, :] = jnp.dot(
            weights, v_ref[:last, :], preferred_element_type=jnp.float32
        )


def own_attention(projected):
    row_count, width = projected.shape
    model_width = width // 4
    head_size = model_width // HEADS

    def columns(part):
        return pl.BlockSpec((row_count, head_size), lambda head: (0, part * HEADS + head))

    return pl.pallas_call(
        functools.partial(own_kernel, head_size ** (-0.5)),
        out_shape=jax.ShapeDtypeStruct((row_count, model_width), jnp.float32),
        grid=(HEADS,),
        in_specs=[columns(1), columns(2), columns(3)],
        out_specs=pl.BlockSpec((row_count, head_size), lambda head: (0, head)),
        compiler_params=pltpu.CompilerParams(vmem_limit_bytes=VMEM_LIMIT),
        cost_estimate=pl.CostEstimate(
            flops=COST_SCALE * 3 * row_count * row_count * model_width,
            bytes_accessed=10 * row_count * model_width,
            transcendentals=row_count * row_count * HEADS,
        ),
    )(projected, projected, projected)


def add_kernel(score_scale, holders, skipped, unrolled, place_ref, q_ref, *refs):
    source_refs, (total_ref, out_ref, slots, arrived) = refs[: len(holders)], refs[-4:]
    head, position = pl.program_id(0), place_ref[2]
    row_count, head_size = q_ref.shape
    tile = row_tile(row_count)
    counts = {}
    for source_ref, positions in zip(source_refs, holders):
        for place in positions:
            slot = counts.get(place, 0)
            counts[place] = slot + 1

            @pl.when((head == 0) & (position == place))
            def _():
                pltpu.make_async_copy(source_ref, slots.at[slot], arrived.at[slot]).start()

    out_ref[...] = total_ref[...]
    count = sum(jnp.where(position == place, number, 0) for place, number in counts.items())
    low = pl.multiple_of((skipped + head) * head_size, head_size)
    key_columns = pl.ds(low, head_size)
    value_columns = pl.ds(pl.multiple_of(slots.shape[2] // 2 + low, head_size), head_size)

    @pl.loop(0, count)
    def _(slot):
        @pl.when(head == 0)
        def _():
            pltpu.make_async_copy(source_refs[0], slots.at[slot], arrived.at[slot]).wait()

        def add_rows(step):
            rows = pl.ds(pl.multiple_of(step * tile, tile), tile)
            logits = dot_nt(q_ref[rows, :], slots[slot, :, key_columns])
            weights = silu_weights(logits, score_scale).astype(jnp.bfloat16)
            out_ref[rows, :] += jnp.dot(
                weights, slots[slot, :, value_columns], preferred_element_type=jnp.float32
            )

        if unrolled:
            for step in range(row_count // tile):
                add_rows(step)
        else:
            pl.loop(0, row_count // tile)(add_rows)


def add_sources(place, projected, totals, sources, first_head, skipped, heads, unrolled):
    row_count, width = projected.shape
    model_width = width // 4
    head_size = model_width // HEADS
    arrays = [array for array, _ in sources]
    holders = [positions for _, positions in sources]
    everyone = [position for positions in holders for position in positions]
    most = max(everyone.count(position) for position in everyone)
    first_head += skipped
    total_spec = pl.BlockSpec((row_count, head_size), lambda head, place: (0, first_head + head))
    return pl.pallas_call(
        functools.partial(add_kernel, head_size ** (-0.5), holders, skipped, unrolled),
        out_shape=jax.ShapeDtypeStruct(totals.shape, totals.dtype),
        grid_spec=pltpu.PrefetchScalarGridSpec(
            num_scalar_prefetch=1,
            grid=(heads,),
            in_specs=[
                pl.BlockSpec((row_count, head_size), lambda head, place: (0, HEADS + first_head + head)),
                *[pl.BlockSpec(memory_space=pl.ANY)] * len(arrays),
                total_spec,
            ],
            out_specs=total_spec,
            scratch_shapes=[
                pltpu.VMEM((most, *arrays[0].shape), projected.dtype),
                pltpu.SemaphoreType.DMA((most,)),
            ],
        ),
        input_output_aliases={2 + len(arrays): 0},
        compiler_params=pltpu.CompilerParams(vmem_limit_bytes=VMEM_LIMIT),
        cost_estimate=pl.CostEstimate(
            flops=COST_SCALE * 4 * row_count * row_count * heads * head_size * most,
            bytes_accessed=(6 + 4 * most) * row_count * heads * head_size,
            transcendentals=row_count * row_count * heads * most,
        ),
    )(place, projected, *arrays, totals)


def pack_kernel(projected_ref, *refs):
    count = (len(refs) - 2) // 2
    packed_refs, held_refs, (loaded, stored) = refs[:count], refs[count:-2], refs[-2:]
    model_width = projected_ref.shape[1] // 4
    low, loads, stores = 0, [], []
    for packed_ref, held_ref in zip(packed_refs, held_refs):
        width = packed_ref.shape[1] // 2
        for part in range(2):
            source = projected_ref.at[:, pl.ds((2 + part) * model_width + low, width)]
            held = held_ref.at[:, pl.ds(part * width, width)]
            target = packed_ref.at[:, pl.ds(part * width, width)]
            loads.append(pltpu.make_async_copy(source, held, loaded.at[len(loads)]))
            stores.append(pltpu.make_async_copy(held, target, stored.at[len(stores)]))
        low += width
    for load in loads:
        load.start()
    for load, store in zip(loads, stores):
        load.wait()
        store.start()
    for store in stores:
        store.wait()


def pack_key_values(projected, parts):
    row_count, width = projected.shape
    anywhere = pl.BlockSpec(memory_space=pl.ANY)
    shapes = [(row_count, heads * width // (2 * HEADS)) for heads in parts]
    return pl.pallas_call(
        pack_kernel,
        out_shape=[jax.ShapeDtypeStruct(shape, projected.dtype) for shape in shapes],
        in_specs=[anywhere],
        out_specs=[anywhere] * len(parts),
        scratch_shapes=[
            *[pltpu.VMEM(shape, projected.dtype) for shape in shapes],
            *[pltpu.SemaphoreType.DMA((2 * len(parts),))] * 2,
        ],
        compiler_params=pltpu.CompilerParams(vmem_limit_bytes=VMEM_LIMIT),
        cost_estimate=pl.CostEstimate(
            flops=0, bytes_accessed=2 * row_count * width, transcendentals=0
        ),
    )(projected)


def tie_kernel(array_ref, after_ref, out_ref):
    pass


def tie(array, after):
    anywhere = pl.BlockSpec(memory_space=pl.ANY)
    return pl.pallas_call(
        tie_kernel,
        out_shape=jax.ShapeDtypeStruct(array.shape, array.dtype),
        in_specs=[anywhere, anywhere],
        out_specs=anywhere,
        input_output_aliases={0: 0},
    )(array, after)


def group_attention(span, residue, peers, place, projected):
    if span == 1:
        return own_attention(projected)
    period = 2 if span == 2 else SPAN

    def send(array, *hops):
        pairs = []
        for position, target in hops:
            lowest, by = (residue + position) % period, target - position
            pairs += [(s, s + by) for s in range(lowest, peers, period) if s + by < peers]
        return lax.ppermute(array, "seq", pairs)

    def swap(array, position):
        lowest = (residue + position) % period
        pairs = [(s, s + 1) for s in range(lowest, peers, period) if s + 1 < peers]
        return lax.ppermute(array, "seq", pairs + [(b, a) for a, b in pairs])

    chips = {}
    for position in range(span):
        chips.setdefault((residue + position) // 2, []).append(position)
    chips = list(chips.values())
    inner = [tuple(chip) for chip in chips if len(chip) == 2]

    def exchange(mine, after):
        if span == 2:
            return [(send(mine, (0, 1)), [1])]
        if span == 3 and len(chips[0]) == 2:
            return [(send(mine, (0, 2)), [2]), (send(mine, (1, 2)), [2])]
        if span == 3:
            came = tie(send(mine, (0, 2)), after)
            return [(came, [2]), (swap(came, 1), [1])]
        came = send(mine, (0, 2), (1, 3))
        if len(chips) == 2:
            came = tie(came, after)
            return [(came, [2, 3]), (swap(came, 2), [2, 3])]
        found = [(send(mine, (2, 3)), [3])]
        came = tie(came, after)
        return [(came, [2, 3]), (swap(came, 1), [1]), *found]

    early, late = CHUNK_PARTS
    mine, rest = pack_key_values(projected, CHUNK_PARTS)
    totals = own_attention(projected)
    if span > 2:
        hops = inner if len(chips) == 2 else [(0, 3), (1, 2)]
        whole = send(pack_key_values(projected, (HEADS,))[0], *hops)
        sources = [(whole, [target for _, target in hops])]
        totals = add_sources(place, projected, totals, sources, 0, 0, HEADS, False)
    found = exchange(mine, totals)
    totals = add_sources(place, projected, totals, found, 0, 0, early - 1, False)
    more = exchange(rest, totals)
    totals = add_sources(place, projected, totals, found, 0, early - 1, 1, False)
    return add_sources(place, projected, totals, more, early, 0, late, True)


def finish_kernel(place_ref, total_ref, u_ref, history_ref, gain_ref, weight_ref, out_ref, last_ref):
    step = pl.program_id(0)
    tile = total_ref.shape[0]
    row_count = tile * pl.num_programs(0)
    span, position, tail = place_ref[0], place_ref[2], place_ref[3]
    valid = jnp.where(position == span - 1, tail, row_count)
    row_ids = step * tile + lax.broadcasted_iota(jnp.int32, (tile, 1), 0)
    attention = jnp.where(row_ids < valid, total_ref[...], 0.0)
    row_mean = jnp.mean(attention, axis=1, keepdims=True)
    centered = attention - row_mean
    row_var = jnp.mean(centered * centered, axis=1, keepdims=True)
    normed = centered * lax.rsqrt(row_var + 1e-06) * gain_ref[...]
    gated = (normed * u_ref[...].astype(jnp.float32)).astype(jnp.bfloat16)
    out = jnp.dot(gated, weight_ref[...], preferred_element_type=jnp.float32)
    out = (out + history_ref[...].astype(jnp.float32)).astype(jnp.bfloat16)
    out_ref[...] = out
    final = jnp.sum(jnp.where(row_ids == valid - 1, out.astype(jnp.float32), 0.0), axis=0, keepdims=True)

    @pl.when(step == 0)
    def _():
        last_ref[...] = final

    @pl.when(step > 0)
    def _():
        last_ref[...] += final


def finish(place, totals, projected, history_in, norm_gain, out_proj):
    row_count, model_width = history_in.shape
    tile = row_tile(row_count)
    rows = pl.BlockSpec((tile, model_width), lambda step, place: (step, 0))
    whole = pl.BlockSpec((1, model_width), lambda step, place: (0, 0))
    return pl.pallas_call(
        finish_kernel,
        out_shape=(
            jax.ShapeDtypeStruct(history_in.shape, history_in.dtype),
            jax.ShapeDtypeStruct((1, model_width), jnp.float32),
        ),
        grid_spec=pltpu.PrefetchScalarGridSpec(
            num_scalar_prefetch=1,
            grid=(row_count // tile,),
            in_specs=[
                rows,
                rows,
                rows,
                whole,
                pl.BlockSpec(out_proj.shape, lambda step, place: (0, 0)),
            ],
            out_specs=(rows, whole),
        ),
        compiler_params=pltpu.CompilerParams(vmem_limit_bytes=VMEM_LIMIT),
        cost_estimate=pl.CostEstimate(
            flops=2 * row_count * model_width * model_width,
            bytes_accessed=10 * row_count * model_width + 2 * model_width * model_width,
            transcendentals=row_count,
        ),
    )(place, totals, projected, history_in, norm_gain.reshape(1, -1), out_proj)


def score_kernel(last_ref, rows_ref, user_ref, cand_ref, down_ref, up_ref, bias_ref, weight_ref, out_ref):
    peers, model_width = rows_ref.shape
    cand_count = cand_ref.shape[0]
    cand_user = user_ref[...]

    def visit(user, found):
        return jnp.where(cand_user == user, last_ref[user], found)

    cand_dev = lax.fori_loop(0, last_ref.shape[0], visit, jnp.zeros_like(cand_user))
    device_ids = lax.broadcasted_iota(jnp.int32, (peers, cand_count), 0)
    selector = jnp.where(device_ids == cand_dev, 1.0, 0.0).astype(jnp.bfloat16)
    user_part = lax.dot_general(
        selector,
        rows_ref[...].astype(jnp.bfloat16),
        (((0,), (0,)), ((), ())),
        preferred_element_type=jnp.float32,
    ).astype(jnp.bfloat16)
    cand_part = cand_ref[...]
    low_rank = jnp.dot(user_part, down_ref[:model_width, :], preferred_element_type=jnp.float32)
    low_rank += jnp.dot(cand_part, down_ref[model_width:, :], preferred_element_type=jnp.float32)
    low_rank = low_rank.astype(jnp.bfloat16)
    score = jnp.zeros((cand_count, 1), jnp.float32)
    for part, low in ((user_part, 0), (cand_part, model_width)):
        cut = slice(low, low + model_width)
        up_part = jnp.dot(low_rank, up_ref[:, cut], preferred_element_type=jnp.float32)
        value = part.astype(jnp.float32)
        crossed = value * (up_part + bias_ref[:, cut]) + value
        score += jnp.sum(crossed * weight_ref[:, cut], axis=1, keepdims=True)
    row_ids = lax.broadcasted_iota(jnp.int32, (cand_count, cand_count), 0)
    column_ids = lax.broadcasted_iota(jnp.int32, (cand_count, cand_count), 1)
    out_ref[...] = jnp.sum(jnp.where(row_ids == column_ids, score, 0.0), axis=0, keepdims=True)


def score(last_dev, user_rows, cand_user, cand_emb, cross_down, cross_up, cross_bias, score_weight):
    vmem = pl.BlockSpec(memory_space=pltpu.VMEM)
    cand_count = cand_emb.shape[0]
    scores = pl.pallas_call(
        score_kernel,
        out_shape=jax.ShapeDtypeStruct((1, cand_count), jnp.float32),
        in_specs=[pl.BlockSpec(memory_space=pltpu.SMEM)] + [vmem] * 7,
        out_specs=vmem,
        compiler_params=pltpu.CompilerParams(vmem_limit_bytes=VMEM_LIMIT),
    )(
        last_dev,
        user_rows,
        cand_user.reshape(1, -1),
        cand_emb,
        cross_down,
        cross_up,
        cross_bias.reshape(1, -1),
        score_weight.reshape(1, -1),
    )
    return scores.reshape(-1)


def body(
    projected,
    history_in,
    norm_gain,
    out_proj,
    user_spans,
    user_tails,
    cand_emb,
    cand_user,
    cross_down,
    cross_up,
    cross_bias,
    score_weight,
):
    peers = lax.axis_size("seq")
    place, last_dev = find_place(lax.axis_index("seq"), user_spans, user_tails)
    branches = [functools.partial(group_attention, 1, 0, peers)]
    for span in range(2, SPAN + 1):
        for residue in range(2 if span == 2 else SPAN):
            branches.append(functools.partial(group_attention, span, residue, peers))
    totals = lax.switch(place[4], branches, place, projected)
    history_out, final_row = finish(place, totals, projected, history_in, norm_gain, out_proj)
    user_rows = lax.all_gather(final_row, "seq", axis=0, tiled=True)
    scores = score(
        last_dev, user_rows, cand_user, cand_emb, cross_down, cross_up, cross_bias, score_weight
    )
    return (history_out, scores)


def solution(mesh):
    in_specs = (
        P(("rep", "seq"), None),
        P(("rep", "seq"), None),
        P(),
        P(),
        P("rep"),
        P("rep"),
        P(("rep", "seq"), None),
        P(("rep", "seq")),
        P(),
        P(),
        P(),
        P(),
    )
    out_specs = (P(("rep", "seq"), None), P(("rep", "seq")))
    return jax.shard_map(body, mesh=mesh, in_specs=in_specs, out_specs=out_specs, check_vma=False)
```

```python
import functools

import jax
import jax.numpy as jnp
from jax import lax
from jax.experimental import pallas as pl
from jax.experimental.pallas import tpu as pltpu
from jax.sharding import PartitionSpec as P

HEADS = 8
SPAN = 4
CHUNK_PARTS = (5, 3)
COST_SCALE = 5
VMEM_LIMIT = 63 * 1024 * 1024


def silu_weights(logits, score_scale):
    half = logits * (0.5 * score_scale)
    return half + half * jnp.tanh(half)


def row_tile(row_count):
    return 256 if row_count % 256 == 0 else row_count


def dot_nt(left, right):
    return lax.dot_general(left, right, (((1,), (1,)), ((), ())), preferred_element_type=jnp.float32)


def place_kernel(me_ref, spans_ref, tails_ref, place_ref, last_ref):
    users = spans_ref.shape[0]
    me = me_ref[0]

    def visit(user, state):
        begin, span, start, tail = state
        end = begin + spans_ref[user]
        mine = (begin <= me) & (me < end)
        last_ref[user] = end - 1
        return (
            end,
            jnp.where(mine, spans_ref[user], span),
            jnp.where(mine, begin, start),
            jnp.where(mine, tails_ref[user], tail),
        )

    zero = jnp.int32(0)
    _, span, start, tail = lax.fori_loop(0, users, visit, (zero, zero + 1, zero, zero))
    place_ref[0] = span
    place_ref[1] = start
    place_ref[2] = me - start
    place_ref[3] = tail
    later = 3 + (span - 3) * SPAN + lax.rem(start, SPAN)
    place_ref[4] = jnp.where(span == 1, 0, jnp.where(span == 2, 1 + lax.rem(start, 2), later))


def find_place(me, user_spans, user_tails):
    smem = pl.BlockSpec(memory_space=pltpu.SMEM)
    return pl.pallas_call(
        place_kernel,
        out_shape=(
            jax.ShapeDtypeStruct((8,), jnp.int32),
            jax.ShapeDtypeStruct(user_spans.shape, jnp.int32),
        ),
        in_specs=[smem] * 3,
        out_specs=(smem, smem),
    )(me.reshape(1), user_spans, user_tails)


def own_kernel(score_scale, q_ref, k_ref, v_ref, out_ref):
    row_count = q_ref.shape[0]
    tile = row_tile(row_count)
    for first in range(0, row_count, tile):
        last = first + tile
        weights = silu_weights(dot_nt(q_ref[first:last, :], k_ref[:last, :]), score_scale)
        row_ids = first + lax.broadcasted_iota(jnp.int32, weights.shape, 0)
        key_ids = lax.broadcasted_iota(jnp.int32, weights.shape, 1)
        weights = jnp.where(key_ids <= row_ids, weights, 0.0).astype(jnp.bfloat16)
        out_ref[first:last, :] = jnp.dot(
            weights, v_ref[:last, :], preferred_element_type=jnp.float32
        )


def own_attention(projected):
    row_count, width = projected.shape
    model_width = width // 4
    head_size = model_width // HEADS

    def columns(part):
        return pl.BlockSpec((row_count, head_size), lambda head: (0, part * HEADS + head))

    return pl.pallas_call(
        functools.partial(own_kernel, head_size ** (-0.5)),
        out_shape=jax.ShapeDtypeStruct((row_count, model_width), jnp.float32),
        grid=(HEADS,),
        in_specs=[columns(1), columns(2), columns(3)],
        out_specs=pl.BlockSpec((row_count, head_size), lambda head: (0, head)),
        compiler_params=pltpu.CompilerParams(vmem_limit_bytes=VMEM_LIMIT),
        cost_estimate=pl.CostEstimate(
            flops=COST_SCALE * 3 * row_count * row_count * model_width,
            bytes_accessed=10 * row_count * model_width,
            transcendentals=row_count * row_count * HEADS,
        ),
    )(projected, projected, projected)


def add_kernel(score_scale, holders, skipped, unrolled, place_ref, q_ref, *refs):
    source_refs, (total_ref, out_ref, slots, arrived) = refs[: len(holders)], refs[-4:]
    head, position = pl.program_id(0), place_ref[2]
    row_count, head_size = q_ref.shape
    tile = row_tile(row_count)
    counts = {}
    for source_ref, positions in zip(source_refs, holders):
        for place in positions:
            slot = counts.get(place, 0)
            counts[place] = slot + 1

            @pl.when((head == 0) & (position == place))
            def _():
                pltpu.make_async_copy(source_ref, slots.at[slot], arrived.at[slot]).start()

    out_ref[...] = total_ref[...]
    count = sum(jnp.where(position == place, number, 0) for place, number in counts.items())
    low = pl.multiple_of((skipped + head) * head_size, head_size)
    key_columns = pl.ds(low, head_size)
    value_columns = pl.ds(pl.multiple_of(slots.shape[2] // 2 + low, head_size), head_size)

    @pl.loop(0, count)
    def _(slot):
        @pl.when(head == 0)
        def _():
            pltpu.make_async_copy(source_refs[0], slots.at[slot], arrived.at[slot]).wait()

        def add_rows(step):
            rows = pl.ds(pl.multiple_of(step * tile, tile), tile)
            logits = dot_nt(q_ref[rows, :], slots[slot, :, key_columns])
            weights = silu_weights(logits, score_scale).astype(jnp.bfloat16)
            out_ref[rows, :] += jnp.dot(
                weights, slots[slot, :, value_columns], preferred_element_type=jnp.float32
            )

        if unrolled:
            for step in range(row_count // tile):
                add_rows(step)
        else:
            pl.loop(0, row_count // tile)(add_rows)


def add_sources(place, projected, totals, sources, first_head, skipped, heads, unrolled):
    row_count, width = projected.shape
    model_width = width // 4
    head_size = model_width // HEADS
    arrays = [array for array, _ in sources]
    holders = [positions for _, positions in sources]
    everyone = [position for positions in holders for position in positions]
    most = max(everyone.count(position) for position in everyone)
    first_head += skipped
    total_spec = pl.BlockSpec((row_count, head_size), lambda head, place: (0, first_head + head))
    return pl.pallas_call(
        functools.partial(add_kernel, head_size ** (-0.5), holders, skipped, unrolled),
        out_shape=jax.ShapeDtypeStruct(totals.shape, totals.dtype),
        grid_spec=pltpu.PrefetchScalarGridSpec(
            num_scalar_prefetch=1,
            grid=(heads,),
            in_specs=[
                pl.BlockSpec((row_count, head_size), lambda head, place: (0, HEADS + first_head + head)),
                *[pl.BlockSpec(memory_space=pl.ANY)] * len(arrays),
                total_spec,
            ],
            out_specs=total_spec,
            scratch_shapes=[
                pltpu.VMEM((most, *arrays[0].shape), projected.dtype),
                pltpu.SemaphoreType.DMA((most,)),
            ],
        ),
        input_output_aliases={2 + len(arrays): 0},
        compiler_params=pltpu.CompilerParams(vmem_limit_bytes=VMEM_LIMIT),
        cost_estimate=pl.CostEstimate(
            flops=COST_SCALE * 4 * row_count * row_count * heads * head_size * most,
            bytes_accessed=(6 + 4 * most) * row_count * heads * head_size,
            transcendentals=row_count * row_count * heads * most,
        ),
    )(place, projected, *arrays, totals)


def pack_kernel(projected_ref, *refs):
    count = (len(refs) - 2) // 2
    packed_refs, held_refs, (loaded, stored) = refs[:count], refs[count:-2], refs[-2:]
    model_width = projected_ref.shape[1] // 4
    low, loads, stores = 0, [], []
    for packed_ref, held_ref in zip(packed_refs, held_refs):
        width = packed_ref.shape[1] // 2
        for part in range(2):
            source = projected_ref.at[:, pl.ds((2 + part) * model_width + low, width)]
            held = held_ref.at[:, pl.ds(part * width, width)]
            target = packed_ref.at[:, pl.ds(part * width, width)]
            loads.append(pltpu.make_async_copy(source, held, loaded.at[len(loads)]))
            stores.append(pltpu.make_async_copy(held, target, stored.at[len(stores)]))
        low += width
    for load in loads:
        load.start()
    for load, store in zip(loads, stores):
        load.wait()
        store.start()
    for store in stores:
        store.wait()


def pack_key_values(projected, parts):
    row_count, width = projected.shape
    anywhere = pl.BlockSpec(memory_space=pl.ANY)
    shapes = [(row_count, heads * width // (2 * HEADS)) for heads in parts]
    return pl.pallas_call(
        pack_kernel,
        out_shape=[jax.ShapeDtypeStruct(shape, projected.dtype) for shape in shapes],
        in_specs=[anywhere],
        out_specs=[anywhere] * len(parts),
        scratch_shapes=[
            *[pltpu.VMEM(shape, projected.dtype) for shape in shapes],
            *[pltpu.SemaphoreType.DMA((2 * len(parts),))] * 2,
        ],
        compiler_params=pltpu.CompilerParams(vmem_limit_bytes=VMEM_LIMIT),
        cost_estimate=pl.CostEstimate(
            flops=0, bytes_accessed=2 * row_count * width, transcendentals=0
        ),
    )(projected)


def tie_kernel(array_ref, after_ref, out_ref):
    pass


def tie(array, after):
    anywhere = pl.BlockSpec(memory_space=pl.ANY)
    return pl.pallas_call(
        tie_kernel,
        out_shape=jax.ShapeDtypeStruct(array.shape, array.dtype),
        in_specs=[anywhere, anywhere],
        out_specs=anywhere,
        input_output_aliases={0: 0},
    )(array, after)


def group_attention(span, residue, peers, place, projected):
    if span == 1:
        return own_attention(projected)
    period = 2 if span == 2 else SPAN

    def send(array, *hops):
        pairs = []
        for position, target in hops:
            lowest, by = (residue + position) % period, target - position
            pairs += [(s, s + by) for s in range(lowest, peers, period) if s + by < peers]
        return lax.ppermute(array, "seq", pairs)

    def swap(array, position):
        lowest = (residue + position) % period
        pairs = [(s, s + 1) for s in range(lowest, peers, period) if s + 1 < peers]
        return lax.ppermute(array, "seq", pairs + [(b, a) for a, b in pairs])

    chips = {}
    for position in range(span):
        chips.setdefault((residue + position) // 2, []).append(position)
    chips = list(chips.values())
    inner = [tuple(chip) for chip in chips if len(chip) == 2]

    def exchange(mine, after):
        if span == 2:
            return [(send(mine, (0, 1)), [1])]
        if span == 3 and len(chips[0]) == 2:
            return [(send(mine, (0, 2)), [2]), (send(mine, (1, 2)), [2])]
        if span == 3:
            came = tie(send(mine, (0, 2)), after)
            return [(came, [2]), (swap(came, 1), [1])]
        came = send(mine, (0, 2), (1, 3))
        if len(chips) == 2:
            came = tie(came, after)
            return [(came, [2, 3]), (swap(came, 2), [2, 3])]
        found = [(send(mine, (2, 3)), [3])]
        came = tie(came, after)
        return [(came, [2, 3]), (swap(came, 1), [1]), *found]

    early, late = CHUNK_PARTS
    mine, rest = pack_key_values(projected, CHUNK_PARTS)
    totals = own_attention(projected)
    if span > 2:
        hops = inner if len(chips) == 2 else [(0, 3), (1, 2)]
        whole = send(pack_key_values(projected, (HEADS,))[0], *hops)
        sources = [(whole, [target for _, target in hops])]
        totals = add_sources(place, projected, totals, sources, 0, 0, early, False)
    found = exchange(mine, totals)
    if span > 2:
        totals = add_sources(place, projected, totals, sources, 0, early, late, False)
    totals = add_sources(place, projected, totals, found, 0, 0, early, False)
    more = exchange(rest, totals)
    return add_sources(place, projected, totals, more, early, 0, late, True)


def finish_kernel(place_ref, total_ref, u_ref, history_ref, gain_ref, weight_ref, out_ref, last_ref):
    step = pl.program_id(0)
    tile = total_ref.shape[0]
    row_count = tile * pl.num_programs(0)
    span, position, tail = place_ref[0], place_ref[2], place_ref[3]
    valid = jnp.where(position == span - 1, tail, row_count)
    row_ids = step * tile + lax.broadcasted_iota(jnp.int32, (tile, 1), 0)
    attention = jnp.where(row_ids < valid, total_ref[...], 0.0)
    row_mean = jnp.mean(attention, axis=1, keepdims=True)
    centered = attention - row_mean
    row_var = jnp.mean(centered * centered, axis=1, keepdims=True)
    normed = centered * lax.rsqrt(row_var + 1e-06) * gain_ref[...]
    gated = (normed * u_ref[...].astype(jnp.float32)).astype(jnp.bfloat16)
    out = jnp.dot(gated, weight_ref[...], preferred_element_type=jnp.float32)
    out = (out + history_ref[...].astype(jnp.float32)).astype(jnp.bfloat16)
    out_ref[...] = out

    @pl.when(valid - 1 - step * tile == jnp.clip(valid - 1 - step * tile, 0, tile - 1))
    def _():
        final = jnp.where(row_ids == valid - 1, out.astype(jnp.float32), 0.0)
        last_ref[...] = jnp.sum(final, axis=0, keepdims=True)


def finish(place, totals, projected, history_in, norm_gain, out_proj):
    row_count, model_width = history_in.shape
    tile = row_tile(row_count)
    rows = pl.BlockSpec((tile, model_width), lambda step, place: (step, 0))
    whole = pl.BlockSpec((1, model_width), lambda step, place: (0, 0))
    return pl.pallas_call(
        finish_kernel,
        out_shape=(
            jax.ShapeDtypeStruct(history_in.shape, history_in.dtype),
            jax.ShapeDtypeStruct((1, model_width), jnp.float32),
        ),
        grid_spec=pltpu.PrefetchScalarGridSpec(
            num_scalar_prefetch=1,
            grid=(row_count // tile,),
            in_specs=[
                rows,
                rows,
                rows,
                whole,
                pl.BlockSpec(out_proj.shape, lambda step, place: (0, 0)),
            ],
            out_specs=(rows, whole),
        ),
        compiler_params=pltpu.CompilerParams(vmem_limit_bytes=VMEM_LIMIT),
        cost_estimate=pl.CostEstimate(
            flops=2 * row_count * model_width * model_width,
            bytes_accessed=10 * row_count * model_width + 2 * model_width * model_width,
            transcendentals=row_count,
        ),
    )(place, totals, projected, history_in, norm_gain.reshape(1, -1), out_proj)


def score_kernel(last_ref, rows_ref, user_ref, cand_ref, down_ref, up_ref, bias_ref, weight_ref, out_ref):
    peers, model_width = rows_ref.shape
    cand_count = cand_ref.shape[0]
    cand_user = user_ref[...]

    def visit(user, found):
        return jnp.where(cand_user == user, last_ref[user], found)

    cand_dev = lax.fori_loop(0, last_ref.shape[0], visit, jnp.zeros_like(cand_user))
    device_ids = lax.broadcasted_iota(jnp.int32, (peers, cand_count), 0)
    selector = jnp.where(device_ids == cand_dev, 1.0, 0.0).astype(jnp.bfloat16)
    user_part = lax.dot_general(
        selector,
        rows_ref[...].astype(jnp.bfloat16),
        (((0,), (0,)), ((), ())),
        preferred_element_type=jnp.float32,
    ).astype(jnp.bfloat16)
    cand_part = cand_ref[...]
    low_rank = jnp.dot(user_part, down_ref[:model_width, :], preferred_element_type=jnp.float32)
    low_rank += jnp.dot(cand_part, down_ref[model_width:, :], preferred_element_type=jnp.float32)
    low_rank = low_rank.astype(jnp.bfloat16)
    score = jnp.zeros((cand_count, 1), jnp.float32)
    for part, low in ((user_part, 0), (cand_part, model_width)):
        cut = slice(low, low + model_width)
        up_part = jnp.dot(low_rank, up_ref[:, cut], preferred_element_type=jnp.float32)
        value = part.astype(jnp.float32)
        crossed = value * (up_part + bias_ref[:, cut]) + value
        score += jnp.sum(crossed * weight_ref[:, cut], axis=1, keepdims=True)
    row_ids = lax.broadcasted_iota(jnp.int32, (cand_count, cand_count), 0)
    column_ids = lax.broadcasted_iota(jnp.int32, (cand_count, cand_count), 1)
    out_ref[...] = jnp.sum(jnp.where(row_ids == column_ids, score, 0.0), axis=0, keepdims=True)


def score(last_dev, user_rows, cand_user, cand_emb, cross_down, cross_up, cross_bias, score_weight):
    vmem = pl.BlockSpec(memory_space=pltpu.VMEM)
    cand_count = cand_emb.shape[0]
    scores = pl.pallas_call(
        score_kernel,
        out_shape=jax.ShapeDtypeStruct((1, cand_count), jnp.float32),
        in_specs=[pl.BlockSpec(memory_space=pltpu.SMEM)] + [vmem] * 7,
        out_specs=vmem,
        compiler_params=pltpu.CompilerParams(vmem_limit_bytes=VMEM_LIMIT),
    )(
        last_dev,
        user_rows,
        cand_user.reshape(1, -1),
        cand_emb,
        cross_down,
        cross_up,
        cross_bias.reshape(1, -1),
        score_weight.reshape(1, -1),
    )
    return scores.reshape(-1)


def body(
    projected,
    history_in,
    norm_gain,
    out_proj,
    user_spans,
    user_tails,
    cand_emb,
    cand_user,
    cross_down,
    cross_up,
    cross_bias,
    score_weight,
):
    peers = lax.axis_size("seq")
    place, last_dev = find_place(lax.axis_index("seq"), user_spans, user_tails)
    branches = [functools.partial(group_attention, 1, 0, peers)]
    for span in range(2, SPAN + 1):
        for residue in range(2 if span == 2 else SPAN):
            branches.append(functools.partial(group_attention, span, residue, peers))
    totals = lax.switch(place[4], branches, place, projected)
    history_out, final_row = finish(place, totals, projected, history_in, norm_gain, out_proj)
    user_rows = lax.all_gather(final_row, "seq", axis=0, tiled=True)
    scores = score(
        last_dev, user_rows, cand_user, cand_emb, cross_down, cross_up, cross_bias, score_weight
    )
    return (history_out, scores)


def solution(mesh):
    in_specs = (
        P(("rep", "seq"), None),
        P(("rep", "seq"), None),
        P(),
        P(),
        P("rep"),
        P("rep"),
        P(("rep", "seq"), None),
        P(("rep", "seq")),
        P(),
        P(),
        P(),
        P(),
    )
    out_specs = (P(("rep", "seq"), None), P(("rep", "seq")))
    return jax.shard_map(body, mesh=mesh, in_specs=in_specs, out_specs=out_specs, check_vma=False)
```

```python
import functools

import jax
import jax.numpy as jnp
from jax import lax
from jax.experimental import pallas as pl
from jax.experimental.pallas import tpu as pltpu
from jax.sharding import PartitionSpec as P

HEADS = 8
SPAN = 4
CHUNK_PARTS = (6, 2)
COST_SCALE = 5
KINDS = (
    (1, 0),
    (2, 1),
    *((4, residue) for residue in range(SPAN)),
    *((3, residue) for residue in range(SPAN)),
    (2, 0),
)
VMEM_LIMIT = 63 * 1024 * 1024


def silu_weights(logits, score_scale):
    half = logits * (0.5 * score_scale)
    return half + half * jnp.tanh(half)


def row_tile(row_count):
    return 256 if row_count % 256 == 0 else row_count


def dot_nt(left, right):
    return lax.dot_general(left, right, (((1,), (1,)), ((), ())), preferred_element_type=jnp.float32)


def place_kernel(me_ref, spans_ref, tails_ref, place_ref, last_ref):
    users = spans_ref.shape[0]
    me = me_ref[0]

    def visit(user, state):
        begin, span, start, tail = state
        end = begin + spans_ref[user]
        mine = (begin <= me) & (me < end)
        last_ref[user] = end - 1
        return (
            end,
            jnp.where(mine, spans_ref[user], span),
            jnp.where(mine, begin, start),
            jnp.where(mine, tails_ref[user], tail),
        )

    zero = jnp.int32(0)
    _, span, start, tail = lax.fori_loop(0, users, visit, (zero, zero + 1, zero, zero))
    place_ref[0] = span
    place_ref[1] = start
    place_ref[2] = me - start
    place_ref[3] = tail
    kind = jnp.int32(0)
    for index, (its_span, residue) in enumerate(KINDS):
        period = 2 if its_span == 2 else SPAN
        fits = (span == its_span) & (lax.rem(start, period) == residue)
        kind = jnp.where(fits, index, kind)
    place_ref[4] = kind


def find_place(me, user_spans, user_tails):
    smem = pl.BlockSpec(memory_space=pltpu.SMEM)
    return pl.pallas_call(
        place_kernel,
        out_shape=(
            jax.ShapeDtypeStruct((8,), jnp.int32),
            jax.ShapeDtypeStruct(user_spans.shape, jnp.int32),
        ),
        in_specs=[smem] * 3,
        out_specs=(smem, smem),
    )(me.reshape(1), user_spans, user_tails)


def own_kernel(score_scale, q_ref, k_ref, v_ref, out_ref):
    row_count = q_ref.shape[0]
    tile = row_tile(row_count)
    for first in range(0, row_count, tile):
        last = first + tile
        weights = silu_weights(dot_nt(q_ref[first:last, :], k_ref[:last, :]), score_scale)
        row_ids = first + lax.broadcasted_iota(jnp.int32, weights.shape, 0)
        key_ids = lax.broadcasted_iota(jnp.int32, weights.shape, 1)
        weights = jnp.where(key_ids <= row_ids, weights, 0.0).astype(jnp.bfloat16)
        out_ref[first:last, :] = jnp.dot(
            weights, v_ref[:last, :], preferred_element_type=jnp.float32
        )


def own_attention(projected):
    row_count, width = projected.shape
    model_width = width // 4
    head_size = model_width // HEADS

    def columns(part):
        return pl.BlockSpec((row_count, head_size), lambda head: (0, part * HEADS + head))

    return pl.pallas_call(
        functools.partial(own_kernel, head_size ** (-0.5)),
        out_shape=jax.ShapeDtypeStruct((row_count, model_width), jnp.float32),
        grid=(HEADS,),
        in_specs=[columns(1), columns(2), columns(3)],
        out_specs=pl.BlockSpec((row_count, head_size), lambda head: (0, head)),
        compiler_params=pltpu.CompilerParams(vmem_limit_bytes=VMEM_LIMIT),
        cost_estimate=pl.CostEstimate(
            flops=COST_SCALE * 3 * row_count * row_count * model_width,
            bytes_accessed=10 * row_count * model_width,
            transcendentals=row_count * row_count * HEADS,
        ),
    )(projected, projected, projected)


def add_kernel(score_scale, holders, skipped, unrolled, place_ref, q_ref, *refs):
    source_refs, (total_ref, out_ref, slots, arrived) = refs[: len(holders)], refs[-4:]
    head, position = pl.program_id(0), place_ref[2]
    row_count, head_size = q_ref.shape
    tile = row_tile(row_count)
    counts = {}
    for source_ref, positions in zip(source_refs, holders):
        for place in positions:
            slot = counts.get(place, 0)
            counts[place] = slot + 1

            @pl.when((head == 0) & (position == place))
            def _():
                pltpu.make_async_copy(source_ref, slots.at[slot], arrived.at[slot]).start()

    out_ref[...] = total_ref[...]
    count = sum(jnp.where(position == place, number, 0) for place, number in counts.items())
    low = pl.multiple_of((skipped + head) * head_size, head_size)
    key_columns = pl.ds(low, head_size)
    value_columns = pl.ds(pl.multiple_of(slots.shape[2] // 2 + low, head_size), head_size)

    @pl.loop(0, count)
    def _(slot):
        @pl.when(head == 0)
        def _():
            pltpu.make_async_copy(source_refs[0], slots.at[slot], arrived.at[slot]).wait()

        def add_rows(step):
            rows = pl.ds(pl.multiple_of(step * tile, tile), tile)
            logits = dot_nt(q_ref[rows, :], slots[slot, :, key_columns])
            weights = silu_weights(logits, score_scale).astype(jnp.bfloat16)
            out_ref[rows, :] += jnp.dot(
                weights, slots[slot, :, value_columns], preferred_element_type=jnp.float32
            )

        if unrolled:
            for step in range(row_count // tile):
                add_rows(step)
        else:
            pl.loop(0, row_count // tile)(add_rows)


def add_sources(place, projected, totals, sources, first_head, skipped, heads, unrolled):
    row_count, width = projected.shape
    model_width = width // 4
    head_size = model_width // HEADS
    arrays = [array for array, _ in sources]
    holders = [positions for _, positions in sources]
    everyone = [position for positions in holders for position in positions]
    most = max(everyone.count(position) for position in everyone)
    first_head += skipped
    total_spec = pl.BlockSpec((row_count, head_size), lambda head, place: (0, first_head + head))
    return pl.pallas_call(
        functools.partial(add_kernel, head_size ** (-0.5), holders, skipped, unrolled),
        out_shape=jax.ShapeDtypeStruct(totals.shape, totals.dtype),
        grid_spec=pltpu.PrefetchScalarGridSpec(
            num_scalar_prefetch=1,
            grid=(heads,),
            in_specs=[
                pl.BlockSpec((row_count, head_size), lambda head, place: (0, HEADS + first_head + head)),
                *[pl.BlockSpec(memory_space=pl.ANY)] * len(arrays),
                total_spec,
            ],
            out_specs=total_spec,
            scratch_shapes=[
                pltpu.VMEM((most, *arrays[0].shape), projected.dtype),
                pltpu.SemaphoreType.DMA((most,)),
            ],
        ),
        input_output_aliases={2 + len(arrays): 0},
        compiler_params=pltpu.CompilerParams(vmem_limit_bytes=VMEM_LIMIT),
        cost_estimate=pl.CostEstimate(
            flops=COST_SCALE * 4 * row_count * row_count * heads * head_size * most,
            bytes_accessed=(6 + 4 * most) * row_count * heads * head_size,
            transcendentals=row_count * row_count * heads * most,
        ),
    )(place, projected, *arrays, totals)


def pack_kernel(projected_ref, *refs):
    count = (len(refs) - 2) // 2
    packed_refs, held_refs, (loaded, stored) = refs[:count], refs[count:-2], refs[-2:]
    model_width = projected_ref.shape[1] // 4
    low, loads, stores = 0, [], []
    for packed_ref, held_ref in zip(packed_refs, held_refs):
        width = packed_ref.shape[1] // 2
        for part in range(2):
            source = projected_ref.at[:, pl.ds((2 + part) * model_width + low, width)]
            held = held_ref.at[:, pl.ds(part * width, width)]
            target = packed_ref.at[:, pl.ds(part * width, width)]
            loads.append(pltpu.make_async_copy(source, held, loaded.at[len(loads)]))
            stores.append(pltpu.make_async_copy(held, target, stored.at[len(stores)]))
        low += width
    for load in loads:
        load.start()
    for load, store in zip(loads, stores):
        load.wait()
        store.start()
    for store in stores:
        store.wait()


def pack_key_values(projected, parts):
    row_count, width = projected.shape
    anywhere = pl.BlockSpec(memory_space=pl.ANY)
    shapes = [(row_count, heads * width // (2 * HEADS)) for heads in parts]
    return pl.pallas_call(
        pack_kernel,
        out_shape=[jax.ShapeDtypeStruct(shape, projected.dtype) for shape in shapes],
        in_specs=[anywhere],
        out_specs=[anywhere] * len(parts),
        scratch_shapes=[
            *[pltpu.VMEM(shape, projected.dtype) for shape in shapes],
            *[pltpu.SemaphoreType.DMA((2 * len(parts),))] * 2,
        ],
        compiler_params=pltpu.CompilerParams(vmem_limit_bytes=VMEM_LIMIT),
        cost_estimate=pl.CostEstimate(
            flops=0, bytes_accessed=2 * row_count * width, transcendentals=0
        ),
    )(projected)


def tie_kernel(array_ref, after_ref, out_ref):
    pass


def tie(array, after):
    anywhere = pl.BlockSpec(memory_space=pl.ANY)
    return pl.pallas_call(
        tie_kernel,
        out_shape=jax.ShapeDtypeStruct(array.shape, array.dtype),
        in_specs=[anywhere, anywhere],
        out_specs=anywhere,
        input_output_aliases={0: 0},
    )(array, after)


def group_attention(span, residue, peers, place, projected):
    if span == 1:
        return own_attention(projected)
    period = 2 if span == 2 else SPAN

    def send(array, *hops):
        pairs = []
        for position, target in hops:
            lowest, by = (residue + position) % period, target - position
            pairs += [(s, s + by) for s in range(lowest, peers, period) if s + by < peers]
        return lax.ppermute(array, "seq", pairs)

    def swap(array, position):
        lowest = (residue + position) % period
        pairs = [(s, s + 1) for s in range(lowest, peers, period) if s + 1 < peers]
        return lax.ppermute(array, "seq", pairs + [(b, a) for a, b in pairs])

    chips = {}
    for position in range(span):
        chips.setdefault((residue + position) // 2, []).append(position)
    chips = list(chips.values())
    inner = [tuple(chip) for chip in chips if len(chip) == 2]

    def exchange(mine, after):
        if span == 2:
            return [(send(mine, (0, 1)), [1])]
        if span == 3 and len(chips[0]) == 2:
            return [(send(mine, (0, 2)), [2]), (send(mine, (1, 2)), [2])]
        if span == 3:
            came = tie(send(mine, (0, 2)), after)
            return [(came, [2]), (swap(came, 1), [1])]
        came = send(mine, (0, 2), (1, 3))
        if len(chips) == 2:
            came = tie(came, after)
            return [(came, [2, 3]), (swap(came, 2), [2, 3])]
        found = [(send(mine, (2, 3)), [3])]
        came = tie(came, after)
        return [(came, [2, 3]), (swap(came, 1), [1]), *found]

    early, late = CHUNK_PARTS
    mine, rest = pack_key_values(projected, CHUNK_PARTS)
    totals = own_attention(projected)
    if span > 2:
        hops = inner if len(chips) == 2 else [(0, 3), (1, 2)]
        holders = [target for _, target in hops]
        first, second = [(send(mine, *hops), holders)], [(send(rest, *hops), holders)]
        totals = add_sources(place, projected, totals, first, 0, 0, early, False)
    found = exchange(mine, totals)
    if span > 2:
        totals = add_sources(place, projected, totals, second, early, 0, late, False)
    totals = add_sources(place, projected, totals, found, 0, 0, early, False)
    more = exchange(rest, totals)
    return add_sources(place, projected, totals, more, early, 0, late, True)


def finish_kernel(place_ref, total_ref, u_ref, history_ref, gain_ref, weight_ref, out_ref, last_ref):
    step = pl.program_id(0)
    tile = total_ref.shape[0]
    row_count = tile * pl.num_programs(0)
    span, position, tail = place_ref[0], place_ref[2], place_ref[3]
    valid = jnp.where(position == span - 1, tail, row_count)
    row_ids = step * tile + lax.broadcasted_iota(jnp.int32, (tile, 1), 0)
    attention = jnp.where(row_ids < valid, total_ref[...], 0.0)
    row_mean = jnp.mean(attention, axis=1, keepdims=True)
    centered = attention - row_mean
    row_var = jnp.mean(centered * centered, axis=1, keepdims=True)
    normed = centered * lax.rsqrt(row_var + 1e-06) * gain_ref[...]
    gated = (normed * u_ref[...].astype(jnp.float32)).astype(jnp.bfloat16)
    out = jnp.dot(gated, weight_ref[...], preferred_element_type=jnp.float32)
    out = (out + history_ref[...].astype(jnp.float32)).astype(jnp.bfloat16)
    out_ref[...] = out

    @pl.when(valid - 1 - step * tile == jnp.clip(valid - 1 - step * tile, 0, tile - 1))
    def _():
        final = jnp.where(row_ids == valid - 1, out.astype(jnp.float32), 0.0)
        last_ref[...] = jnp.sum(final, axis=0, keepdims=True)


def finish(place, totals, projected, history_in, norm_gain, out_proj):
    row_count, model_width = history_in.shape
    tile = row_tile(row_count)
    rows = pl.BlockSpec((tile, model_width), lambda step, place: (step, 0))
    whole = pl.BlockSpec((1, model_width), lambda step, place: (0, 0))
    return pl.pallas_call(
        finish_kernel,
        out_shape=(
            jax.ShapeDtypeStruct(history_in.shape, history_in.dtype),
            jax.ShapeDtypeStruct((1, model_width), jnp.float32),
        ),
        grid_spec=pltpu.PrefetchScalarGridSpec(
            num_scalar_prefetch=1,
            grid=(row_count // tile,),
            in_specs=[
                rows,
                rows,
                rows,
                whole,
                pl.BlockSpec(out_proj.shape, lambda step, place: (0, 0)),
            ],
            out_specs=(rows, whole),
        ),
        compiler_params=pltpu.CompilerParams(vmem_limit_bytes=VMEM_LIMIT),
        cost_estimate=pl.CostEstimate(
            flops=2 * row_count * model_width * model_width,
            bytes_accessed=10 * row_count * model_width + 2 * model_width * model_width,
            transcendentals=row_count,
        ),
    )(place, totals, projected, history_in, norm_gain.reshape(1, -1), out_proj)


def score_kernel(last_ref, rows_ref, user_ref, cand_ref, down_ref, up_ref, bias_ref, weight_ref, out_ref):
    peers, model_width = rows_ref.shape
    cand_count = cand_ref.shape[0]
    cand_user = user_ref[...]

    def visit(user, found):
        return jnp.where(cand_user == user, last_ref[user], found)

    cand_dev = lax.fori_loop(0, last_ref.shape[0], visit, jnp.zeros_like(cand_user))
    device_ids = lax.broadcasted_iota(jnp.int32, (peers, cand_count), 0)
    selector = jnp.where(device_ids == cand_dev, 1.0, 0.0).astype(jnp.bfloat16)
    user_part = lax.dot_general(
        selector,
        rows_ref[...].astype(jnp.bfloat16),
        (((0,), (0,)), ((), ())),
        preferred_element_type=jnp.float32,
    ).astype(jnp.bfloat16)
    cand_part = cand_ref[...]
    low_rank = jnp.dot(user_part, down_ref[:model_width, :], preferred_element_type=jnp.float32)
    low_rank += jnp.dot(cand_part, down_ref[model_width:, :], preferred_element_type=jnp.float32)
    low_rank = low_rank.astype(jnp.bfloat16)
    score = jnp.zeros((cand_count, 1), jnp.float32)
    for part, low in ((user_part, 0), (cand_part, model_width)):
        cut = slice(low, low + model_width)
        up_part = jnp.dot(low_rank, up_ref[:, cut], preferred_element_type=jnp.float32)
        value = part.astype(jnp.float32)
        crossed = value * (up_part + bias_ref[:, cut]) + value
        score += jnp.sum(crossed * weight_ref[:, cut], axis=1, keepdims=True)
    row_ids = lax.broadcasted_iota(jnp.int32, (cand_count, cand_count), 0)
    column_ids = lax.broadcasted_iota(jnp.int32, (cand_count, cand_count), 1)
    out_ref[...] = jnp.sum(jnp.where(row_ids == column_ids, score, 0.0), axis=0, keepdims=True)


def score(last_dev, user_rows, cand_user, cand_emb, cross_down, cross_up, cross_bias, score_weight):
    vmem = pl.BlockSpec(memory_space=pltpu.VMEM)
    cand_count = cand_emb.shape[0]
    scores = pl.pallas_call(
        score_kernel,
        out_shape=jax.ShapeDtypeStruct((1, cand_count), jnp.float32),
        in_specs=[pl.BlockSpec(memory_space=pltpu.SMEM)] + [vmem] * 7,
        out_specs=vmem,
        compiler_params=pltpu.CompilerParams(vmem_limit_bytes=VMEM_LIMIT),
    )(
        last_dev,
        user_rows,
        cand_user.reshape(1, -1),
        cand_emb,
        cross_down,
        cross_up,
        cross_bias.reshape(1, -1),
        score_weight.reshape(1, -1),
    )
    return scores.reshape(-1)


def body(
    projected,
    history_in,
    norm_gain,
    out_proj,
    user_spans,
    user_tails,
    cand_emb,
    cand_user,
    cross_down,
    cross_up,
    cross_bias,
    score_weight,
):
    peers = lax.axis_size("seq")
    place, last_dev = find_place(lax.axis_index("seq"), user_spans, user_tails)
    branches = [
        functools.partial(group_attention, span, residue, peers) for span, residue in KINDS
    ]
    totals = lax.switch(place[4], branches, place, projected)
    history_out, final_row = finish(place, totals, projected, history_in, norm_gain, out_proj)
    user_rows = lax.all_gather(final_row, "seq", axis=0, tiled=True)
    scores = score(
        last_dev, user_rows, cand_user, cand_emb, cross_down, cross_up, cross_bias, score_weight
    )
    return (history_out, scores)


def solution(mesh):
    in_specs = (
        P(("rep", "seq"), None),
        P(("rep", "seq"), None),
        P(),
        P(),
        P("rep"),
        P("rep"),
        P(("rep", "seq"), None),
        P(("rep", "seq")),
        P(),
        P(),
        P(),
        P(),
    )
    out_specs = (P(("rep", "seq"), None), P(("rep", "seq")))
    return jax.shard_map(body, mesh=mesh, in_specs=in_specs, out_specs=out_specs, check_vma=False)
```

```python
import functools

import jax
import jax.numpy as jnp
from jax import lax
from jax.experimental import pallas as pl
from jax.experimental.pallas import tpu as pltpu
from jax.sharding import PartitionSpec as P

HEADS = 8
SPAN = 4
CHUNK_PARTS = (5, 3)
COST_SCALE = 5
KINDS = (
    (1, 0),
    (2, 0),
    (2, 1),
    *((3, residue) for residue in range(SPAN)),
    *((4, residue) for residue in range(SPAN)),
)
VMEM_LIMIT = 63 * 1024 * 1024


def silu_weights(logits, score_scale):
    half = logits * (0.5 * score_scale)
    return half + half * jnp.tanh(half)


def row_tile(row_count):
    return 256 if row_count % 256 == 0 else row_count


def dot_nt(left, right):
    return lax.dot_general(left, right, (((1,), (1,)), ((), ())), preferred_element_type=jnp.float32)


def place_kernel(me_ref, spans_ref, tails_ref, place_ref, last_ref):
    users = spans_ref.shape[0]
    me = me_ref[0]

    def visit(user, state):
        begin, span, start, tail = state
        end = begin + spans_ref[user]
        mine = (begin <= me) & (me < end)
        last_ref[user] = end - 1
        return (
            end,
            jnp.where(mine, spans_ref[user], span),
            jnp.where(mine, begin, start),
            jnp.where(mine, tails_ref[user], tail),
        )

    zero = jnp.int32(0)
    _, span, start, tail = lax.fori_loop(0, users, visit, (zero, zero + 1, zero, zero))
    place_ref[0] = span
    place_ref[1] = start
    place_ref[2] = me - start
    place_ref[3] = tail
    kind = jnp.int32(0)
    for index, (its_span, residue) in enumerate(KINDS):
        period = 2 if its_span == 2 else SPAN
        fits = (span == its_span) & (lax.rem(start, period) == residue)
        kind = jnp.where(fits, index, kind)
    place_ref[4] = kind


def find_place(me, user_spans, user_tails):
    smem = pl.BlockSpec(memory_space=pltpu.SMEM)
    return pl.pallas_call(
        place_kernel,
        out_shape=(
            jax.ShapeDtypeStruct((8,), jnp.int32),
            jax.ShapeDtypeStruct(user_spans.shape, jnp.int32),
        ),
        in_specs=[smem] * 3,
        out_specs=(smem, smem),
    )(me.reshape(1), user_spans, user_tails)


def own_kernel(score_scale, q_ref, k_ref, v_ref, out_ref):
    row_count = q_ref.shape[0]
    tile = row_tile(row_count)

    @pl.loop(0, row_count // tile)
    def _(step):
        rows = pl.ds(pl.multiple_of(step * tile, tile), tile)
        weights = silu_weights(dot_nt(q_ref[rows, :], k_ref[...]), score_scale)
        row_ids = step * tile + lax.broadcasted_iota(jnp.int32, weights.shape, 0)
        key_ids = lax.broadcasted_iota(jnp.int32, weights.shape, 1)
        weights = jnp.where(key_ids <= row_ids, weights, 0.0).astype(jnp.bfloat16)
        out_ref[rows, :] = jnp.dot(weights, v_ref[...], preferred_element_type=jnp.float32)


def own_attention(projected):
    row_count, width = projected.shape
    model_width = width // 4
    head_size = model_width // HEADS

    def columns(part):
        return pl.BlockSpec((row_count, head_size), lambda head: (0, part * HEADS + head))

    return pl.pallas_call(
        functools.partial(own_kernel, head_size ** (-0.5)),
        out_shape=jax.ShapeDtypeStruct((row_count, model_width), jnp.float32),
        grid=(HEADS,),
        in_specs=[columns(1), columns(2), columns(3)],
        out_specs=pl.BlockSpec((row_count, head_size), lambda head: (0, head)),
        compiler_params=pltpu.CompilerParams(vmem_limit_bytes=VMEM_LIMIT),
        cost_estimate=pl.CostEstimate(
            flops=COST_SCALE * 3 * row_count * row_count * model_width,
            bytes_accessed=10 * row_count * model_width,
            transcendentals=row_count * row_count * HEADS,
        ),
    )(projected, projected, projected)


def add_kernel(score_scale, holders, skipped, unrolled, place_ref, q_ref, *refs):
    source_refs, (total_ref, out_ref, slots, arrived) = refs[: len(holders)], refs[-4:]
    head, position = pl.program_id(0), place_ref[2]
    row_count, head_size = q_ref.shape
    tile = row_tile(row_count)
    counts = {}
    for source_ref, positions in zip(source_refs, holders):
        for place in positions:
            slot = counts.get(place, 0)
            counts[place] = slot + 1

            @pl.when((head == 0) & (position == place))
            def _():
                pltpu.make_async_copy(source_ref, slots.at[slot], arrived.at[slot]).start()

    out_ref[...] = total_ref[...]
    count = sum(jnp.where(position == place, number, 0) for place, number in counts.items())
    low = pl.multiple_of((skipped + head) * head_size, head_size)
    key_columns = pl.ds(low, head_size)
    value_columns = pl.ds(pl.multiple_of(slots.shape[2] // 2 + low, head_size), head_size)

    @pl.loop(0, count)
    def _(slot):
        @pl.when(head == 0)
        def _():
            pltpu.make_async_copy(source_refs[0], slots.at[slot], arrived.at[slot]).wait()

        def add_rows(step):
            rows = pl.ds(pl.multiple_of(step * tile, tile), tile)
            logits = dot_nt(q_ref[rows, :], slots[slot, :, key_columns])
            weights = silu_weights(logits, score_scale).astype(jnp.bfloat16)
            out_ref[rows, :] += jnp.dot(
                weights, slots[slot, :, value_columns], preferred_element_type=jnp.float32
            )

        if unrolled:
            for step in range(row_count // tile):
                add_rows(step)
        else:
            pl.loop(0, row_count // tile)(add_rows)


def add_sources(place, projected, totals, sources, first_head, skipped, heads, unrolled):
    row_count, width = projected.shape
    model_width = width // 4
    head_size = model_width // HEADS
    arrays = [array for array, _ in sources]
    holders = [positions for _, positions in sources]
    everyone = [position for positions in holders for position in positions]
    most = max(everyone.count(position) for position in everyone)
    first_head += skipped
    total_spec = pl.BlockSpec((row_count, head_size), lambda head, place: (0, first_head + head))
    return pl.pallas_call(
        functools.partial(add_kernel, head_size ** (-0.5), holders, skipped, unrolled),
        out_shape=jax.ShapeDtypeStruct(totals.shape, totals.dtype),
        grid_spec=pltpu.PrefetchScalarGridSpec(
            num_scalar_prefetch=1,
            grid=(heads,),
            in_specs=[
                pl.BlockSpec((row_count, head_size), lambda head, place: (0, HEADS + first_head + head)),
                *[pl.BlockSpec(memory_space=pl.ANY)] * len(arrays),
                total_spec,
            ],
            out_specs=total_spec,
            scratch_shapes=[
                pltpu.VMEM((most, *arrays[0].shape), projected.dtype),
                pltpu.SemaphoreType.DMA((most,)),
            ],
        ),
        input_output_aliases={2 + len(arrays): 0},
        compiler_params=pltpu.CompilerParams(vmem_limit_bytes=VMEM_LIMIT),
        cost_estimate=pl.CostEstimate(
            flops=COST_SCALE * 4 * row_count * row_count * heads * head_size * most,
            bytes_accessed=(6 + 4 * most) * row_count * heads * head_size,
            transcendentals=row_count * row_count * heads * most,
        ),
    )(place, projected, *arrays, totals)


def pack_kernel(projected_ref, *refs):
    count = (len(refs) - 2) // 2
    packed_refs, held_refs, (loaded, stored) = refs[:count], refs[count:-2], refs[-2:]
    model_width = projected_ref.shape[1] // 4
    low, loads, stores = 0, [], []
    for packed_ref, held_ref in zip(packed_refs, held_refs):
        width = packed_ref.shape[1] // 2
        for part in range(2):
            source = projected_ref.at[:, pl.ds((2 + part) * model_width + low, width)]
            held = held_ref.at[:, pl.ds(part * width, width)]
            target = packed_ref.at[:, pl.ds(part * width, width)]
            loads.append(pltpu.make_async_copy(source, held, loaded.at[len(loads)]))
            stores.append(pltpu.make_async_copy(held, target, stored.at[len(stores)]))
        low += width
    for load in loads:
        load.start()
    for load, store in zip(loads, stores):
        load.wait()
        store.start()
    for store in stores:
        store.wait()


def pack_key_values(projected, parts):
    row_count, width = projected.shape
    anywhere = pl.BlockSpec(memory_space=pl.ANY)
    shapes = [(row_count, heads * width // (2 * HEADS)) for heads in parts]
    return pl.pallas_call(
        pack_kernel,
        out_shape=[jax.ShapeDtypeStruct(shape, projected.dtype) for shape in shapes],
        in_specs=[anywhere],
        out_specs=[anywhere] * len(parts),
        scratch_shapes=[
            *[pltpu.VMEM(shape, projected.dtype) for shape in shapes],
            *[pltpu.SemaphoreType.DMA((2 * len(parts),))] * 2,
        ],
        compiler_params=pltpu.CompilerParams(vmem_limit_bytes=VMEM_LIMIT),
        cost_estimate=pl.CostEstimate(
            flops=0, bytes_accessed=2 * row_count * width, transcendentals=0
        ),
    )(projected)


def tie_kernel(array_ref, after_ref, out_ref):
    pass


def tie(array, after):
    anywhere = pl.BlockSpec(memory_space=pl.ANY)
    return pl.pallas_call(
        tie_kernel,
        out_shape=jax.ShapeDtypeStruct(array.shape, array.dtype),
        in_specs=[anywhere, anywhere],
        out_specs=anywhere,
        input_output_aliases={0: 0},
    )(array, after)


def group_attention(span, residue, peers, place, projected):
    if span == 1:
        return own_attention(projected)
    period = 2 if span == 2 else SPAN

    def send(array, *hops):
        pairs = []
        for position, target in hops:
            lowest, by = (residue + position) % period, target - position
            pairs += [(s, s + by) for s in range(lowest, peers, period) if s + by < peers]
        return lax.ppermute(array, "seq", pairs)

    def swap(array, position):
        lowest = (residue + position) % period
        pairs = [(s, s + 1) for s in range(lowest, peers, period) if s + 1 < peers]
        return lax.ppermute(array, "seq", pairs + [(b, a) for a, b in pairs])

    chips = {}
    for position in range(span):
        chips.setdefault((residue + position) // 2, []).append(position)
    chips = list(chips.values())
    inner = [tuple(chip) for chip in chips if len(chip) == 2]

    def exchange(mine, after):
        if span == 2:
            return [(send(mine, (0, 1)), [1])]
        if span == 3 and len(chips[0]) == 2:
            return [(send(mine, (0, 2)), [2]), (send(mine, (1, 2)), [2])]
        if span == 3:
            came = tie(send(mine, (0, 2)), after)
            return [(came, [2]), (swap(came, 1), [1])]
        came = send(mine, (0, 2), (1, 3))
        if len(chips) == 2:
            came = tie(came, after)
            return [(came, [2, 3]), (swap(came, 2), [2, 3])]
        found = [(send(mine, (2, 3)), [3])]
        came = tie(came, after)
        return [(came, [2, 3]), (swap(came, 1), [1]), *found]

    early, late = CHUNK_PARTS
    mine, rest = pack_key_values(projected, CHUNK_PARTS)
    totals = own_attention(projected)
    if span > 2:
        hops = inner if len(chips) == 2 else [(0, 3), (1, 2)]
        holders = [target for _, target in hops]
        first, second = [(send(mine, *hops), holders)], [(send(rest, *hops), holders)]
        totals = add_sources(place, projected, totals, first, 0, 0, early, False)
    found = exchange(mine, totals)
    if span > 2:
        totals = add_sources(place, projected, totals, second, early, 0, late, False)
    totals = add_sources(place, projected, totals, found, 0, 0, early, False)
    more = exchange(rest, totals)
    return add_sources(place, projected, totals, more, early, 0, late, True)


def finish_kernel(place_ref, total_ref, u_ref, history_ref, gain_ref, weight_ref, out_ref, last_ref):
    step = pl.program_id(0)
    tile = total_ref.shape[0]
    row_count = tile * pl.num_programs(0)
    span, position, tail = place_ref[0], place_ref[2], place_ref[3]
    valid = jnp.where(position == span - 1, tail, row_count)
    row_ids = step * tile + lax.broadcasted_iota(jnp.int32, (tile, 1), 0)
    attention = jnp.where(row_ids < valid, total_ref[...], 0.0)
    row_mean = jnp.mean(attention, axis=1, keepdims=True)
    centered = attention - row_mean
    row_var = jnp.mean(centered * centered, axis=1, keepdims=True)
    normed = centered * lax.rsqrt(row_var + 1e-06) * gain_ref[...]
    gated = (normed * u_ref[...].astype(jnp.float32)).astype(jnp.bfloat16)
    out = jnp.dot(gated, weight_ref[...], preferred_element_type=jnp.float32)
    out = (out + history_ref[...].astype(jnp.float32)).astype(jnp.bfloat16)
    out_ref[...] = out

    @pl.when(valid - 1 - step * tile == jnp.clip(valid - 1 - step * tile, 0, tile - 1))
    def _():
        final = jnp.where(row_ids == valid - 1, out.astype(jnp.float32), 0.0)
        last_ref[...] = jnp.sum(final, axis=0, keepdims=True)


def finish(place, totals, projected, history_in, norm_gain, out_proj):
    row_count, model_width = history_in.shape
    tile = row_tile(row_count)
    rows = pl.BlockSpec((tile, model_width), lambda step, place: (step, 0))
    whole = pl.BlockSpec((1, model_width), lambda step, place: (0, 0))
    return pl.pallas_call(
        finish_kernel,
        out_shape=(
            jax.ShapeDtypeStruct(history_in.shape, history_in.dtype),
            jax.ShapeDtypeStruct((1, model_width), jnp.float32),
        ),
        grid_spec=pltpu.PrefetchScalarGridSpec(
            num_scalar_prefetch=1,
            grid=(row_count // tile,),
            in_specs=[
                rows,
                rows,
                rows,
                whole,
                pl.BlockSpec(out_proj.shape, lambda step, place: (0, 0)),
            ],
            out_specs=(rows, whole),
        ),
        compiler_params=pltpu.CompilerParams(vmem_limit_bytes=VMEM_LIMIT),
        cost_estimate=pl.CostEstimate(
            flops=2 * row_count * model_width * model_width,
            bytes_accessed=10 * row_count * model_width + 2 * model_width * model_width,
            transcendentals=row_count,
        ),
    )(place, totals, projected, history_in, norm_gain.reshape(1, -1), out_proj)


def score_kernel(last_ref, rows_ref, user_ref, cand_ref, down_ref, up_ref, bias_ref, weight_ref, out_ref):
    peers, model_width = rows_ref.shape
    cand_count = cand_ref.shape[0]
    cand_user = user_ref[...]

    def visit(user, found):
        return jnp.where(cand_user == user, last_ref[user], found)

    cand_dev = lax.fori_loop(0, last_ref.shape[0], visit, jnp.zeros_like(cand_user))
    device_ids = lax.broadcasted_iota(jnp.int32, (peers, cand_count), 0)
    selector = jnp.where(device_ids == cand_dev, 1.0, 0.0).astype(jnp.bfloat16)
    user_part = lax.dot_general(
        selector,
        rows_ref[...].astype(jnp.bfloat16),
        (((0,), (0,)), ((), ())),
        preferred_element_type=jnp.float32,
    ).astype(jnp.bfloat16)
    cand_part = cand_ref[...]
    low_rank = jnp.dot(user_part, down_ref[:model_width, :], preferred_element_type=jnp.float32)
    low_rank += jnp.dot(cand_part, down_ref[model_width:, :], preferred_element_type=jnp.float32)
    low_rank = low_rank.astype(jnp.bfloat16)
    score = jnp.zeros((cand_count, 1), jnp.float32)
    for part, low in ((user_part, 0), (cand_part, model_width)):
        cut = slice(low, low + model_width)
        up_part = jnp.dot(low_rank, up_ref[:, cut], preferred_element_type=jnp.float32)
        value = part.astype(jnp.float32)
        crossed = value * (up_part + bias_ref[:, cut]) + value
        score += jnp.sum(crossed * weight_ref[:, cut], axis=1, keepdims=True)
    row_ids = lax.broadcasted_iota(jnp.int32, (cand_count, cand_count), 0)
    column_ids = lax.broadcasted_iota(jnp.int32, (cand_count, cand_count), 1)
    out_ref[...] = jnp.sum(jnp.where(row_ids == column_ids, score, 0.0), axis=0, keepdims=True)


def score(last_dev, user_rows, cand_user, cand_emb, cross_down, cross_up, cross_bias, score_weight):
    vmem = pl.BlockSpec(memory_space=pltpu.VMEM)
    cand_count = cand_emb.shape[0]
    scores = pl.pallas_call(
        score_kernel,
        out_shape=jax.ShapeDtypeStruct((1, cand_count), jnp.float32),
        in_specs=[pl.BlockSpec(memory_space=pltpu.SMEM)] + [vmem] * 7,
        out_specs=vmem,
        compiler_params=pltpu.CompilerParams(vmem_limit_bytes=VMEM_LIMIT),
    )(
        last_dev,
        user_rows,
        cand_user.reshape(1, -1),
        cand_emb,
        cross_down,
        cross_up,
        cross_bias.reshape(1, -1),
        score_weight.reshape(1, -1),
    )
    return scores.reshape(-1)


def body(
    projected,
    history_in,
    norm_gain,
    out_proj,
    user_spans,
    user_tails,
    cand_emb,
    cand_user,
    cross_down,
    cross_up,
    cross_bias,
    score_weight,
):
    peers = lax.axis_size("seq")
    place, last_dev = find_place(lax.axis_index("seq"), user_spans, user_tails)
    branches = [
        functools.partial(group_attention, span, residue, peers) for span, residue in KINDS
    ]
    totals = lax.switch(place[4], branches, place, projected)
    history_out, final_row = finish(place, totals, projected, history_in, norm_gain, out_proj)
    user_rows = lax.all_gather(final_row, "seq", axis=0, tiled=True)
    scores = score(
        last_dev, user_rows, cand_user, cand_emb, cross_down, cross_up, cross_bias, score_weight
    )
    return (history_out, scores)


def solution(mesh):
    in_specs = (
        P(("rep", "seq"), None),
        P(("rep", "seq"), None),
        P(),
        P(),
        P("rep"),
        P("rep"),
        P(("rep", "seq"), None),
        P(("rep", "seq")),
        P(),
        P(),
        P(),
        P(),
    )
    out_specs = (P(("rep", "seq"), None), P(("rep", "seq")))
    return jax.shard_map(body, mesh=mesh, in_specs=in_specs, out_specs=out_specs, check_vma=False)
```

```python
import functools

import jax
import jax.numpy as jnp
from jax import lax
from jax.experimental import pallas as pl
from jax.experimental.pallas import tpu as pltpu
from jax.sharding import PartitionSpec as P

HEADS = 8
SPAN = 4
CHUNK_PARTS = (5, 3)
COST_SCALE = 5
KINDS = (
    (1, 0),
    (2, 0),
    (2, 1),
    *((3, residue) for residue in range(SPAN)),
    *((4, residue) for residue in range(SPAN)),
)
VMEM_LIMIT = 63 * 1024 * 1024


def silu_weights(logits, score_scale):
    half = logits * (0.5 * score_scale)
    return half + half * jnp.tanh(half)


def row_tile(row_count):
    return 256 if row_count % 256 == 0 else row_count


def dot_nt(left, right):
    return lax.dot_general(left, right, (((1,), (1,)), ((), ())), preferred_element_type=jnp.float32)


def place_kernel(me_ref, spans_ref, tails_ref, place_ref, last_ref):
    users = spans_ref.shape[0]
    me = me_ref[0]

    def visit(user, state):
        begin, span, start, tail = state
        end = begin + spans_ref[user]
        mine = (begin <= me) & (me < end)
        last_ref[user] = end - 1
        return (
            end,
            jnp.where(mine, spans_ref[user], span),
            jnp.where(mine, begin, start),
            jnp.where(mine, tails_ref[user], tail),
        )

    zero = jnp.int32(0)
    _, span, start, tail = lax.fori_loop(0, users, visit, (zero, zero + 1, zero, zero))
    place_ref[0] = span
    place_ref[1] = start
    place_ref[2] = me - start
    place_ref[3] = tail
    kind = jnp.int32(0)
    for index, (its_span, residue) in enumerate(KINDS):
        period = 2 if its_span == 2 else SPAN
        fits = (span == its_span) & (lax.rem(start, period) == residue)
        kind = jnp.where(fits, index, kind)
    place_ref[4] = kind


def find_place(me, user_spans, user_tails):
    smem = pl.BlockSpec(memory_space=pltpu.SMEM)
    return pl.pallas_call(
        place_kernel,
        out_shape=(
            jax.ShapeDtypeStruct((8,), jnp.int32),
            jax.ShapeDtypeStruct(user_spans.shape, jnp.int32),
        ),
        in_specs=[smem] * 3,
        out_specs=(smem, smem),
    )(me.reshape(1), user_spans, user_tails)


def own_kernel(score_scale, q_ref, k_ref, v_ref, out_ref):
    row_count = q_ref.shape[0]
    tile = row_tile(row_count)

    @pl.loop(0, row_count // tile)
    def _(step):
        rows = pl.ds(pl.multiple_of(step * tile, tile), tile)
        weights = silu_weights(dot_nt(q_ref[rows, :], k_ref[...]), score_scale)
        row_ids = step * tile + lax.broadcasted_iota(jnp.int32, weights.shape, 0)
        key_ids = lax.broadcasted_iota(jnp.int32, weights.shape, 1)
        weights = jnp.where(key_ids <= row_ids, weights, 0.0).astype(jnp.bfloat16)
        out_ref[rows, :] = jnp.dot(weights, v_ref[...], preferred_element_type=jnp.float32)


def own_attention(projected):
    row_count, width = projected.shape
    model_width = width // 4
    head_size = model_width // HEADS

    def columns(part):
        return pl.BlockSpec((row_count, head_size), lambda head: (0, part * HEADS + head))

    return pl.pallas_call(
        functools.partial(own_kernel, head_size ** (-0.5)),
        out_shape=jax.ShapeDtypeStruct((row_count, model_width), jnp.float32),
        grid=(HEADS,),
        in_specs=[columns(1), columns(2), columns(3)],
        out_specs=pl.BlockSpec((row_count, head_size), lambda head: (0, head)),
        compiler_params=pltpu.CompilerParams(vmem_limit_bytes=VMEM_LIMIT),
        cost_estimate=pl.CostEstimate(
            flops=COST_SCALE * 3 * row_count * row_count * model_width,
            bytes_accessed=10 * row_count * model_width,
            transcendentals=row_count * row_count * HEADS,
        ),
    )(projected, projected, projected)


def add_kernel(score_scale, holders, skipped, unrolled, place_ref, q_ref, *refs):
    source_refs, (total_ref, out_ref, slots, arrived) = refs[: len(holders)], refs[-4:]
    head, position = pl.program_id(0), place_ref[2]
    row_count, head_size = q_ref.shape
    tile = row_tile(row_count)
    counts = {}
    for source_ref, positions in zip(source_refs, holders):
        for place in positions:
            slot = counts.get(place, 0)
            counts[place] = slot + 1

            @pl.when((head == 0) & (position == place))
            def _():
                pltpu.make_async_copy(source_ref, slots.at[slot], arrived.at[slot]).start()

    out_ref[...] = total_ref[...]
    count = sum(jnp.where(position == place, number, 0) for place, number in counts.items())
    low = pl.multiple_of((skipped + head) * head_size, head_size)
    key_columns = pl.ds(low, head_size)
    value_columns = pl.ds(pl.multiple_of(slots.shape[2] // 2 + low, head_size), head_size)

    @pl.loop(0, count)
    def _(slot):
        @pl.when(head == 0)
        def _():
            pltpu.make_async_copy(source_refs[0], slots.at[slot], arrived.at[slot]).wait()

        def add_rows(step):
            rows = pl.ds(pl.multiple_of(step * tile, tile), tile)
            logits = dot_nt(q_ref[rows, :], slots[slot, :, key_columns])
            weights = silu_weights(logits, score_scale).astype(jnp.bfloat16)
            out_ref[rows, :] += jnp.dot(
                weights, slots[slot, :, value_columns], preferred_element_type=jnp.float32
            )

        if unrolled:
            for step in range(row_count // tile):
                add_rows(step)
        else:
            pl.loop(0, row_count // tile)(add_rows)


def add_sources(place, projected, totals, sources, first_head, skipped, heads, unrolled):
    row_count, width = projected.shape
    model_width = width // 4
    head_size = model_width // HEADS
    arrays = [array for array, _ in sources]
    holders = [positions for _, positions in sources]
    everyone = [position for positions in holders for position in positions]
    most = max(everyone.count(position) for position in everyone)
    first_head += skipped
    total_spec = pl.BlockSpec((row_count, head_size), lambda head, place: (0, first_head + head))
    return pl.pallas_call(
        functools.partial(add_kernel, head_size ** (-0.5), holders, skipped, unrolled),
        out_shape=jax.ShapeDtypeStruct(totals.shape, totals.dtype),
        grid_spec=pltpu.PrefetchScalarGridSpec(
            num_scalar_prefetch=1,
            grid=(heads,),
            in_specs=[
                pl.BlockSpec((row_count, head_size), lambda head, place: (0, HEADS + first_head + head)),
                *[pl.BlockSpec(memory_space=pl.ANY)] * len(arrays),
                total_spec,
            ],
            out_specs=total_spec,
            scratch_shapes=[
                pltpu.VMEM((most, *arrays[0].shape), projected.dtype),
                pltpu.SemaphoreType.DMA((most,)),
            ],
        ),
        input_output_aliases={2 + len(arrays): 0},
        compiler_params=pltpu.CompilerParams(vmem_limit_bytes=VMEM_LIMIT),
        cost_estimate=pl.CostEstimate(
            flops=COST_SCALE * 4 * row_count * row_count * heads * head_size * most,
            bytes_accessed=(6 + 4 * most) * row_count * heads * head_size,
            transcendentals=row_count * row_count * heads * most,
        ),
    )(place, projected, *arrays, totals)


def pack_kernel(projected_ref, *refs):
    count = (len(refs) - 2) // 2
    packed_refs, held_refs, (loaded, stored) = refs[:count], refs[count:-2], refs[-2:]
    model_width = projected_ref.shape[1] // 4
    low, loads, stores = 0, [], []
    for packed_ref, held_ref in zip(packed_refs, held_refs):
        width = packed_ref.shape[1] // 2
        for part in range(2):
            source = projected_ref.at[:, pl.ds((2 + part) * model_width + low, width)]
            held = held_ref.at[:, pl.ds(part * width, width)]
            target = packed_ref.at[:, pl.ds(part * width, width)]
            loads.append(pltpu.make_async_copy(source, held, loaded.at[len(loads)]))
            stores.append(pltpu.make_async_copy(held, target, stored.at[len(stores)]))
        low += width
    for load in loads:
        load.start()
    for load, store in zip(loads, stores):
        load.wait()
        store.start()
    for store in stores:
        store.wait()


def pack_key_values(projected, parts):
    row_count, width = projected.shape
    anywhere = pl.BlockSpec(memory_space=pl.ANY)
    shapes = [(row_count, heads * width // (2 * HEADS)) for heads in parts]
    return pl.pallas_call(
        pack_kernel,
        out_shape=[jax.ShapeDtypeStruct(shape, projected.dtype) for shape in shapes],
        in_specs=[anywhere],
        out_specs=[anywhere] * len(parts),
        scratch_shapes=[
            *[pltpu.VMEM(shape, projected.dtype) for shape in shapes],
            *[pltpu.SemaphoreType.DMA((2 * len(parts),))] * 2,
        ],
        compiler_params=pltpu.CompilerParams(vmem_limit_bytes=VMEM_LIMIT),
        cost_estimate=pl.CostEstimate(
            flops=0, bytes_accessed=2 * row_count * width, transcendentals=0
        ),
    )(projected)


def tie_kernel(array_ref, after_ref, out_ref):
    pass


def tie(array, after):
    anywhere = pl.BlockSpec(memory_space=pl.ANY)
    return pl.pallas_call(
        tie_kernel,
        out_shape=jax.ShapeDtypeStruct(array.shape, array.dtype),
        in_specs=[anywhere, anywhere],
        out_specs=anywhere,
        input_output_aliases={0: 0},
    )(array, after)


def group_attention(span, residue, peers, place, projected):
    if span == 1:
        return own_attention(projected)
    period = 2 if span == 2 else SPAN

    def send(array, *hops):
        pairs = []
        for position, target in hops:
            lowest, by = (residue + position) % period, target - position
            pairs += [(s, s + by) for s in range(lowest, peers, period) if s + by < peers]
        return lax.ppermute(array, "seq", pairs)

    def swap(array, position):
        lowest = (residue + position) % period
        pairs = [(s, s + 1) for s in range(lowest, peers, period) if s + 1 < peers]
        return lax.ppermute(array, "seq", pairs + [(b, a) for a, b in pairs])

    chips = {}
    for position in range(span):
        chips.setdefault((residue + position) // 2, []).append(position)
    chips = list(chips.values())
    inner = [tuple(chip) for chip in chips if len(chip) == 2]

    def exchange(mine, after):
        if span == 2:
            return [(send(mine, (0, 1)), [1])]
        if span == 3 and len(chips[0]) == 2:
            return [(send(mine, (0, 2)), [2]), (send(mine, (1, 2)), [2])]
        if span == 3:
            came = tie(send(mine, (0, 2)), after)
            return [(came, [2]), (swap(came, 1), [1])]
        came = send(mine, (0, 2), (1, 3))
        if len(chips) == 2:
            came = tie(came, after)
            return [(came, [2, 3]), (swap(came, 2), [2, 3])]
        found = [(send(mine, (2, 3)), [3])]
        came = tie(came, after)
        return [(came, [2, 3]), (swap(came, 1), [1]), *found]

    if span == 2 or (span == 3 and len(chips[0]) == 1):
        (mine,) = pack_key_values(projected, (HEADS,))
        totals = own_attention(projected)
        found = exchange(mine, totals)
        if span == 3:
            found.append((send(mine, *inner), [2]))
        return add_sources(place, projected, totals, found, 0, 0, HEADS, False)
    early, late = CHUNK_PARTS
    mine, rest = pack_key_values(projected, CHUNK_PARTS)
    totals = own_attention(projected)
    hops = inner if len(chips) == 2 else [(0, 3), (1, 2)]
    holders = [target for _, target in hops]
    first, second = [(send(mine, *hops), holders)], [(send(rest, *hops), holders)]
    totals = add_sources(place, projected, totals, first, 0, 0, early, False)
    found = exchange(mine, totals)
    totals = add_sources(place, projected, totals, second, early, 0, late, False)
    totals = add_sources(place, projected, totals, found, 0, 0, early, False)
    more = exchange(rest, totals)
    return add_sources(place, projected, totals, more, early, 0, late, True)


def finish_kernel(place_ref, total_ref, u_ref, history_ref, gain_ref, weight_ref, out_ref, last_ref):
    step = pl.program_id(0)
    tile = total_ref.shape[0]
    row_count = tile * pl.num_programs(0)
    span, position, tail = place_ref[0], place_ref[2], place_ref[3]
    valid = jnp.where(position == span - 1, tail, row_count)
    row_ids = step * tile + lax.broadcasted_iota(jnp.int32, (tile, 1), 0)
    attention = jnp.where(row_ids < valid, total_ref[...], 0.0)
    row_mean = jnp.mean(attention, axis=1, keepdims=True)
    centered = attention - row_mean
    row_var = jnp.mean(centered * centered, axis=1, keepdims=True)
    normed = centered * lax.rsqrt(row_var + 1e-06) * gain_ref[...]
    gated = (normed * u_ref[...].astype(jnp.float32)).astype(jnp.bfloat16)
    out = jnp.dot(gated, weight_ref[...], preferred_element_type=jnp.float32)
    out = (out + history_ref[...].astype(jnp.float32)).astype(jnp.bfloat16)
    out_ref[...] = out

    @pl.when(valid - 1 - step * tile == jnp.clip(valid - 1 - step * tile, 0, tile - 1))
    def _():
        final = jnp.where(row_ids == valid - 1, out.astype(jnp.float32), 0.0)
        last_ref[...] = jnp.sum(final, axis=0, keepdims=True)


def finish(place, totals, projected, history_in, norm_gain, out_proj):
    row_count, model_width = history_in.shape
    tile = row_tile(row_count)
    rows = pl.BlockSpec((tile, model_width), lambda step, place: (step, 0))
    whole = pl.BlockSpec((1, model_width), lambda step, place: (0, 0))
    return pl.pallas_call(
        finish_kernel,
        out_shape=(
            jax.ShapeDtypeStruct(history_in.shape, history_in.dtype),
            jax.ShapeDtypeStruct((1, model_width), jnp.float32),
        ),
        grid_spec=pltpu.PrefetchScalarGridSpec(
            num_scalar_prefetch=1,
            grid=(row_count // tile,),
            in_specs=[
                rows,
                rows,
                rows,
                whole,
                pl.BlockSpec(out_proj.shape, lambda step, place: (0, 0)),
            ],
            out_specs=(rows, whole),
        ),
        compiler_params=pltpu.CompilerParams(vmem_limit_bytes=VMEM_LIMIT),
        cost_estimate=pl.CostEstimate(
            flops=2 * row_count * model_width * model_width,
            bytes_accessed=10 * row_count * model_width + 2 * model_width * model_width,
            transcendentals=row_count,
        ),
    )(place, totals, projected, history_in, norm_gain.reshape(1, -1), out_proj)


def score_kernel(last_ref, rows_ref, user_ref, cand_ref, down_ref, up_ref, bias_ref, weight_ref, out_ref):
    peers, model_width = rows_ref.shape
    cand_count = cand_ref.shape[0]
    cand_user = user_ref[...]

    def visit(user, found):
        return jnp.where(cand_user == user, last_ref[user], found)

    cand_dev = lax.fori_loop(0, last_ref.shape[0], visit, jnp.zeros_like(cand_user))
    device_ids = lax.broadcasted_iota(jnp.int32, (peers, cand_count), 0)
    selector = jnp.where(device_ids == cand_dev, 1.0, 0.0).astype(jnp.bfloat16)
    user_part = lax.dot_general(
        selector,
        rows_ref[...].astype(jnp.bfloat16),
        (((0,), (0,)), ((), ())),
        preferred_element_type=jnp.float32,
    ).astype(jnp.bfloat16)
    cand_part = cand_ref[...]
    low_rank = jnp.dot(user_part, down_ref[:model_width, :], preferred_element_type=jnp.float32)
    low_rank += jnp.dot(cand_part, down_ref[model_width:, :], preferred_element_type=jnp.float32)
    low_rank = low_rank.astype(jnp.bfloat16)
    score = jnp.zeros((cand_count, 1), jnp.float32)
    for part, low in ((user_part, 0), (cand_part, model_width)):
        cut = slice(low, low + model_width)
        up_part = jnp.dot(low_rank, up_ref[:, cut], preferred_element_type=jnp.float32)
        value = part.astype(jnp.float32)
        crossed = value * (up_part + bias_ref[:, cut]) + value
        score += jnp.sum(crossed * weight_ref[:, cut], axis=1, keepdims=True)
    row_ids = lax.broadcasted_iota(jnp.int32, (cand_count, cand_count), 0)
    column_ids = lax.broadcasted_iota(jnp.int32, (cand_count, cand_count), 1)
    out_ref[...] = jnp.sum(jnp.where(row_ids == column_ids, score, 0.0), axis=0, keepdims=True)


def score(last_dev, user_rows, cand_user, cand_emb, cross_down, cross_up, cross_bias, score_weight):
    vmem = pl.BlockSpec(memory_space=pltpu.VMEM)
    cand_count = cand_emb.shape[0]
    scores = pl.pallas_call(
        score_kernel,
        out_shape=jax.ShapeDtypeStruct((1, cand_count), jnp.float32),
        in_specs=[pl.BlockSpec(memory_space=pltpu.SMEM)] + [vmem] * 7,
        out_specs=vmem,
        compiler_params=pltpu.CompilerParams(vmem_limit_bytes=VMEM_LIMIT),
    )(
        last_dev,
        user_rows,
        cand_user.reshape(1, -1),
        cand_emb,
        cross_down,
        cross_up,
        cross_bias.reshape(1, -1),
        score_weight.reshape(1, -1),
    )
    return scores.reshape(-1)


def body(
    projected,
    history_in,
    norm_gain,
    out_proj,
    user_spans,
    user_tails,
    cand_emb,
    cand_user,
    cross_down,
    cross_up,
    cross_bias,
    score_weight,
):
    peers = lax.axis_size("seq")
    place, last_dev = find_place(lax.axis_index("seq"), user_spans, user_tails)
    branches = [
        functools.partial(group_attention, span, residue, peers) for span, residue in KINDS
    ]
    totals = lax.switch(place[4], branches, place, projected)
    history_out, final_row = finish(place, totals, projected, history_in, norm_gain, out_proj)
    user_rows = lax.all_gather(final_row, "seq", axis=0, tiled=True)
    scores = score(
        last_dev, user_rows, cand_user, cand_emb, cross_down, cross_up, cross_bias, score_weight
    )
    return (history_out, scores)


def solution(mesh):
    in_specs = (
        P(("rep", "seq"), None),
        P(("rep", "seq"), None),
        P(),
        P(),
        P("rep"),
        P("rep"),
        P(("rep", "seq"), None),
        P(("rep", "seq")),
        P(),
        P(),
        P(),
        P(),
    )
    out_specs = (P(("rep", "seq"), None), P(("rep", "seq")))
    return jax.shard_map(body, mesh=mesh, in_specs=in_specs, out_specs=out_specs, check_vma=False)
```

```python
import functools

import jax
import jax.numpy as jnp
from jax import lax
from jax.experimental import pallas as pl
from jax.experimental.pallas import tpu as pltpu
from jax.sharding import PartitionSpec as P

HEADS = 8
SPAN = 4
CHUNK_PARTS = (5, 3)
COST_SCALE = 5
KINDS = (
    (1, 0),
    (2, 0),
    (2, 1),
    *((3, residue) for residue in range(SPAN)),
    *((4, residue) for residue in range(SPAN)),
)
VMEM_LIMIT = 63 * 1024 * 1024


def silu_weights(logits, score_scale):
    half = logits * (0.5 * score_scale)
    return half + half * jnp.tanh(half)


def row_tile(row_count):
    return 256 if row_count % 256 == 0 else row_count


def dot_nt(left, right):
    return lax.dot_general(left, right, (((1,), (1,)), ((), ())), preferred_element_type=jnp.float32)


def place_kernel(me_ref, spans_ref, tails_ref, place_ref, last_ref):
    users = spans_ref.shape[0]
    me = me_ref[0]

    def visit(user, state):
        begin, span, start, tail = state
        end = begin + spans_ref[user]
        mine = (begin <= me) & (me < end)
        last_ref[user] = end - 1
        return (
            end,
            jnp.where(mine, spans_ref[user], span),
            jnp.where(mine, begin, start),
            jnp.where(mine, tails_ref[user], tail),
        )

    zero = jnp.int32(0)
    _, span, start, tail = lax.fori_loop(0, users, visit, (zero, zero + 1, zero, zero))
    place_ref[0] = span
    place_ref[1] = start
    place_ref[2] = me - start
    place_ref[3] = tail
    kind = jnp.int32(0)
    for index, (its_span, residue) in enumerate(KINDS):
        period = 2 if its_span == 2 else SPAN
        fits = (span == its_span) & (lax.rem(start, period) == residue)
        kind = jnp.where(fits, index, kind)
    place_ref[4] = kind


def find_place(me, user_spans, user_tails):
    smem = pl.BlockSpec(memory_space=pltpu.SMEM)
    return pl.pallas_call(
        place_kernel,
        out_shape=(
            jax.ShapeDtypeStruct((8,), jnp.int32),
            jax.ShapeDtypeStruct(user_spans.shape, jnp.int32),
        ),
        in_specs=[smem] * 3,
        out_specs=(smem, smem),
    )(me.reshape(1), user_spans, user_tails)


def own_kernel(score_scale, q_ref, k_ref, v_ref, out_ref):
    row_count = q_ref.shape[0]
    tile = row_tile(row_count)

    @pl.loop(0, row_count // tile)
    def _(step):
        rows = pl.ds(pl.multiple_of(step * tile, tile), tile)
        weights = silu_weights(dot_nt(q_ref[rows, :], k_ref[...]), score_scale)
        row_ids = step * tile + lax.broadcasted_iota(jnp.int32, weights.shape, 0)
        key_ids = lax.broadcasted_iota(jnp.int32, weights.shape, 1)
        weights = jnp.where(key_ids <= row_ids, weights, 0.0).astype(jnp.bfloat16)
        out_ref[rows, :] = jnp.dot(weights, v_ref[...], preferred_element_type=jnp.float32)


def own_attention(projected):
    row_count, width = projected.shape
    model_width = width // 4
    head_size = model_width // HEADS

    def columns(part):
        return pl.BlockSpec((row_count, head_size), lambda head: (0, part * HEADS + head))

    return pl.pallas_call(
        functools.partial(own_kernel, head_size ** (-0.5)),
        out_shape=jax.ShapeDtypeStruct((row_count, model_width), jnp.float32),
        grid=(HEADS,),
        in_specs=[columns(1), columns(2), columns(3)],
        out_specs=pl.BlockSpec((row_count, head_size), lambda head: (0, head)),
        compiler_params=pltpu.CompilerParams(vmem_limit_bytes=VMEM_LIMIT),
        cost_estimate=pl.CostEstimate(
            flops=COST_SCALE * 3 * row_count * row_count * model_width,
            bytes_accessed=10 * row_count * model_width,
            transcendentals=row_count * row_count * HEADS,
        ),
    )(projected, projected, projected)


def add_kernel(score_scale, holders, skipped, unrolled, place_ref, q_ref, *refs):
    source_refs, (total_ref, out_ref, slots, arrived) = refs[: len(holders)], refs[-4:]
    head, position = pl.program_id(0), place_ref[2]
    row_count, head_size = q_ref.shape
    tile = row_tile(row_count)
    counts = {}
    for source_ref, positions in zip(source_refs, holders):
        for place in positions:
            slot = counts.get(place, 0)
            counts[place] = slot + 1

            @pl.when((head == 0) & (position == place))
            def _():
                pltpu.make_async_copy(source_ref, slots.at[slot], arrived.at[slot]).start()

    out_ref[...] = total_ref[...]
    count = sum(jnp.where(position == place, number, 0) for place, number in counts.items())
    low = pl.multiple_of((skipped + head) * head_size, head_size)
    key_columns = pl.ds(low, head_size)
    value_columns = pl.ds(pl.multiple_of(slots.shape[2] // 2 + low, head_size), head_size)

    @pl.loop(0, count)
    def _(slot):
        @pl.when(head == 0)
        def _():
            pltpu.make_async_copy(source_refs[0], slots.at[slot], arrived.at[slot]).wait()

        def add_rows(step):
            rows = pl.ds(pl.multiple_of(step * tile, tile), tile)
            logits = dot_nt(q_ref[rows, :], slots[slot, :, key_columns])
            weights = silu_weights(logits, score_scale).astype(jnp.bfloat16)
            out_ref[rows, :] += jnp.dot(
                weights, slots[slot, :, value_columns], preferred_element_type=jnp.float32
            )

        if unrolled:
            for step in range(row_count // tile):
                add_rows(step)
        else:
            pl.loop(0, row_count // tile)(add_rows)


def add_sources(place, projected, totals, sources, first_head, skipped, heads, unrolled):
    row_count, width = projected.shape
    model_width = width // 4
    head_size = model_width // HEADS
    arrays = [array for array, _ in sources]
    holders = [positions for _, positions in sources]
    everyone = [position for positions in holders for position in positions]
    most = max(everyone.count(position) for position in everyone)
    first_head += skipped
    total_spec = pl.BlockSpec((row_count, head_size), lambda head, place: (0, first_head + head))
    return pl.pallas_call(
        functools.partial(add_kernel, head_size ** (-0.5), holders, skipped, unrolled),
        out_shape=jax.ShapeDtypeStruct(totals.shape, totals.dtype),
        grid_spec=pltpu.PrefetchScalarGridSpec(
            num_scalar_prefetch=1,
            grid=(heads,),
            in_specs=[
                pl.BlockSpec((row_count, head_size), lambda head, place: (0, HEADS + first_head + head)),
                *[pl.BlockSpec(memory_space=pl.ANY)] * len(arrays),
                total_spec,
            ],
            out_specs=total_spec,
            scratch_shapes=[
                pltpu.VMEM((most, *arrays[0].shape), projected.dtype),
                pltpu.SemaphoreType.DMA((most,)),
            ],
        ),
        input_output_aliases={2 + len(arrays): 0},
        compiler_params=pltpu.CompilerParams(vmem_limit_bytes=VMEM_LIMIT),
        cost_estimate=pl.CostEstimate(
            flops=COST_SCALE * 4 * row_count * row_count * heads * head_size * most,
            bytes_accessed=(6 + 4 * most) * row_count * heads * head_size,
            transcendentals=row_count * row_count * heads * most,
        ),
    )(place, projected, *arrays, totals)


def pack_kernel(projected_ref, *refs):
    count = (len(refs) - 2) // 2
    packed_refs, held_refs, (loaded, stored) = refs[:count], refs[count:-2], refs[-2:]
    model_width = projected_ref.shape[1] // 4
    low, loads, stores = 0, [], []
    for packed_ref, held_ref in zip(packed_refs, held_refs):
        width = packed_ref.shape[1] // 2
        for part in range(2):
            source = projected_ref.at[:, pl.ds((2 + part) * model_width + low, width)]
            held = held_ref.at[:, pl.ds(part * width, width)]
            target = packed_ref.at[:, pl.ds(part * width, width)]
            loads.append(pltpu.make_async_copy(source, held, loaded.at[len(loads)]))
            stores.append(pltpu.make_async_copy(held, target, stored.at[len(stores)]))
        low += width
    for load in loads:
        load.start()
    for load, store in zip(loads, stores):
        load.wait()
        store.start()
    for store in stores:
        store.wait()


def pack_key_values(projected, parts):
    row_count, width = projected.shape
    anywhere = pl.BlockSpec(memory_space=pl.ANY)
    shapes = [(row_count, heads * width // (2 * HEADS)) for heads in parts]
    return pl.pallas_call(
        pack_kernel,
        out_shape=[jax.ShapeDtypeStruct(shape, projected.dtype) for shape in shapes],
        in_specs=[anywhere],
        out_specs=[anywhere] * len(parts),
        scratch_shapes=[
            *[pltpu.VMEM(shape, projected.dtype) for shape in shapes],
            *[pltpu.SemaphoreType.DMA((2 * len(parts),))] * 2,
        ],
        compiler_params=pltpu.CompilerParams(vmem_limit_bytes=VMEM_LIMIT),
        cost_estimate=pl.CostEstimate(
            flops=0, bytes_accessed=2 * row_count * width, transcendentals=0
        ),
    )(projected)


def tie_kernel(array_ref, after_ref, out_ref):
    pass


def tie(array, after):
    anywhere = pl.BlockSpec(memory_space=pl.ANY)
    return pl.pallas_call(
        tie_kernel,
        out_shape=jax.ShapeDtypeStruct(array.shape, array.dtype),
        in_specs=[anywhere, anywhere],
        out_specs=anywhere,
        input_output_aliases={0: 0},
    )(array, after)


def group_attention(span, residue, peers, place, projected):
    if span == 1:
        return own_attention(projected)
    period = 2 if span == 2 else SPAN

    def send(array, *hops):
        pairs = []
        for position, target in hops:
            lowest, by = (residue + position) % period, target - position
            pairs += [(s, s + by) for s in range(lowest, peers, period) if s + by < peers]
        return lax.ppermute(array, "seq", pairs)

    def swap(array, position):
        lowest = (residue + position) % period
        pairs = [(s, s + 1) for s in range(lowest, peers, period) if s + 1 < peers]
        return lax.ppermute(array, "seq", pairs + [(b, a) for a, b in pairs])

    chips = {}
    for position in range(span):
        chips.setdefault((residue + position) // 2, []).append(position)
    chips = list(chips.values())
    inner = [tuple(chip) for chip in chips if len(chip) == 2]

    def exchange(mine, after):
        if span == 2:
            return [(send(mine, (0, 1)), [1])]
        if span == 3 and len(chips[0]) == 2:
            return [(send(mine, (0, 2)), [2]), (send(mine, (1, 2)), [2]), (send(mine, *inner), [1])]
        if span == 3:
            came = tie(send(mine, (0, 2)), after)
            return [(came, [2]), (swap(came, 1), [1])]
        came = send(mine, (0, 2), (1, 3))
        if len(chips) == 2:
            came = tie(came, after)
            return [(came, [2, 3]), (swap(came, 2), [2, 3])]
        found = [(send(mine, (2, 3)), [3])]
        came = tie(came, after)
        return [(came, [2, 3]), (swap(came, 1), [1]), *found]

    if span == 2 or (span == 3 and len(chips[0]) == 1):
        (mine,) = pack_key_values(projected, (HEADS,))
        totals = own_attention(projected)
        found = exchange(mine, totals)
        if span == 3:
            found.append((send(mine, *inner), [2]))
        return add_sources(place, projected, totals, found, 0, 0, HEADS, False)
    early, late = CHUNK_PARTS
    mine, rest = pack_key_values(projected, CHUNK_PARTS)
    totals = own_attention(projected)
    if span == 3:
        found, more = exchange(mine, totals), exchange(rest, totals)
        totals = add_sources(place, projected, totals, found, 0, 0, early, False)
        return add_sources(place, projected, totals, more, early, 0, late, False)
    hops = inner if len(chips) == 2 else [(0, 3), (1, 2)]
    holders = [target for _, target in hops]
    first, second = [(send(mine, *hops), holders)], [(send(rest, *hops), holders)]
    totals = add_sources(place, projected, totals, first, 0, 0, early, False)
    found = exchange(mine, totals)
    totals = add_sources(place, projected, totals, second, early, 0, late, False)
    totals = add_sources(place, projected, totals, found, 0, 0, early, False)
    more = exchange(rest, totals)
    return add_sources(place, projected, totals, more, early, 0, late, False)


def finish_kernel(place_ref, total_ref, u_ref, history_ref, gain_ref, weight_ref, out_ref, last_ref):
    step = pl.program_id(0)
    tile = total_ref.shape[0]
    row_count = tile * pl.num_programs(0)
    span, position, tail = place_ref[0], place_ref[2], place_ref[3]
    valid = jnp.where(position == span - 1, tail, row_count)
    row_ids = step * tile + lax.broadcasted_iota(jnp.int32, (tile, 1), 0)
    attention = jnp.where(row_ids < valid, total_ref[...], 0.0)
    row_mean = jnp.mean(attention, axis=1, keepdims=True)
    centered = attention - row_mean
    row_var = jnp.mean(centered * centered, axis=1, keepdims=True)
    normed = centered * lax.rsqrt(row_var + 1e-06) * gain_ref[...]
    gated = (normed * u_ref[...].astype(jnp.float32)).astype(jnp.bfloat16)
    out = jnp.dot(gated, weight_ref[...], preferred_element_type=jnp.float32)
    out = (out + history_ref[...].astype(jnp.float32)).astype(jnp.bfloat16)
    out_ref[...] = out

    @pl.when(valid - 1 - step * tile == jnp.clip(valid - 1 - step * tile, 0, tile - 1))
    def _():
        final = jnp.where(row_ids == valid - 1, out.astype(jnp.float32), 0.0)
        last_ref[...] = jnp.sum(final, axis=0, keepdims=True)


def finish(place, totals, projected, history_in, norm_gain, out_proj):
    row_count, model_width = history_in.shape
    tile = row_tile(row_count)
    rows = pl.BlockSpec((tile, model_width), lambda step, place: (step, 0))
    whole = pl.BlockSpec((1, model_width), lambda step, place: (0, 0))
    return pl.pallas_call(
        finish_kernel,
        out_shape=(
            jax.ShapeDtypeStruct(history_in.shape, history_in.dtype),
            jax.ShapeDtypeStruct((1, model_width), jnp.float32),
        ),
        grid_spec=pltpu.PrefetchScalarGridSpec(
            num_scalar_prefetch=1,
            grid=(row_count // tile,),
            in_specs=[
                rows,
                rows,
                rows,
                whole,
                pl.BlockSpec(out_proj.shape, lambda step, place: (0, 0)),
            ],
            out_specs=(rows, whole),
        ),
        compiler_params=pltpu.CompilerParams(vmem_limit_bytes=VMEM_LIMIT),
        cost_estimate=pl.CostEstimate(
            flops=2 * row_count * model_width * model_width,
            bytes_accessed=10 * row_count * model_width + 2 * model_width * model_width,
            transcendentals=row_count,
        ),
    )(place, totals, projected, history_in, norm_gain.reshape(1, -1), out_proj)


def score_kernel(last_ref, rows_ref, user_ref, cand_ref, down_ref, up_ref, bias_ref, weight_ref, out_ref):
    peers, model_width = rows_ref.shape
    cand_count = cand_ref.shape[0]
    cand_user = user_ref[...]

    def visit(user, found):
        return jnp.where(cand_user == user, last_ref[user], found)

    cand_dev = lax.fori_loop(0, last_ref.shape[0], visit, jnp.zeros_like(cand_user))
    device_ids = lax.broadcasted_iota(jnp.int32, (peers, cand_count), 0)
    selector = jnp.where(device_ids == cand_dev, 1.0, 0.0).astype(jnp.bfloat16)
    user_part = lax.dot_general(
        selector,
        rows_ref[...].astype(jnp.bfloat16),
        (((0,), (0,)), ((), ())),
        preferred_element_type=jnp.float32,
    ).astype(jnp.bfloat16)
    cand_part = cand_ref[...]
    low_rank = jnp.dot(user_part, down_ref[:model_width, :], preferred_element_type=jnp.float32)
    low_rank += jnp.dot(cand_part, down_ref[model_width:, :], preferred_element_type=jnp.float32)
    low_rank = low_rank.astype(jnp.bfloat16)
    score = jnp.zeros((cand_count, 1), jnp.float32)
    for part, low in ((user_part, 0), (cand_part, model_width)):
        cut = slice(low, low + model_width)
        up_part = jnp.dot(low_rank, up_ref[:, cut], preferred_element_type=jnp.float32)
        value = part.astype(jnp.float32)
        crossed = value * (up_part + bias_ref[:, cut]) + value
        score += jnp.sum(crossed * weight_ref[:, cut], axis=1, keepdims=True)
    row_ids = lax.broadcasted_iota(jnp.int32, (cand_count, cand_count), 0)
    column_ids = lax.broadcasted_iota(jnp.int32, (cand_count, cand_count), 1)
    out_ref[...] = jnp.sum(jnp.where(row_ids == column_ids, score, 0.0), axis=0, keepdims=True)


def score(last_dev, user_rows, cand_user, cand_emb, cross_down, cross_up, cross_bias, score_weight):
    vmem = pl.BlockSpec(memory_space=pltpu.VMEM)
    cand_count = cand_emb.shape[0]
    scores = pl.pallas_call(
        score_kernel,
        out_shape=jax.ShapeDtypeStruct((1, cand_count), jnp.float32),
        in_specs=[pl.BlockSpec(memory_space=pltpu.SMEM)] + [vmem] * 7,
        out_specs=vmem,
        compiler_params=pltpu.CompilerParams(vmem_limit_bytes=VMEM_LIMIT),
    )(
        last_dev,
        user_rows,
        cand_user.reshape(1, -1),
        cand_emb,
        cross_down,
        cross_up,
        cross_bias.reshape(1, -1),
        score_weight.reshape(1, -1),
    )
    return scores.reshape(-1)


def body(
    projected,
    history_in,
    norm_gain,
    out_proj,
    user_spans,
    user_tails,
    cand_emb,
    cand_user,
    cross_down,
    cross_up,
    cross_bias,
    score_weight,
):
    peers = lax.axis_size("seq")
    place, last_dev = find_place(lax.axis_index("seq"), user_spans, user_tails)
    branches = [
        functools.partial(group_attention, span, residue, peers) for span, residue in KINDS
    ]
    totals = lax.switch(place[4], branches, place, projected)
    history_out, final_row = finish(place, totals, projected, history_in, norm_gain, out_proj)
    user_rows = lax.all_gather(final_row, "seq", axis=0, tiled=True)
    scores = score(
        last_dev, user_rows, cand_user, cand_emb, cross_down, cross_up, cross_bias, score_weight
    )
    return (history_out, scores)


def solution(mesh):
    in_specs = (
        P(("rep", "seq"), None),
        P(("rep", "seq"), None),
        P(),
        P(),
        P("rep"),
        P("rep"),
        P(("rep", "seq"), None),
        P(("rep", "seq")),
        P(),
        P(),
        P(),
        P(),
    )
    out_specs = (P(("rep", "seq"), None), P(("rep", "seq")))
    return jax.shard_map(body, mesh=mesh, in_specs=in_specs, out_specs=out_specs, check_vma=False)
```

```python
import functools

import jax
import jax.numpy as jnp
from jax import lax
from jax.experimental import pallas as pl
from jax.experimental.pallas import tpu as pltpu
from jax.sharding import PartitionSpec as P

HEADS = 8
SPAN = 4
CHUNK_PARTS = (5, 3)
COST_SCALE = 5
KINDS = (
    (1, 0),
    (2, 0),
    (2, 1),
    *((3, residue) for residue in range(SPAN)),
    *((4, residue) for residue in range(SPAN)),
)
VMEM_LIMIT = 63 * 1024 * 1024


def silu_weights(logits, score_scale):
    half = logits * (0.5 * score_scale)
    return half + half * jnp.tanh(half)


def row_tile(row_count):
    return 256 if row_count % 256 == 0 else row_count


def dot_nt(left, right):
    return lax.dot_general(left, right, (((1,), (1,)), ((), ())), preferred_element_type=jnp.float32)


def place_kernel(me_ref, spans_ref, tails_ref, place_ref, last_ref):
    users = spans_ref.shape[0]
    me = me_ref[0]

    def visit(user, state):
        begin, span, start, tail = state
        end = begin + spans_ref[user]
        mine = (begin <= me) & (me < end)
        last_ref[user] = end - 1
        return (
            end,
            jnp.where(mine, spans_ref[user], span),
            jnp.where(mine, begin, start),
            jnp.where(mine, tails_ref[user], tail),
        )

    zero = jnp.int32(0)
    _, span, start, tail = lax.fori_loop(0, users, visit, (zero, zero + 1, zero, zero))
    place_ref[0] = span
    place_ref[1] = start
    place_ref[2] = me - start
    place_ref[3] = tail
    kind = jnp.int32(0)
    for index, (its_span, residue) in enumerate(KINDS):
        period = 2 if its_span == 2 else SPAN
        fits = (span == its_span) & (lax.rem(start, period) == residue)
        kind = jnp.where(fits, index, kind)
    place_ref[4] = kind


def find_place(me, user_spans, user_tails):
    smem = pl.BlockSpec(memory_space=pltpu.SMEM)
    return pl.pallas_call(
        place_kernel,
        out_shape=(
            jax.ShapeDtypeStruct((8,), jnp.int32),
            jax.ShapeDtypeStruct(user_spans.shape, jnp.int32),
        ),
        in_specs=[smem] * 3,
        out_specs=(smem, smem),
    )(me.reshape(1), user_spans, user_tails)


def own_kernel(score_scale, q_ref, k_ref, v_ref, out_ref):
    row_count = q_ref.shape[0]
    tile = row_tile(row_count)

    @pl.loop(0, row_count // tile)
    def _(step):
        rows = pl.ds(pl.multiple_of(step * tile, tile), tile)
        weights = silu_weights(dot_nt(q_ref[rows, :], k_ref[...]), score_scale)
        row_ids = step * tile + lax.broadcasted_iota(jnp.int32, weights.shape, 0)
        key_ids = lax.broadcasted_iota(jnp.int32, weights.shape, 1)
        weights = jnp.where(key_ids <= row_ids, weights, 0.0).astype(jnp.bfloat16)
        out_ref[rows, :] = jnp.dot(weights, v_ref[...], preferred_element_type=jnp.float32)


def own_attention(projected):
    row_count, width = projected.shape
    model_width = width // 4
    head_size = model_width // HEADS

    def columns(part):
        return pl.BlockSpec((row_count, head_size), lambda head: (0, part * HEADS + head))

    return pl.pallas_call(
        functools.partial(own_kernel, head_size ** (-0.5)),
        out_shape=jax.ShapeDtypeStruct((row_count, model_width), jnp.float32),
        grid=(HEADS,),
        in_specs=[columns(1), columns(2), columns(3)],
        out_specs=pl.BlockSpec((row_count, head_size), lambda head: (0, head)),
        compiler_params=pltpu.CompilerParams(vmem_limit_bytes=VMEM_LIMIT),
        cost_estimate=pl.CostEstimate(
            flops=COST_SCALE * 3 * row_count * row_count * model_width,
            bytes_accessed=10 * row_count * model_width,
            transcendentals=row_count * row_count * HEADS,
        ),
    )(projected, projected, projected)


def add_kernel(score_scale, holders, skipped, unrolled, place_ref, q_ref, *refs):
    source_refs, (total_ref, out_ref, slots, arrived) = refs[: len(holders)], refs[-4:]
    head, position = pl.program_id(0), place_ref[2]
    row_count, head_size = q_ref.shape
    tile = row_tile(row_count)
    counts = {}
    for source_ref, positions in zip(source_refs, holders):
        for place in positions:
            slot = counts.get(place, 0)
            counts[place] = slot + 1

            @pl.when((head == 0) & (position == place))
            def _():
                pltpu.make_async_copy(source_ref, slots.at[slot], arrived.at[slot]).start()

    out_ref[...] = total_ref[...]
    count = sum(jnp.where(position == place, number, 0) for place, number in counts.items())
    low = pl.multiple_of((skipped + head) * head_size, head_size)
    key_columns = pl.ds(low, head_size)
    value_columns = pl.ds(pl.multiple_of(slots.shape[2] // 2 + low, head_size), head_size)

    @pl.loop(0, count)
    def _(slot):
        @pl.when(head == 0)
        def _():
            pltpu.make_async_copy(source_refs[0], slots.at[slot], arrived.at[slot]).wait()

        def add_rows(step):
            rows = pl.ds(pl.multiple_of(step * tile, tile), tile)
            logits = dot_nt(q_ref[rows, :], slots[slot, :, key_columns])
            weights = silu_weights(logits, score_scale).astype(jnp.bfloat16)
            out_ref[rows, :] += jnp.dot(
                weights, slots[slot, :, value_columns], preferred_element_type=jnp.float32
            )

        if unrolled:
            for step in range(row_count // tile):
                add_rows(step)
        else:
            pl.loop(0, row_count // tile)(add_rows)


def add_sources(place, projected, totals, sources, first_head, skipped, heads, unrolled):
    row_count, width = projected.shape
    model_width = width // 4
    head_size = model_width // HEADS
    arrays = [array for array, _ in sources]
    holders = [positions for _, positions in sources]
    everyone = [position for positions in holders for position in positions]
    most = max(everyone.count(position) for position in everyone)
    first_head += skipped
    total_spec = pl.BlockSpec((row_count, head_size), lambda head, place: (0, first_head + head))
    return pl.pallas_call(
        functools.partial(add_kernel, head_size ** (-0.5), holders, skipped, unrolled),
        out_shape=jax.ShapeDtypeStruct(totals.shape, totals.dtype),
        grid_spec=pltpu.PrefetchScalarGridSpec(
            num_scalar_prefetch=1,
            grid=(heads,),
            in_specs=[
                pl.BlockSpec((row_count, head_size), lambda head, place: (0, HEADS + first_head + head)),
                *[pl.BlockSpec(memory_space=pl.ANY)] * len(arrays),
                total_spec,
            ],
            out_specs=total_spec,
            scratch_shapes=[
                pltpu.VMEM((most, *arrays[0].shape), projected.dtype),
                pltpu.SemaphoreType.DMA((most,)),
            ],
        ),
        input_output_aliases={2 + len(arrays): 0},
        compiler_params=pltpu.CompilerParams(vmem_limit_bytes=VMEM_LIMIT),
        cost_estimate=pl.CostEstimate(
            flops=COST_SCALE * 4 * row_count * row_count * heads * head_size * most,
            bytes_accessed=(6 + 4 * most) * row_count * heads * head_size,
            transcendentals=row_count * row_count * heads * most,
        ),
    )(place, projected, *arrays, totals)


def pack_kernel(projected_ref, *refs):
    count = (len(refs) - 2) // 2
    packed_refs, held_refs, (loaded, stored) = refs[:count], refs[count:-2], refs[-2:]
    model_width = projected_ref.shape[1] // 4
    low, loads, stores = 0, [], []
    for packed_ref, held_ref in zip(packed_refs, held_refs):
        width = packed_ref.shape[1] // 2
        for part in range(2):
            source = projected_ref.at[:, pl.ds((2 + part) * model_width + low, width)]
            held = held_ref.at[:, pl.ds(part * width, width)]
            target = packed_ref.at[:, pl.ds(part * width, width)]
            loads.append(pltpu.make_async_copy(source, held, loaded.at[len(loads)]))
            stores.append(pltpu.make_async_copy(held, target, stored.at[len(stores)]))
        low += width
    for load in loads:
        load.start()
    for load, store in zip(loads, stores):
        load.wait()
        store.start()
    for store in stores:
        store.wait()


def pack_key_values(projected, parts):
    row_count, width = projected.shape
    anywhere = pl.BlockSpec(memory_space=pl.ANY)
    shapes = [(row_count, heads * width // (2 * HEADS)) for heads in parts]
    return pl.pallas_call(
        pack_kernel,
        out_shape=[jax.ShapeDtypeStruct(shape, projected.dtype) for shape in shapes],
        in_specs=[anywhere],
        out_specs=[anywhere] * len(parts),
        scratch_shapes=[
            *[pltpu.VMEM(shape, projected.dtype) for shape in shapes],
            *[pltpu.SemaphoreType.DMA((2 * len(parts),))] * 2,
        ],
        compiler_params=pltpu.CompilerParams(vmem_limit_bytes=VMEM_LIMIT),
        cost_estimate=pl.CostEstimate(
            flops=0, bytes_accessed=2 * row_count * width, transcendentals=0
        ),
    )(projected)


def tie_kernel(array_ref, after_ref, out_ref):
    pass


def tie(array, after):
    anywhere = pl.BlockSpec(memory_space=pl.ANY)
    return pl.pallas_call(
        tie_kernel,
        out_shape=jax.ShapeDtypeStruct(array.shape, array.dtype),
        in_specs=[anywhere, anywhere],
        out_specs=anywhere,
        input_output_aliases={0: 0},
    )(array, after)


def group_attention(span, residue, peers, place, projected):
    if span == 1:
        return own_attention(projected)
    period = 2 if span == 2 else SPAN

    def send(array, *hops):
        pairs = []
        for position, target in hops:
            lowest, by = (residue + position) % period, target - position
            pairs += [(s, s + by) for s in range(lowest, peers, period) if s + by < peers]
        return lax.ppermute(array, "seq", pairs)

    def swap(array, position):
        lowest = (residue + position) % period
        pairs = [(s, s + 1) for s in range(lowest, peers, period) if s + 1 < peers]
        return lax.ppermute(array, "seq", pairs + [(b, a) for a, b in pairs])

    chips = {}
    for position in range(span):
        chips.setdefault((residue + position) // 2, []).append(position)
    chips = list(chips.values())
    inner = [tuple(chip) for chip in chips if len(chip) == 2]

    def exchange(mine, after):
        if span == 2:
            return [(send(mine, (0, 1)), [1])]
        if span == 3 and len(chips[0]) == 2:
            return [(send(mine, (0, 2)), [2]), (send(mine, (1, 2)), [2]), (send(mine, *inner), [1])]
        if span == 3:
            came = tie(send(mine, (0, 2)), after)
            return [(came, [2]), (swap(came, 1), [1])]
        came = send(mine, (0, 2), (1, 3))
        if len(chips) == 2:
            came = tie(came, after)
            return [(came, [2, 3]), (swap(came, 2), [2, 3])]
        found = [(send(mine, (2, 3)), [3])]
        came = tie(came, after)
        return [(came, [2, 3]), (swap(came, 1), [1]), *found]

    if span == 2 or (span == 3 and len(chips[0]) == 1):
        (mine,) = pack_key_values(projected, (HEADS,))
        totals = own_attention(projected)
        found = exchange(mine, totals)
        if span == 3:
            found.append((send(mine, *inner), [2]))
        return add_sources(place, projected, totals, found, 0, 0, HEADS, False)
    early, late = CHUNK_PARTS
    mine, rest = pack_key_values(projected, CHUNK_PARTS)
    totals = own_attention(projected)
    if span == 3:
        found, more = exchange(mine, totals), exchange(rest, totals)
        totals = add_sources(place, projected, totals, found, 0, 0, early, False)
        return add_sources(place, projected, totals, more, early, 0, late, False)
    hops = inner if len(chips) == 2 else [(0, 3), (1, 2)]
    holders = [target for _, target in hops]
    first, second = [(send(mine, *hops), holders)], [(send(rest, *hops), holders)]
    totals = add_sources(place, projected, totals, first, 0, 0, early, False)
    found = exchange(mine, totals)
    totals = add_sources(place, projected, totals, second, early, 0, late, False)
    totals = add_sources(place, projected, totals, found, 0, 0, early, False)
    more = exchange(rest, totals)
    return add_sources(place, projected, totals, more, early, 0, late, True)


def finish_kernel(place_ref, total_ref, u_ref, history_ref, gain_ref, weight_ref, out_ref, last_ref):
    step = pl.program_id(0)
    tile = total_ref.shape[0]
    row_count = tile * pl.num_programs(0)
    span, position, tail = place_ref[0], place_ref[2], place_ref[3]
    valid = jnp.where(position == span - 1, tail, row_count)
    row_ids = step * tile + lax.broadcasted_iota(jnp.int32, (tile, 1), 0)
    attention = jnp.where(row_ids < valid, total_ref[...], 0.0)
    row_mean = jnp.mean(attention, axis=1, keepdims=True)
    centered = attention - row_mean
    row_var = jnp.mean(centered * centered, axis=1, keepdims=True)
    normed = centered * lax.rsqrt(row_var + 1e-06) * gain_ref[...]
    gated = (normed * u_ref[...].astype(jnp.float32)).astype(jnp.bfloat16)
    out = jnp.dot(gated, weight_ref[...], preferred_element_type=jnp.float32)
    out = (out + history_ref[...].astype(jnp.float32)).astype(jnp.bfloat16)
    out_ref[...] = out

    @pl.when(valid - 1 - step * tile == jnp.clip(valid - 1 - step * tile, 0, tile - 1))
    def _():
        final = jnp.where(row_ids == valid - 1, out.astype(jnp.float32), 0.0)
        last_ref[...] = jnp.sum(final, axis=0, keepdims=True)


def finish(place, totals, projected, history_in, norm_gain, out_proj):
    row_count, model_width = history_in.shape
    tile = row_tile(row_count) // 2
    rows = pl.BlockSpec((tile, model_width), lambda step, place: (step, 0))
    whole = pl.BlockSpec((1, model_width), lambda step, place: (0, 0))
    return pl.pallas_call(
        finish_kernel,
        out_shape=(
            jax.ShapeDtypeStruct(history_in.shape, history_in.dtype),
            jax.ShapeDtypeStruct((1, model_width), jnp.float32),
        ),
        grid_spec=pltpu.PrefetchScalarGridSpec(
            num_scalar_prefetch=1,
            grid=(row_count // tile,),
            in_specs=[
                rows,
                rows,
                rows,
                whole,
                pl.BlockSpec(out_proj.shape, lambda step, place: (0, 0)),
            ],
            out_specs=(rows, whole),
        ),
        compiler_params=pltpu.CompilerParams(vmem_limit_bytes=VMEM_LIMIT),
        cost_estimate=pl.CostEstimate(
            flops=2 * row_count * model_width * model_width,
            bytes_accessed=10 * row_count * model_width + 2 * model_width * model_width,
            transcendentals=row_count,
        ),
    )(place, totals, projected, history_in, norm_gain.reshape(1, -1), out_proj)


def score_kernel(last_ref, rows_ref, user_ref, cand_ref, down_ref, up_ref, bias_ref, weight_ref, out_ref):
    peers, model_width = rows_ref.shape
    cand_count = cand_ref.shape[0]
    cand_user = user_ref[...]

    def visit(user, found):
        return jnp.where(cand_user == user, last_ref[user], found)

    cand_dev = lax.fori_loop(0, last_ref.shape[0], visit, jnp.zeros_like(cand_user))
    device_ids = lax.broadcasted_iota(jnp.int32, (peers, cand_count), 0)
    selector = jnp.where(device_ids == cand_dev, 1.0, 0.0).astype(jnp.bfloat16)
    user_part = lax.dot_general(
        selector,
        rows_ref[...].astype(jnp.bfloat16),
        (((0,), (0,)), ((), ())),
        preferred_element_type=jnp.float32,
    ).astype(jnp.bfloat16)
    cand_part = cand_ref[...]
    low_rank = jnp.dot(user_part, down_ref[:model_width, :], preferred_element_type=jnp.float32)
    low_rank += jnp.dot(cand_part, down_ref[model_width:, :], preferred_element_type=jnp.float32)
    low_rank = low_rank.astype(jnp.bfloat16)
    score = jnp.zeros((cand_count, 1), jnp.float32)
    for part, low in ((user_part, 0), (cand_part, model_width)):
        cut = slice(low, low + model_width)
        up_part = jnp.dot(low_rank, up_ref[:, cut], preferred_element_type=jnp.float32)
        value = part.astype(jnp.float32)
        crossed = value * (up_part + bias_ref[:, cut]) + value
        score += jnp.sum(crossed * weight_ref[:, cut], axis=1, keepdims=True)
    row_ids = lax.broadcasted_iota(jnp.int32, (cand_count, cand_count), 0)
    column_ids = lax.broadcasted_iota(jnp.int32, (cand_count, cand_count), 1)
    out_ref[...] = jnp.sum(jnp.where(row_ids == column_ids, score, 0.0), axis=0, keepdims=True)


def score(last_dev, user_rows, cand_user, cand_emb, cross_down, cross_up, cross_bias, score_weight):
    vmem = pl.BlockSpec(memory_space=pltpu.VMEM)
    cand_count = cand_emb.shape[0]
    scores = pl.pallas_call(
        score_kernel,
        out_shape=jax.ShapeDtypeStruct((1, cand_count), jnp.float32),
        in_specs=[pl.BlockSpec(memory_space=pltpu.SMEM)] + [vmem] * 7,
        out_specs=vmem,
        compiler_params=pltpu.CompilerParams(vmem_limit_bytes=VMEM_LIMIT),
    )(
        last_dev,
        user_rows,
        cand_user.reshape(1, -1),
        cand_emb,
        cross_down,
        cross_up,
        cross_bias.reshape(1, -1),
        score_weight.reshape(1, -1),
    )
    return scores.reshape(-1)


def body(
    projected,
    history_in,
    norm_gain,
    out_proj,
    user_spans,
    user_tails,
    cand_emb,
    cand_user,
    cross_down,
    cross_up,
    cross_bias,
    score_weight,
):
    peers = lax.axis_size("seq")
    place, last_dev = find_place(lax.axis_index("seq"), user_spans, user_tails)
    branches = [
        functools.partial(group_attention, span, residue, peers) for span, residue in KINDS
    ]
    totals = lax.switch(place[4], branches, place, projected)
    history_out, final_row = finish(place, totals, projected, history_in, norm_gain, out_proj)
    user_rows = lax.all_gather(final_row, "seq", axis=0, tiled=True)
    scores = score(
        last_dev, user_rows, cand_user, cand_emb, cross_down, cross_up, cross_bias, score_weight
    )
    return (history_out, scores)


def solution(mesh):
    in_specs = (
        P(("rep", "seq"), None),
        P(("rep", "seq"), None),
        P(),
        P(),
        P("rep"),
        P("rep"),
        P(("rep", "seq"), None),
        P(("rep", "seq")),
        P(),
        P(),
        P(),
        P(),
    )
    out_specs = (P(("rep", "seq"), None), P(("rep", "seq")))
    return jax.shard_map(body, mesh=mesh, in_specs=in_specs, out_specs=out_specs, check_vma=False)
```

```python
import functools

import jax
import jax.numpy as jnp
from jax import lax
from jax.experimental import pallas as pl
from jax.experimental.pallas import tpu as pltpu
from jax.sharding import PartitionSpec as P

HEADS = 8
SPAN = 4
CHUNK_PARTS = (5, 3)
COST_SCALE = 5
KINDS = (
    (1, 0),
    (2, 0),
    (2, 1),
    *((3, residue) for residue in range(SPAN)),
    *((4, residue) for residue in range(SPAN)),
)
VMEM_LIMIT = 63 * 1024 * 1024


def silu_weights(logits, score_scale):
    half = logits * (0.5 * score_scale)
    return half + half * jnp.tanh(half)


def row_tile(row_count):
    return 256 if row_count % 256 == 0 else row_count


def dot_nt(left, right):
    return lax.dot_general(left, right, (((1,), (1,)), ((), ())), preferred_element_type=jnp.float32)


def place_kernel(me_ref, spans_ref, tails_ref, place_ref, last_ref):
    users = spans_ref.shape[0]
    me = me_ref[0]

    def visit(user, state):
        begin, span, start, tail = state
        end = begin + spans_ref[user]
        mine = (begin <= me) & (me < end)
        last_ref[user] = end - 1
        return (
            end,
            jnp.where(mine, spans_ref[user], span),
            jnp.where(mine, begin, start),
            jnp.where(mine, tails_ref[user], tail),
        )

    zero = jnp.int32(0)
    _, span, start, tail = lax.fori_loop(0, users, visit, (zero, zero + 1, zero, zero))
    place_ref[0] = span
    place_ref[1] = start
    place_ref[2] = me - start
    place_ref[3] = tail
    kind = jnp.int32(0)
    for index, (its_span, residue) in enumerate(KINDS):
        period = 2 if its_span == 2 else SPAN
        fits = (span == its_span) & (lax.rem(start, period) == residue)
        kind = jnp.where(fits, index, kind)
    place_ref[4] = kind


def find_place(me, user_spans, user_tails):
    smem = pl.BlockSpec(memory_space=pltpu.SMEM)
    return pl.pallas_call(
        place_kernel,
        out_shape=(
            jax.ShapeDtypeStruct((8,), jnp.int32),
            jax.ShapeDtypeStruct(user_spans.shape, jnp.int32),
        ),
        in_specs=[smem] * 3,
        out_specs=(smem, smem),
    )(me.reshape(1), user_spans, user_tails)


def own_kernel(score_scale, q_ref, k_ref, v_ref, out_ref):
    row_count = q_ref.shape[0]
    tile = row_tile(row_count)

    @pl.loop(0, row_count // tile)
    def _(step):
        rows = pl.ds(pl.multiple_of(step * tile, tile), tile)
        weights = silu_weights(dot_nt(q_ref[rows, :], k_ref[...]), score_scale)
        row_ids = step * tile + lax.broadcasted_iota(jnp.int32, weights.shape, 0)
        key_ids = lax.broadcasted_iota(jnp.int32, weights.shape, 1)
        weights = jnp.where(key_ids <= row_ids, weights, 0.0).astype(jnp.bfloat16)
        out_ref[rows, :] = jnp.dot(weights, v_ref[...], preferred_element_type=jnp.float32)


def own_attention(projected):
    row_count, width = projected.shape
    model_width = width // 4
    head_size = model_width // HEADS

    def columns(part):
        return pl.BlockSpec((row_count, head_size), lambda head: (0, part * HEADS + head))

    return pl.pallas_call(
        functools.partial(own_kernel, head_size ** (-0.5)),
        out_shape=jax.ShapeDtypeStruct((row_count, model_width), jnp.float32),
        grid=(HEADS,),
        in_specs=[columns(1), columns(2), columns(3)],
        out_specs=pl.BlockSpec((row_count, head_size), lambda head: (0, head)),
        compiler_params=pltpu.CompilerParams(vmem_limit_bytes=VMEM_LIMIT),
        cost_estimate=pl.CostEstimate(
            flops=COST_SCALE * 3 * row_count * row_count * model_width,
            bytes_accessed=10 * row_count * model_width,
            transcendentals=row_count * row_count * HEADS,
        ),
    )(projected, projected, projected)


def add_kernel(score_scale, holders, skipped, unrolled, place_ref, q_ref, *refs):
    source_refs, (total_ref, out_ref, slots, arrived) = refs[: len(holders)], refs[-4:]
    head, position = pl.program_id(0), place_ref[2]
    row_count, head_size = q_ref.shape
    tile = row_tile(row_count)
    counts = {}
    for source_ref, positions in zip(source_refs, holders):
        for place in positions:
            slot = counts.get(place, 0)
            counts[place] = slot + 1

            @pl.when((head == 0) & (position == place))
            def _():
                pltpu.make_async_copy(source_ref, slots.at[slot], arrived.at[slot]).start()

    out_ref[...] = total_ref[...]
    count = sum(jnp.where(position == place, number, 0) for place, number in counts.items())
    low = pl.multiple_of((skipped + head) * head_size, head_size)
    key_columns = pl.ds(low, head_size)
    value_columns = pl.ds(pl.multiple_of(slots.shape[2] // 2 + low, head_size), head_size)

    @pl.loop(0, count)
    def _(slot):
        @pl.when(head == 0)
        def _():
            pltpu.make_async_copy(source_refs[0], slots.at[slot], arrived.at[slot]).wait()

        def add_rows(step):
            rows = pl.ds(pl.multiple_of(step * tile, tile), tile)
            logits = dot_nt(q_ref[rows, :], slots[slot, :, key_columns])
            weights = silu_weights(logits, score_scale).astype(jnp.bfloat16)
            out_ref[rows, :] += jnp.dot(
                weights, slots[slot, :, value_columns], preferred_element_type=jnp.float32
            )

        if unrolled:
            for step in range(row_count // tile):
                add_rows(step)
        else:
            pl.loop(0, row_count // tile)(add_rows)


def add_sources(place, projected, totals, sources, first_head, skipped, heads, unrolled):
    row_count, width = projected.shape
    model_width = width // 4
    head_size = model_width // HEADS
    arrays = [array for array, _ in sources]
    holders = [positions for _, positions in sources]
    everyone = [position for positions in holders for position in positions]
    most = max(everyone.count(position) for position in everyone)
    first_head += skipped
    total_spec = pl.BlockSpec((row_count, head_size), lambda head, place: (0, first_head + head))
    return pl.pallas_call(
        functools.partial(add_kernel, head_size ** (-0.5), holders, skipped, unrolled),
        out_shape=jax.ShapeDtypeStruct(totals.shape, totals.dtype),
        grid_spec=pltpu.PrefetchScalarGridSpec(
            num_scalar_prefetch=1,
            grid=(heads,),
            in_specs=[
                pl.BlockSpec((row_count, head_size), lambda head, place: (0, HEADS + first_head + head)),
                *[pl.BlockSpec(memory_space=pl.ANY)] * len(arrays),
                total_spec,
            ],
            out_specs=total_spec,
            scratch_shapes=[
                pltpu.VMEM((most, *arrays[0].shape), projected.dtype),
                pltpu.SemaphoreType.DMA((most,)),
            ],
        ),
        input_output_aliases={2 + len(arrays): 0},
        compiler_params=pltpu.CompilerParams(vmem_limit_bytes=VMEM_LIMIT),
        cost_estimate=pl.CostEstimate(
            flops=COST_SCALE * 4 * row_count * row_count * heads * head_size * most,
            bytes_accessed=(6 + 4 * most) * row_count * heads * head_size,
            transcendentals=row_count * row_count * heads * most,
        ),
    )(place, projected, *arrays, totals)


def pack_kernel(projected_ref, *refs):
    count = (len(refs) - 2) // 2
    packed_refs, held_refs, (loaded, stored) = refs[:count], refs[count:-2], refs[-2:]
    model_width = projected_ref.shape[1] // 4
    low, loads, stores = 0, [], []
    for packed_ref, held_ref in zip(packed_refs, held_refs):
        width = packed_ref.shape[1] // 2
        for part in range(2):
            source = projected_ref.at[:, pl.ds((2 + part) * model_width + low, width)]
            held = held_ref.at[:, pl.ds(part * width, width)]
            target = packed_ref.at[:, pl.ds(part * width, width)]
            loads.append(pltpu.make_async_copy(source, held, loaded.at[len(loads)]))
            stores.append(pltpu.make_async_copy(held, target, stored.at[len(stores)]))
        low += width
    for load in loads:
        load.start()
    for load, store in zip(loads, stores):
        load.wait()
        store.start()
    for store in stores:
        store.wait()


def pack_key_values(projected, parts):
    row_count, width = projected.shape
    anywhere = pl.BlockSpec(memory_space=pl.ANY)
    shapes = [(row_count, heads * width // (2 * HEADS)) for heads in parts]
    return pl.pallas_call(
        pack_kernel,
        out_shape=[jax.ShapeDtypeStruct(shape, projected.dtype) for shape in shapes],
        in_specs=[anywhere],
        out_specs=[anywhere] * len(parts),
        scratch_shapes=[
            *[pltpu.VMEM(shape, projected.dtype) for shape in shapes],
            *[pltpu.SemaphoreType.DMA((2 * len(parts),))] * 2,
        ],
        compiler_params=pltpu.CompilerParams(vmem_limit_bytes=VMEM_LIMIT),
        cost_estimate=pl.CostEstimate(
            flops=0, bytes_accessed=2 * row_count * width, transcendentals=0
        ),
    )(projected)


def tie_kernel(array_ref, after_ref, out_ref):
    pass


def tie(array, after):
    anywhere = pl.BlockSpec(memory_space=pl.ANY)
    return pl.pallas_call(
        tie_kernel,
        out_shape=jax.ShapeDtypeStruct(array.shape, array.dtype),
        in_specs=[anywhere, anywhere],
        out_specs=anywhere,
        input_output_aliases={0: 0},
    )(array, after)


def group_attention(span, residue, peers, place, projected):
    if span == 1:
        return own_attention(projected)
    period = 2 if span == 2 else SPAN

    def send(array, *hops):
        pairs = []
        for position, target in hops:
            lowest, by = (residue + position) % period, target - position
            pairs += [(s, s + by) for s in range(lowest, peers, period) if s + by < peers]
        return lax.ppermute(array, "seq", pairs)

    def swap(array, position):
        lowest = (residue + position) % period
        pairs = [(s, s + 1) for s in range(lowest, peers, period) if s + 1 < peers]
        return lax.ppermute(array, "seq", pairs + [(b, a) for a, b in pairs])

    chips = {}
    for position in range(span):
        chips.setdefault((residue + position) // 2, []).append(position)
    chips = list(chips.values())
    inner = [tuple(chip) for chip in chips if len(chip) == 2]

    def exchange(mine, after):
        if span == 2:
            return [(send(mine, (0, 1)), [1])]
        if span == 3 and len(chips[0]) == 2:
            return [(send(mine, (0, 2)), [2]), (send(mine, (1, 2)), [2]), (send(mine, *inner), [1])]
        if span == 3:
            came = tie(send(mine, (0, 2)), after)
            return [(came, [2]), (swap(came, 1), [1])]
        came = send(mine, (0, 2), (1, 3))
        if len(chips) == 2:
            came = tie(came, after)
            return [(came, [2, 3]), (swap(came, 2), [2, 3])]
        found = [(send(mine, (2, 3)), [3])]
        came = tie(came, after)
        return [(came, [2, 3]), (swap(came, 1), [1]), *found]

    if span == 2 or (span == 3 and len(chips[0]) == 1):
        (mine,) = pack_key_values(projected, (HEADS,))
        totals = own_attention(projected)
        found = exchange(mine, totals)
        if span == 3:
            found.append((send(mine, *inner), [2]))
        return add_sources(place, projected, totals, found, 0, 0, HEADS, False)
    early, late = CHUNK_PARTS
    mine, rest = pack_key_values(projected, CHUNK_PARTS)
    totals = own_attention(projected)
    if span == 3:
        found, more = exchange(mine, totals), exchange(rest, totals)
        totals = add_sources(place, projected, totals, found, 0, 0, early, False)
        return add_sources(place, projected, totals, more, early, 0, late, False)
    hops = inner if len(chips) == 2 else [(0, 3), (1, 2)]
    holders = [target for _, target in hops]
    first, second = [(send(mine, *hops), holders)], [(send(rest, *hops), holders)]
    totals = add_sources(place, projected, totals, first, 0, 0, early, False)
    found = exchange(mine, totals)
    totals = add_sources(place, projected, totals, second, early, 0, late, False)
    totals = add_sources(place, projected, totals, found, 0, 0, early, False)
    more = exchange(rest, totals)
    return add_sources(place, projected, totals, more, early, 0, late, True)


def finish_kernel(place_ref, total_ref, u_ref, history_ref, gain_ref, weight_ref, out_ref, last_ref):
    step = pl.program_id(0)
    tile = total_ref.shape[0]
    row_count = tile * pl.num_programs(0)
    span, position, tail = place_ref[0], place_ref[2], place_ref[3]
    valid = jnp.where(position == span - 1, tail, row_count)
    row_ids = step * tile + lax.broadcasted_iota(jnp.int32, (tile, 1), 0)
    attention = jnp.where(row_ids < valid, total_ref[...], 0.0)
    row_mean = jnp.mean(attention, axis=1, keepdims=True)
    centered = attention - row_mean
    row_var = jnp.mean(centered * centered, axis=1, keepdims=True)
    normed = centered * lax.rsqrt(row_var + 1e-06) * gain_ref[...]
    gated = (normed * u_ref[...].astype(jnp.float32)).astype(jnp.bfloat16)
    out = jnp.dot(gated, weight_ref[...], preferred_element_type=jnp.float32)
    out = (out + history_ref[...].astype(jnp.float32)).astype(jnp.bfloat16)
    out_ref[...] = out

    @pl.when(valid - 1 - step * tile == jnp.clip(valid - 1 - step * tile, 0, tile - 1))
    def _():
        final = jnp.where(row_ids == valid - 1, out.astype(jnp.float32), 0.0)
        last_ref[...] = jnp.sum(final, axis=0, keepdims=True)


def finish(place, totals, projected, history_in, norm_gain, out_proj):
    row_count, model_width = history_in.shape
    tile = row_tile(row_count)
    rows = pl.BlockSpec((tile, model_width), lambda step, place: (step, 0))
    whole = pl.BlockSpec((1, model_width), lambda step, place: (0, 0))
    return pl.pallas_call(
        finish_kernel,
        out_shape=(
            jax.ShapeDtypeStruct(history_in.shape, history_in.dtype),
            jax.ShapeDtypeStruct((1, model_width), jnp.float32),
        ),
        grid_spec=pltpu.PrefetchScalarGridSpec(
            num_scalar_prefetch=1,
            grid=(row_count // tile,),
            in_specs=[
                rows,
                rows,
                rows,
                whole,
                pl.BlockSpec(out_proj.shape, lambda step, place: (0, 0)),
            ],
            out_specs=(rows, whole),
        ),
        compiler_params=pltpu.CompilerParams(vmem_limit_bytes=VMEM_LIMIT),
        cost_estimate=pl.CostEstimate(
            flops=2 * row_count * model_width * model_width,
            bytes_accessed=10 * row_count * model_width + 2 * model_width * model_width,
            transcendentals=row_count,
        ),
    )(place, totals, projected, history_in, norm_gain.reshape(1, -1), out_proj)


def score_kernel(last_ref, rows_ref, user_ref, cand_ref, down_ref, up_ref, bias_ref, weight_ref, out_ref):
    peers, model_width = rows_ref.shape
    cand_count = cand_ref.shape[0]
    cand_user = user_ref[...]

    def visit(user, found):
        return jnp.where(cand_user == user, last_ref[user], found)

    cand_dev = lax.fori_loop(0, last_ref.shape[0], visit, jnp.zeros_like(cand_user))
    device_ids = lax.broadcasted_iota(jnp.int32, (peers, cand_count), 0)
    selector = jnp.where(device_ids == cand_dev, 1.0, 0.0).astype(jnp.bfloat16)
    user_part = lax.dot_general(
        selector,
        rows_ref[...].astype(jnp.bfloat16),
        (((0,), (0,)), ((), ())),
        preferred_element_type=jnp.float32,
    ).astype(jnp.bfloat16)
    cand_part = cand_ref[...]
    low_rank = jnp.dot(user_part, down_ref[:model_width, :], preferred_element_type=jnp.float32)
    low_rank += jnp.dot(cand_part, down_ref[model_width:, :], preferred_element_type=jnp.float32)
    low_rank = low_rank.astype(jnp.bfloat16)
    score = jnp.zeros((cand_count, 1), jnp.float32)
    for part, low in ((user_part, 0), (cand_part, model_width)):
        cut = slice(low, low + model_width)
        up_part = jnp.dot(low_rank, up_ref[:, cut], preferred_element_type=jnp.float32)
        value = part.astype(jnp.float32)
        crossed = value * (up_part + bias_ref[:, cut]) + value
        score += jnp.sum(crossed * weight_ref[:, cut], axis=1, keepdims=True)
    row_ids = lax.broadcasted_iota(jnp.int32, (cand_count, cand_count), 0)
    column_ids = lax.broadcasted_iota(jnp.int32, (cand_count, cand_count), 1)
    out_ref[...] = jnp.sum(jnp.where(row_ids == column_ids, score, 0.0), axis=0, keepdims=True)


def score(last_dev, user_rows, cand_user, cand_emb, cross_down, cross_up, cross_bias, score_weight):
    vmem = pl.BlockSpec(memory_space=pltpu.VMEM)
    cand_count = cand_emb.shape[0]
    scores = pl.pallas_call(
        score_kernel,
        out_shape=jax.ShapeDtypeStruct((1, cand_count), jnp.float32),
        in_specs=[pl.BlockSpec(memory_space=pltpu.SMEM)] + [vmem] * 7,
        out_specs=vmem,
        compiler_params=pltpu.CompilerParams(vmem_limit_bytes=VMEM_LIMIT),
    )(
        last_dev,
        user_rows,
        cand_user.reshape(1, -1),
        cand_emb,
        cross_down,
        cross_up,
        cross_bias.reshape(1, -1),
        score_weight.reshape(1, -1),
    )
    return scores.reshape(-1)


def body(
    projected,
    history_in,
    norm_gain,
    out_proj,
    user_spans,
    user_tails,
    cand_emb,
    cand_user,
    cross_down,
    cross_up,
    cross_bias,
    score_weight,
):
    peers = lax.axis_size("seq")
    place, last_dev = find_place(lax.axis_index("seq"), user_spans, user_tails)
    branches = [
        functools.partial(group_attention, span, residue, peers) for span, residue in KINDS
    ]
    totals = lax.switch(place[4], branches, place, projected)
    history_out, final_row = finish(place, totals, projected, history_in, norm_gain, out_proj)
    user_rows = lax.all_gather(final_row, "seq", axis=0, tiled=True)
    scores = score(
        last_dev, user_rows, cand_user, cand_emb, cross_down, cross_up, cross_bias, score_weight
    )
    return (history_out, scores)


def solution(mesh):
    in_specs = (
        P(("rep", "seq"), None),
        P(("rep", "seq"), None),
        P(),
        P(),
        P("rep"),
        P("rep"),
        P(("rep", "seq"), None),
        P(("rep", "seq")),
        P(),
        P(),
        P(),
        P(),
    )
    out_specs = (P(("rep", "seq"), None), P(("rep", "seq")))
    return jax.shard_map(body, mesh=mesh, in_specs=in_specs, out_specs=out_specs, check_vma=False)
```
